32 devices in a mesh: dp: 8 (over y, x, core), tp: 4 (over z).
Axes of the slice: x: 2, y: 2, z: 4, core: 2. Of those that a mesh axis runs over, the one named last changes fastest.
Arguments:
- hidden_in: bfloat16 [4096, 768], P('dp'), may hold values from -6 to 6
- out_grad: bfloat16 [4096, 768], P('dp'), may hold values from -6 to 6
- segment_ids: int32 [8, 512], P('dp'), may hold values from 0 to 6, as said below
- loss_mask: int32 [8, 512], P('dp'), may hold values from 0 to 1, as said below
- w_qkv: bfloat16 [2, 768, 3, 768], P(None, None, None, 'tp'), may hold values from -0.21875 to 0.21875
- b_query_value: float32 [2, 2, 768], P(None, None, 'tp'), may hold values from -3 to 3
- w_out: bfloat16 [2, 768, 768], P(None, 'tp'), may hold values from -1.75 to 1.75
- branch_bias: float32 [2, 2, 768], replicated, may hold values from -2 to 2
- norm_gain: float32 [2, 2, 768], replicated, may hold values from 0.5 to 1.5
- norm_shift: float32 [2, 2, 768], replicated, may hold values from -2 to 2
- w_up: bfloat16 [2, 768, 3072], P(None, None, 'tp'), may hold values from -0.21875 to 0.21875
- b_up: float32 [2, 3072], P(None, 'tp'), may hold values from -3 to 3
- w_down: bfloat16 [2, 3072, 768], P(None, 'tp'), may hold values from -0.109375 to 0.109375
Outputs:
- final_hidden: float32 [4096, 768], P(('dp', 'tp'))
- input_grad: float32 [4096, 768], P(('dp', 'tp'))
- grad_w_qkv: float32 [2, 768, 3, 768], P(None, None, None, 'tp')
- grad_b_query_value: float32 [2, 2, 768], P(None, None, 'tp')
- grad_w_out: float32 [2, 768, 768], P(None, 'tp')
- grad_branch_bias: float32 [2, 2, 768], replicated
- grad_norm_gain: float32 [2, 2, 768], replicated
- grad_norm_shift: float32 [2, 2, 768], replicated
- grad_w_up: float32 [2, 768, 3072], P(None, None, 'tp')
- grad_b_up: float32 [2, 3072], P(None, 'tp')
- grad_w_down: float32 [2, 3072, 768], P(None, 'tp')
The draws below stay inside these ranges and needn't reach their ends.
Inputs may be any that keep to these rules, and one draw needn't show every extreme that they name: `segment_ids`: along a row the ids never fall; id 6 marks padding and fills the last 1 to 128 positions of every row; ids 0 to 5 are the row's documents, some possibly empty, and a row always begins with id 0. `loss_mask`: 1 exactly where segment_ids is under 6, 0 at the padding.
All inputs are finite; a program needn't handle non-finite values.
Results may differ from the reference program's by a relative error of at most 0.024.
Values may be sent and summed in bfloat16 or wider, within the bound.
No kernel may reach another device: no remote copies, remote signals or barrier semaphores. Data moves between devices by JAX's collectives and lax.ppermute only.
A program may use at most 128 MiB of HBM per device.

```python
import jax
import jax.numpy as jnp
from jax import lax

D = 768
HEAD_DIM = 64
FF = 3072
LEN = 512
LAYERS = 2
SEQS = 8
TOKENS = 4096


def packed_layout(key):
    pad_key, cut_key = jax.random.split(key)
    pad_len = jax.random.randint(pad_key, (SEQS, 1), 1, LEN // 4 + 1)
    cuts = jax.random.randint(cut_key, (SEQS, 5, 1), 1, LEN - LEN // 4)
    places = jnp.arange(LEN, dtype=jnp.int32)
    doc_ids = jnp.sum((cuts <= places[None, None, :]).astype(jnp.int32), axis=1)
    padded = places[None, :] >= LEN - pad_len
    return (jnp.where(padded, 6, doc_ids).astype(jnp.int32), jnp.where(padded, 0, 1).astype(jnp.int32))


def draw_segment_ids(key, part):
    layout = packed_layout(key)
    return layout[0]


def draw_loss_mask(key, part):
    layout = packed_layout(key)
    return layout[1]


def level_of(stream_key, extent, pieces, least, high):
    def one(axis_at, blocks):
        steps = jax.random.uniform(jax.random.fold_in(jax.random.fold_in(stream_key, 6), axis_at), (blocks,), jnp.float32, least / len(pieces), high / len(pieces))
        return jnp.repeat(jnp.exp(steps), extent[axis_at] // blocks).reshape((-1,) + (1,) * (len(extent) - axis_at - 1))

    gain = one(*pieces[0])
    for cut in pieces[1:]:
        gain = gain * one(*cut)
    return gain


def bell_draw(key, extent, scale, limit, pieces=(), kind=jnp.bfloat16):
    level = level_of(key, extent, pieces, -0.22, 0.18) if pieces else 1.0
    values = jax.random.normal(key, extent, jnp.float32) * scale * level
    return jnp.minimum(jnp.maximum(values, -limit), limit).astype(kind)


def setup_inputs(seed: int = 0) -> dict:
    key_list = jax.random.split(jax.random.key(seed), 14)
    hidden_in = bell_draw(key_list[0], (TOKENS, D), 1.0, 6.0, ((0, 8),))
    out_grad = bell_draw(key_list[1], (TOKENS, D), 1.0, 6.0, ((0, 8),))
    segment_ids = draw_segment_ids(jax.random.fold_in(key_list[13], 71), 0)
    loss_mask = draw_loss_mask(jax.random.fold_in(key_list[13], 71), 0)
    w_qkv = bell_draw(key_list[4], (LAYERS, D, 3, D), D ** -0.5, 0.21875, ((3, 4),))
    b_query_value = bell_draw(key_list[5], (LAYERS, 2, D), 0.5, 3.0, ((2, 4),), jnp.float32)
    w_out = bell_draw(key_list[6], (LAYERS, D, D), (D // 64) ** -0.5, 1.75, ((1, 4),))
    branch_bias = bell_draw(key_list[7], (LAYERS, 2, D), 0.3, 2.0, (), jnp.float32)
    norm_gain = jnp.clip(1.0 + 0.1 * jax.random.normal(key_list[8], (LAYERS, 2, D), jnp.float32), 0.5, 1.5)
    norm_shift = bell_draw(key_list[9], (LAYERS, 2, D), 0.3, 2.0, (), jnp.float32)
    w_up = bell_draw(key_list[10], (LAYERS, D, FF), D ** -0.5, 0.21875, ((2, 4),))
    b_up = bell_draw(key_list[11], (LAYERS, FF), 0.5, 3.0, ((1, 4),), jnp.float32)
    w_down = bell_draw(key_list[12], (LAYERS, FF, D), FF ** -0.5, 0.109375, ((1, 4),))
    return dict(hidden_in=hidden_in, out_grad=out_grad, segment_ids=segment_ids, loss_mask=loss_mask, w_qkv=w_qkv, b_query_value=b_query_value, w_out=w_out, branch_bias=branch_bias, norm_gain=norm_gain, norm_shift=norm_shift, w_up=w_up, b_up=b_up, w_down=w_down)


EPS = 1e-06
NEG = -1e+30
HIGH = lax.Precision.HIGHEST

@jax.custom_vjp
def low(v):
    return lax.optimization_barrier(v.astype(jnp.bfloat16)).astype(jnp.float32)

@jax.custom_vjp
def low_back(v):
    return v

def low_keep(v):
    return (low(v), None)

def low_pass(kept, grad):
    return (grad,)

def back_keep(v):
    return (v, None)

def back_low(kept, grad):
    return (low(grad),)
low.defvjp(low_keep, low_pass)
low_back.defvjp(back_keep, back_low)

def layer_norm(values, gain_row, shift_row):
    center = values - lax.optimization_barrier(jnp.mean(values, axis=-1, keepdims=True))
    spread = lax.optimization_barrier(jnp.mean(center * center, axis=-1, keepdims=True))
    return center * lax.rsqrt(spread + EPS) * gain_row + shift_row

def matmul(left, right):
    return jnp.dot(left, right, precision=HIGH)

def encoder_block(hidden, same_doc, weights, layer_no, is_last):
    w_qkv, b_qv, w_out, b_branch, n_gain, n_shift, w_up, b_up, w_down = [tensor[layer_no] for tensor in weights]
    length = hidden.shape[0]
    width = hidden.shape[1]
    heads = width // HEAD_DIM
    proj = matmul(hidden, w_qkv.reshape(width, 3 * width)).reshape(length, 3, width)
    zero_row = jnp.zeros_like(b_qv[0])
    proj = low_back(low(proj + jnp.stack([b_qv[0], zero_row, b_qv[1]])[None]))
    queries = proj[:, 0].reshape(length, heads, HEAD_DIM)
    key_rows = proj[:, 1].reshape(length, heads, HEAD_DIM)
    value_rows = proj[:, 2].reshape(length, heads, HEAD_DIM)
    scores = low_back(jnp.einsum('qhe,khe->hqk', queries, key_rows, precision=HIGH) * HEAD_DIM ** (-0.5))
    scores = jnp.where(same_doc[None], scores, NEG)
    probs = low(jax.nn.softmax(scores, axis=-1))
    mixed = jnp.einsum('hqk,khe->qhe', probs, value_rows, precision=HIGH).reshape(length, width)
    mixed = low_back(low(mixed))
    attended = low_back(matmul(mixed, w_out) + b_branch[0])
    normed = layer_norm(hidden + attended, n_gain[0], n_shift[0])
    upper = low_back(matmul(low(normed), w_up) + b_up)
    activ = low(jax.nn.gelu(upper, approximate=False))
    branch = low_back(matmul(activ, w_down) + b_branch[1])
    result = layer_norm(normed + branch, n_gain[1], n_shift[1])
    if is_last:
        return result
    return low(result)

def reference(hidden_in, out_grad, segment_ids, loss_mask, w_qkv, b_query_value, w_out, branch_bias, norm_gain, norm_shift, w_up, b_up, w_down):
    params = tuple((tensor.astype(jnp.float32) for tensor in (w_qkv, b_query_value, w_out, branch_bias, norm_gain, norm_shift, w_up, b_up, w_down)))
    inputs = hidden_in.astype(jnp.float32).reshape(SEQS, LEN, D)
    cotans = out_grad.astype(jnp.float32).reshape(SEQS, LEN, D)
    masks = loss_mask.astype(jnp.float32)

    def per_sequence(totals, item):
        hidden, cotan, seg_row, mask_row = item
        same_doc = seg_row[:, None] == seg_row[None, :]

        def network(start, *weights):
            state = start
            for layer_no in range(LAYERS):
                state = encoder_block(state, same_doc, weights, layer_no, layer_no + 1 == LAYERS)
            return state
        output, pull = jax.vjp(network, hidden, *params)
        grads = pull(cotan * mask_row[:, None])
        totals = tuple((accum + fresh for accum, fresh in zip(totals, grads[1:])))
        return (totals, (output, grads[0]))
    zeros = tuple((jnp.zeros_like(tensor) for tensor in params))
    totals, (outputs, in_grads) = lax.scan(per_sequence, zeros, (inputs, cotans, segment_ids, masks))
    return (outputs.reshape(TOKENS, D), in_grads.reshape(TOKENS, D), totals[0], totals[1], totals[2], totals[3], totals[4], totals[5], totals[6], totals[7], totals[8])
```

```python
import jax
import jax.numpy as jnp
from jax import lax
from jax.sharding import PartitionSpec as P

HEAD_DIM = 64
EPS = 1e-06
NEG = -1e30
AXES = ("dp", "tp")
BF = jnp.bfloat16
F32 = jnp.float32


class Place:
    def __init__(self):
        self.groups = lax.axis_size("dp")
        self.quad = lax.axis_size("tp")
        self.blocks = self.groups // self.quad
        self.d = lax.axis_index("dp")
        self.z = lax.axis_index("tp")
        self.q = self.d % self.quad
        self.blk = self.d // self.quad

    def move(self, values, where):
        pairs = []
        for blk in range(self.blocks):
            for q in range(self.quad):
                for z in range(self.quad):
                    to = where(blk, q, z)
                    if to is not None:
                        source = (blk * self.quad + q) * self.quad + z
                        pairs.append((source, (to[0] * self.quad + to[1]) * self.quad + to[2]))
        return lax.ppermute(values, AXES, pairs)

    def core(self, values):
        return self.move(values, lambda b, q, z: (b, q ^ 1, z))

    def side(self, values):
        return self.move(values, lambda b, q, z: (b, q ^ 2, z))

    def swap(self, values):
        return self.move(values, lambda b, q, z: (b, z, q))


def layer_norm(values, gain_row, shift_row):
    center = values - jnp.mean(values, axis=-1, keepdims=True)
    spread = jnp.mean(center * center, axis=-1, keepdims=True)
    return center * lax.rsqrt(spread + EPS) * gain_row + shift_row


def dot_f(left, right):
    return jnp.dot(left, right, preferred_element_type=F32)


def gelu_exact(upper):
    return jax.nn.gelu(upper, approximate=False)


def half_first(values, flag):
    half = values.shape[0] // 2
    swapped = jnp.concatenate([values[half:], values[:half]], axis=0)
    return jnp.where(flag == 1, swapped, values)


def quad_sum(place, part):
    half = part.shape[0] // 2
    own = part[:half] + place.core(part[half:].astype(BF)).astype(F32)
    return own + place.side(own.astype(BF)).astype(F32)


def quad_gather(place, values):
    return jnp.concatenate([values, place.core(values)], axis=0)


def line_gather(values):
    return lax.all_gather(values, "tp", axis=0, tiled=True)


def attention_forward(hidden_b, weight, bias_qv, same_doc):
    width = weight.shape[-1] // 3
    proj = dot_f(hidden_b, weight)
    zero_row = jnp.zeros_like(bias_qv[0])
    qkv = (proj + jnp.concatenate([bias_qv[0], zero_row, bias_qv[1]])[None]).astype(BF)
    parts = qkv.reshape(-1, 3, width // HEAD_DIM, HEAD_DIM)
    queries, key_rows, value_rows = parts[:, 0], parts[:, 1], parts[:, 2]
    scores = (
        jnp.einsum("qhe,khe->hqk", queries, key_rows, preferred_element_type=F32)
        * HEAD_DIM ** (-0.5)
    )
    scores = jnp.where(same_doc[None], scores, NEG)
    top = jnp.max(scores, axis=-1, keepdims=True)
    expon = jnp.exp(scores - top)
    totals = jnp.sum(expon, axis=-1, keepdims=True)
    log_sum = top + jnp.log(totals)
    probs_b = (expon / totals).astype(BF)
    mixed = jnp.einsum("hqk,khe->qhe", probs_b, value_rows, preferred_element_type=F32)
    return qkv, log_sum, mixed.reshape(-1, width).astype(BF)


def attention_backward(qkv, log_sum, grad_mixed, same_doc):
    width = qkv.shape[-1] // 3
    scale = HEAD_DIM ** (-0.5)
    parts = qkv.reshape(-1, 3, width // HEAD_DIM, HEAD_DIM)
    queries, key_rows, value_rows = parts[:, 0], parts[:, 1], parts[:, 2]
    scores = jnp.einsum("qhe,khe->hqk", queries, key_rows, preferred_element_type=F32) * scale
    scores = jnp.where(same_doc[None], scores, NEG)
    probs = jnp.exp(scores - log_sum)
    probs_b = probs.astype(BF)
    grad_heads = grad_mixed.reshape(queries.shape)
    grad_probs = jnp.einsum("qhe,khe->hqk", grad_heads, value_rows, preferred_element_type=F32)
    grad_value = jnp.einsum("hqk,qhe->khe", probs_b, grad_heads, preferred_element_type=F32)
    grad_scores = (
        probs * (grad_probs - jnp.sum(probs * grad_probs, axis=-1, keepdims=True))
    ).astype(BF)
    grad_query = (
        jnp.einsum("hqk,khe->qhe", grad_scores, key_rows, preferred_element_type=F32) * scale
    )
    grad_keys = (
        jnp.einsum("hqk,qhe->khe", grad_scores, queries, preferred_element_type=F32) * scale
    )
    stacked = jnp.stack([grad_query, grad_keys, grad_value], axis=1)
    return stacked.reshape(-1, 3 * width).astype(BF)


def norm_backward(values, gain_row, grad):
    center = values - jnp.mean(values, axis=-1, keepdims=True)
    spread = jnp.mean(center * center, axis=-1, keepdims=True)
    inv = lax.rsqrt(spread + EPS)
    unit = center * inv
    scaled = grad * gain_row
    first = jnp.mean(scaled, axis=-1, keepdims=True)
    second = jnp.mean(scaled * unit, axis=-1, keepdims=True)
    back = inv * (scaled - first - unit * second)
    return back, jnp.sum(grad * unit, axis=0), jnp.sum(grad, axis=0)


def share_over_blocks(place, values, axis):
    count = place.blocks
    values = jnp.moveaxis(values, axis, 0)
    while count > 1:
        count //= 2
        mine = (place.blk // count) % 2
        pair = values.reshape((2, count) + values.shape[1:])
        keep = lax.dynamic_index_in_dim(pair, mine, 0, keepdims=False)
        send = lax.dynamic_index_in_dim(pair, 1 - mine, 0, keepdims=False)
        got = place.move(send.astype(BF), lambda b, q, z, k=count: (b ^ k, q, z))
        values = keep.astype(F32) + got.astype(F32)
    return values[0]


def add_over(place, values, steps):
    for where in steps:
        values = values + place.move(values, where)
    return values


def on_device(
    hidden_in,
    out_grad,
    segment_ids,
    loss_mask,
    w_qkv,
    b_query_value,
    w_out,
    branch_bias,
    norm_gain,
    norm_shift,
    w_up,
    b_up,
    w_down,
):
    place = Place()
    layers, features = w_qkv.shape[:2]
    width = w_qkv.shape[-1]
    hidden_units = w_up.shape[-1]
    tokens = hidden_in.shape[0]
    half = tokens // 2
    quad, blocks, q, z = place.quad, place.blocks, place.q, place.z
    cell = hidden_units // (quad * blocks)
    core_no = q % 2

    def unit_rows(rows):
        parts = rows.reshape(blocks, quad, cell, features)
        return lax.dynamic_index_in_dim(parts, q, 1, keepdims=False).reshape(-1, features)

    def own_piece(values):
        rows = values.shape[0] // quad
        return lax.dynamic_slice_in_dim(values, q * rows, rows, 0)

    def share_of(values):
        return line_gather(place.swap(own_piece(values)))

    plane_out = [share_of(w_out[0])]
    plane_up, plane_down = [], []
    plane_qkv = [None]
    for layer_no in range(layers):
        if layer_no:
            flat = w_qkv[layer_no].reshape(features, 3 * width)
            plane_qkv.append(share_of(flat))
            plane_out.append(share_of(w_out[layer_no]))
        plane_up.append(line_gather(unit_rows(w_up[layer_no].T)))
        plane_down.append(line_gather(unit_rows(w_down[layer_no])))
    zeros = jnp.zeros((quad, layers, hidden_units // quad + 2 * width), F32)
    my_b_up = lax.dynamic_index_in_dim(
        b_up.reshape(layers, blocks, quad, cell), q, 2, keepdims=False
    ).reshape(layers, -1)
    mine = jnp.concatenate([my_b_up, b_query_value.reshape(layers, -1)], axis=1)
    biases = lax.dynamic_update_index_in_dim(zeros, mine, z, 0)
    biases = add_over(
        place, biases, [lambda b, q, z: (b, q, z ^ 1), lambda b, q, z: (b, q, z ^ 2)]
    )
    plane_b_up = [biases[:, n, : hidden_units // quad].reshape(-1) for n in range(layers)]
    all_bqv = biases[:, :, hidden_units // quad :].reshape(quad, layers, 2, width)
    plane_bqv = lax.dynamic_index_in_dim(all_bqv, q, 0, keepdims=False)

    def spread_row(kept, other):
        got = jnp.where(q == z, kept, jnp.zeros_like(kept))
        for k in range(1, quad):
            source = kept if k % 2 == 0 else other
            got = got + place.move(
                source, lambda b, q, z, k=k: (b, q ^ k, z) if q == z else None
            )
        return got

    home_b = half_first(hidden_in, z % 2)
    home_seg = half_first(segment_ids.reshape(-1), z % 2)
    home_same = home_seg[:, None] == home_seg[None, :]
    grad_in = out_grad * loss_mask.reshape(-1)[:, None].astype(BF)
    grad_in = half_first(grad_in, z % 2)
    row_seg = place.swap(home_seg)
    row_same = row_seg[:, None] == row_seg[None, :]
    hidden_rows = spread_row(home_b[:half], home_b[half:]).astype(F32)
    grad_y = spread_row(grad_in[:half], grad_in[half:]).astype(F32)

    flat_home = w_qkv[0].reshape(features, 3 * width)
    kept = []
    hidden_b = None
    final_rows = None
    for layer_no in range(layers):
        if layer_no == 0:
            qkv, log_sum, mixed = attention_forward(home_b, flat_home, b_query_value[0], home_same)
            mixed = place.swap(mixed)
        else:
            qkv, log_sum, mixed = attention_forward(
                hidden_b, plane_qkv[layer_no], plane_bqv[layer_no], row_same
            )
        attended = quad_sum(place, dot_f(mixed, plane_out[layer_no])) + branch_bias[layer_no, 0]
        pre_one = hidden_rows + attended
        normed = layer_norm(pre_one, norm_gain[layer_no, 0], norm_shift[layer_no, 0])
        normed_b = quad_gather(place, normed.astype(BF))
        upper = (
            jnp.einsum("td,fd->tf", normed_b, plane_up[layer_no], preferred_element_type=F32)
            + plane_b_up[layer_no]
        )
        activ = gelu_exact(upper).astype(BF)
        branch = quad_sum(place, dot_f(activ, plane_down[layer_no])) + branch_bias[layer_no, 1]
        pre_two = normed + branch
        out_rows = layer_norm(pre_two, norm_gain[layer_no, 1], norm_shift[layer_no, 1])
        kept.append((hidden_b, qkv, log_sum, mixed, pre_one, normed_b, upper, pre_two))
        if layer_no + 1 < layers:
            out_low = out_rows.astype(BF)
            hidden_b = quad_gather(place, out_low)
            hidden_rows = out_low.astype(F32)
        else:
            final_rows = out_rows

    quarter = half // 2

    def rows_home(values):
        part = lax.dynamic_slice_in_dim(values, (q // 2) * quarter, quarter, 0)
        return place.move(part, lambda b, q, z: (b, z, 2 * (q % 2) + q // 2))

    final_out = rows_home(final_rows)

    pieces = {}
    small = {}

    def unit_share(grads):
        parts = grads.reshape(quad, blocks, cell, features)
        shared = share_over_blocks(place, parts, 1)
        shared = lax.psum_scatter(shared.astype(BF), "tp", scatter_dimension=0, tiled=False)
        return shared

    def head_share(grads):
        parts = grads.reshape(blocks, quad, -1, grads.shape[-1])
        shared = share_over_blocks(place, parts, 0)
        shared = lax.psum_scatter(shared.astype(BF), "tp", scatter_dimension=0, tiled=False)
        return place.swap(shared)

    for layer_no in reversed(range(layers)):
        layer_in, qkv, log_sum, mixed, pre_one, normed_b, upper, pre_two = kept[layer_no]
        grad_pre2, gain_two, shift_two = norm_backward(pre_two, norm_gain[layer_no, 1], grad_y)
        low = grad_pre2.astype(BF)
        bias_two = jnp.sum(low.astype(F32), axis=0)
        grad_branch = quad_gather(place, low)
        activ_f, pull_gelu = jax.vjp(gelu_exact, upper)
        grad_activ = jnp.einsum(
            "td,fd->tf", grad_branch, plane_down[layer_no], preferred_element_type=F32
        )
        grad_upper = pull_gelu(grad_activ)[0].astype(BF)
        grad_normed = grad_pre2 + quad_sum(place, dot_f(grad_upper, plane_up[layer_no]))
        dw_down = jnp.einsum(
            "tf,td->fd", activ_f.astype(BF), grad_branch, preferred_element_type=F32
        )
        dw_up = jnp.einsum("tf,td->fd", grad_upper, normed_b, preferred_element_type=F32)
        pieces["down", layer_no] = unit_share(dw_down)
        pieces["up", layer_no] = unit_share(dw_up)
        d_bup = jnp.sum(grad_upper.astype(F32), axis=0).reshape(quad, blocks, cell)
        grad_pre1, gain_one, shift_one = norm_backward(
            pre_one, norm_gain[layer_no, 0], grad_normed
        )
        low = grad_pre1.astype(BF)
        bias_one = jnp.sum(low.astype(F32), axis=0)
        grad_att = quad_gather(place, low)
        small[layer_no] = (
            jnp.stack([bias_one, bias_two, gain_one, gain_two, shift_one, shift_two]),
            d_bup,
        )
        grad_mixed = jnp.einsum(
            "td,xd->tx", grad_att, plane_out[layer_no], preferred_element_type=F32
        ).astype(BF)
        dw_out = jnp.einsum("tx,td->xd", mixed, grad_att, preferred_element_type=F32)
        pieces["out", layer_no] = head_share(dw_out)
        if layer_no:
            grad_qkv = attention_backward(qkv, log_sum, grad_mixed, row_same)
            part = jnp.einsum(
                "tx,dx->td", grad_qkv, plane_qkv[layer_no], preferred_element_type=F32
            )
            grad_y = grad_pre1 + quad_sum(place, part)
            dw_qkv = jnp.einsum("td,tx->dx", layer_in, grad_qkv, preferred_element_type=F32)
            pieces["qkv", layer_no] = head_share(dw_qkv)
            sums = jnp.sum(grad_qkv.astype(F32), axis=0).reshape(3, width)
            small["bqv", layer_no] = jnp.stack([sums[0], sums[2]])
        else:
            kept_rows = rows_home(grad_pre1)
            grad_qkv = attention_backward(qkv, log_sum, place.swap(grad_mixed), home_same)
            part = jnp.einsum("tx,dx->td", grad_qkv, flat_home, preferred_element_type=F32)
            part = half_first(part.astype(BF), z % 2)
            input_grad = kept_rows + lax.psum_scatter(
                part, "tp", scatter_dimension=0, tiled=True
            ).astype(F32)
            dw_qkv = jnp.einsum("td,tx->dx", home_b, grad_qkv, preferred_element_type=F32)
            pieces["qkv", layer_no] = lax.psum_scatter(
                dw_qkv.astype(BF), "dp", scatter_dimension=0, tiled=True
            )
            sums = jnp.sum(grad_qkv.astype(F32), axis=0).reshape(3, width)
            small["bqv", layer_no] = jnp.stack([sums[0], sums[2]])

    rows_part = jnp.stack([small[n][0] for n in range(layers)]) * 0.5
    bup_zero = jnp.zeros((quad, layers, blocks, quad, cell), F32)
    bup_mine = jnp.stack([small[n][1] for n in range(layers)], axis=1)
    bup_part = lax.dynamic_update_slice_in_dim(bup_zero, bup_mine[:, :, :, None], q, 3)
    bqv_part = jnp.zeros((layers, 2, quad, width), F32)
    home_slot = (jnp.arange(quad) == z)[None, :, None]
    plane_slot = (jnp.arange(quad) == q)[None, :, None]
    bqv_part = jnp.stack(
        [
            jnp.where(plane_slot if n else home_slot, small["bqv", n][:, None], 0.0)
            for n in range(layers)
        ]
    )
    flat = jnp.concatenate([rows_part.reshape(-1), bup_part.reshape(-1), bqv_part.reshape(-1)])
    steps = [lambda b, q, z, k=k: (b, q ^ k, z) for k in (1, 2)]
    steps += [lambda b, q, z, k=k: (b, q, z ^ k) for k in (1, 2)]
    count = 1
    while count < blocks:
        steps.append(lambda b, q, z, k=count: (b ^ k, q, z))
        count *= 2
    total = add_over(place, flat, steps)
    n_rows, n_bup = rows_part.size, bup_part.size
    rows_all = total[:n_rows].reshape(layers, 6, features)
    bup_all = total[n_rows : n_rows + n_bup].reshape(quad, layers, hidden_units)
    bqv_all = total[n_rows + n_bup :].reshape(layers, 2, quad, width)
    grad_bup = lax.dynamic_index_in_dim(bup_all, z, 0, keepdims=False)
    grad_bqv = lax.dynamic_index_in_dim(bqv_all, z, 2, keepdims=False)

    def whole(name):
        return [
            lax.all_gather(pieces[name, n], "dp", axis=0, tiled=True).astype(F32)
            for n in range(layers)
        ]

    grad_qkv_all = jnp.stack([g.reshape(features, 3, width) for g in whole("qkv")])
    grad_out_all = jnp.stack(whole("out"))
    grad_up_all = jnp.stack([g.T for g in whole("up")])
    grad_down_all = jnp.stack(whole("down"))
    return (
        final_out,
        input_grad,
        grad_qkv_all,
        grad_bqv,
        grad_out_all,
        rows_all[:, 0:2],
        rows_all[:, 2:4],
        rows_all[:, 4:6],
        grad_up_all,
        grad_bup,
        grad_down_all,
    )


def solution(mesh):
    return jax.shard_map(
        on_device,
        mesh=mesh,
        in_specs=(
            P("dp", None),
            P("dp", None),
            P("dp", None),
            P("dp", None),
            P(None, None, None, "tp"),
            P(None, None, "tp"),
            P(None, "tp", None),
            P(),
            P(),
            P(),
            P(None, None, "tp"),
            P(None, "tp"),
            P(None, "tp", None),
        ),
        out_specs=(
            P(("dp", "tp"), None),
            P(("dp", "tp"), None),
            P(None, None, None, "tp"),
            P(None, None, "tp"),
            P(None, "tp", None),
            P(),
            P(),
            P(),
            P(None, None, "tp"),
            P(None, "tp"),
            P(None, "tp", None),
        ),
        check_vma=False,
    )
```

```python
import functools

import jax
import jax.numpy as jnp
from jax import lax
from jax.experimental import pallas as pl
from jax.experimental.pallas import tpu as pltpu
from jax.sharding import Mesh
from jax.sharding import PartitionSpec as P

HEAD_DIM = 64
EPS = 1e-06
NEG = -1e30
EXTRA = 16
AXES = ("far", "u", "v", "c", "tp")
BF = jnp.bfloat16
F32 = jnp.float32
VMEM_BYTES = 48 << 20


class Place:
    def __init__(self):
        self.fars = lax.axis_size("far")
        self.core_no = lax.axis_index("c")
        self.z = lax.axis_index("tp")
        self.native = self.core_no == self.z // 2
        chip = lax.axis_index("u") * 2 + lax.axis_index("v")
        self.vector = jnp.stack(
            [chip, self.core_no, self.z, self.native.astype(jnp.int32)]
        ).astype(jnp.int32)

    def move(self, values, where):
        pairs = []
        for far in range(self.fars):
            for chip in range(4):
                for c in range(2):
                    for z in range(4):
                        to = where(chip, c, z)
                        if to is not None:
                            base = far * 4
                            source = ((base + chip) * 2 + c) * 4 + z
                            target = ((base + to[0]) * 2 + to[1]) * 4 + to[2]
                            pairs.append((source, target))
        return lax.ppermute(values, AXES, pairs)

    def core(self, values):
        return self.move(values, lambda i, c, z: (i, c ^ 1, z))

    def to_foreign(self, values):
        return self.move(values, lambda i, c, z: (i, c ^ 1, z) if c == z // 2 else None)

    def side(self, values):
        return self.move(values, lambda i, c, z: (i, c, z ^ 1))

    def cross(self, values):
        return self.move(values, lambda i, c, z: (i, c ^ 1, z ^ 2) if c != z // 2 else None)

    def mix(self, values):
        def where(i, c, z):
            return (i, c ^ 1, z) if c == z // 2 else (i, c, z ^ 2)

        return self.move(values, where)

    def chip(self, values, k, native=None):
        def where(i, c, z):
            if native is None or native == (c == z // 2):
                return (i ^ k, c, z)
            return None

        return self.move(values, where)

    def add_far(self, values):
        step = 1
        while step < self.fars:
            pairs = []
            for far in range(self.fars):
                pairs += [(far * 32 + i, (far ^ step) * 32 + i) for i in range(32)]
            got = lax.ppermute(values, AXES, pairs)
            values = (values.astype(F32) + got.astype(F32)).astype(values.dtype)
            step *= 2
        return values


class Layer:
    def __init__(self, whole, n):
        self.whole, self.n = whole, n


def run(name, kernel, outs, *args, scratch=(), after=(), hbm=(), hbm_out=(), cost=1):
    n = len(args)

    def body(*refs):
        kernel(*refs[:n], *refs[n + len(after) :])

    anywhere = pl.BlockSpec(memory_space=pl.ANY)
    vmem = pl.BlockSpec(memory_space=pltpu.VMEM)
    in_specs, given = [pl.BlockSpec(memory_space=pltpu.SMEM)], [args[0]]
    for i in range(1, n):
        arg = args[i]
        if isinstance(arg, Layer):
            block = (None,) + arg.whole.shape[1:]
            zeros = (0,) * (arg.whole.ndim - 1)
            in_specs.append(pl.BlockSpec(block, lambda i, at=(arg.n,) + zeros: at))
            given.append(arg.whole)
        else:
            in_specs.append(anywhere if i in hbm else vmem)
            given.append(arg)
    in_specs += [anywhere] * len(after)
    return pl.pallas_call(
        body,
        name=name,
        grid=(1,) if any(isinstance(arg, Layer) for arg in args) else (),
        out_shape=[jax.ShapeDtypeStruct(s, d) for s, d in outs],
        in_specs=in_specs,
        out_specs=[anywhere if i in hbm_out else vmem for i in range(len(outs))],
        scratch_shapes=list(scratch),
        cost_estimate=pl.CostEstimate(
            flops=cost * 10**9, bytes_accessed=10**6, transcendentals=0
        ),
        compiler_params=pltpu.CompilerParams(vmem_limit_bytes=VMEM_BYTES),
    )(*given, *after)


def dot_nn(a, b):
    return lax.dot_general(a, b, (((1,), (0,)), ((), ())), preferred_element_type=F32)


def dot_nt(a, b):
    return lax.dot_general(a, b, (((1,), (1,)), ((), ())), preferred_element_type=F32)


def dot_tn(a, b):
    return lax.dot_general(a, b, (((0,), (0,)), ((), ())), preferred_element_type=F32)


def thirds(value):
    hi = value.astype(BF).astype(F32)
    mid = (value - hi).astype(BF).astype(F32)
    return hi, mid, value - hi - mid


def extra_rows(rows, columns):
    padded = [
        jnp.concatenate([r, jnp.zeros((1, columns - r.shape[1]), F32)], axis=1)
        if r.shape[1] < columns
        else r
        for r in rows
    ]
    return jnp.concatenate(padded + [jnp.zeros((EXTRA - len(rows), columns), F32)], axis=0)


def multiple(index, size):
    return pl.ds(pl.multiple_of(index * size, size), size)


def copy_all(pairs, sem):
    copies = [pltpu.make_async_copy(a, b, sem.at[i]) for i, (a, b) in enumerate(pairs)]
    for copy in copies:
        copy.start()
    for copy in copies:
        copy.wait()


def pack_units(place, up, down, bias, piece, tail, sem, n):
    rows = up.shape[1] // 4
    at = multiple(place[0], rows)
    tail[...] = extra_rows(thirds(bias[n : n + 1]), up.shape[2]).astype(BF)
    copy_all(
        [
            (up.at[n, at], piece.at[0:rows]),
            (down.at[n, at], piece.at[rows : 2 * rows]),
            (tail, piece.at[2 * rows :]),
        ],
        sem,
    )


def head_biases(bias):
    both = jnp.concatenate([bias[0:1], bias[1:2]], axis=1)
    return extra_rows(thirds(both), 4 * bias.shape[1]).astype(BF)


def pack_heads(place, qkv_w, out_w, bias, piece, tail, sem, n):
    rows = out_w.shape[1]
    chip = place[0]
    inner = qkv_w.shape[1] // rows
    tail[...] = head_biases(bias)

    @pl.when(chip < inner)
    def _():
        copy_all([(qkv_w.at[n, multiple(chip, rows)], piece.at[0:rows])], sem)

    @pl.when(chip >= inner)
    def _():
        copy_all([(out_w.at[n], piece.at[0:rows])], sem)

    copy_all([(tail, piece.at[rows:])], sem)


def pack_inner(place, qkv_w, bias, pack, tail, sem):
    inner = qkv_w.shape[1]
    tail[...] = head_biases(bias)
    copy_all([(qkv_w.at[0], pack.at[0:inner]), (tail, pack.at[inner:])], sem)


def pack_rows(place, hidden, grad, seg, mask, own, other):
    c = place[1]
    tokens, features = hidden.shape
    half = tokens // 2
    for ref, first in ((own, c), (other, 1 - c)):
        ids = []
        for i, h in enumerate((first, 1 - first)):
            at = multiple(h, half)
            ref[i * half : (i + 1) * half] = hidden[at]
            ids.append(seg[0:1, at])
        at = multiple(first, half)
        scale = seg_column(mask[0:1, at].astype(F32))
        ref[tokens : tokens + half] = (grad[at].astype(F32) * scale).astype(BF)
        ids = jnp.concatenate(ids, axis=1).astype(F32)
        ref[tokens + half :] = extra_rows([ids], features).astype(BF)


def piece_pairs(pieces, chip):
    if len(pieces) == 1:
        return [(pieces[0].at[p], p) for p in range(4)]
    return [(ref, chip ^ k) for k, ref in enumerate(pieces)]


def choose_units(place, up, down, bias, *refs, n):
    *pieces, both, bias_out, tail, sem = refs
    chip, native = place[0], place[3]
    rows = up.shape[1] // 4

    @pl.when(native == 1)
    def _():
        copy_all([(up.at[n], both.at[0]), (down.at[n], both.at[1])], sem)
        bias_out[...] = bias[n : n + 1]

    @pl.when(native == 0)
    def _():
        given = piece_pairs(pieces, chip)
        pairs = [(given[0][0].at[2 * rows : 2 * rows + EXTRA], tail)]
        for ref, p in given:
            for m in range(2):
                pairs.append((ref.at[m * rows : (m + 1) * rows], both.at[m, multiple(p, rows)]))
        copy_all(pairs, sem)
        parts = tail[...].astype(F32)
        bias_out[...] = parts[0:1] + parts[1:2] + parts[2:3]


def inner_bias(tail, width):
    parts = tail.astype(F32)
    row = parts[0:1] + parts[1:2] + parts[2:3]
    return qkv_bias(row[:, :width], row[:, width : 2 * width])


def choose_heads(place, qkv_w, out_w, bias, *refs, n):
    *pieces, matrix, bias_out, tail, sem = refs
    chip, native = place[0], place[3]
    rows = out_w.shape[1]
    inner = qkv_w.shape[1]

    @pl.when(native == 1)
    def _():
        copy_all([(qkv_w.at[n], matrix.at[0:inner]), (out_w.at[n], matrix.at[inner:])], sem)
        bias_out[...] = qkv_bias(bias[0:1], bias[1:2])

    @pl.when(native == 0)
    def _():
        given = piece_pairs(pieces, chip)
        pairs = [(given[0][0].at[rows : rows + EXTRA], tail)]
        pairs += [(ref.at[0:rows], matrix.at[multiple(p, rows)]) for ref, p in given]
        copy_all(pairs, sem)
        bias_out[...] = inner_bias(tail[...], rows)


def choose_first(place, qkv_w, out_w, bias, got_inner, got_out, matrix, bias_out, tail, sem):
    native = place[3]
    inner = qkv_w.shape[1]

    @pl.when(native == 1)
    def _():
        copy_all([(qkv_w.at[0], matrix.at[0:inner]), (out_w.at[0], matrix.at[inner:])], sem)
        bias_out[...] = qkv_bias(bias[0:1], bias[1:2])

    @pl.when(native == 0)
    def _():
        pairs = [
            (got_inner.at[0:inner], matrix.at[0:inner]),
            (got_out, matrix.at[inner:]),
            (got_inner.at[inner:], tail),
        ]
        copy_all(pairs, sem)
        bias_out[...] = inner_bias(tail[...], inner // 3)


def seg_column(seg_row):
    n = seg_row.shape[1]
    parts = [
        jnp.broadcast_to(seg_row[:, i : i + 128], (128, 128)).T[:, 0:1] for i in range(0, n, 128)
    ]
    return jnp.concatenate(parts, axis=0)


def attend(qkv, seg_row, mixed, lse, tile):
    tokens = qkv.shape[0]
    width = qkv.shape[1] // 3
    heads = width // HEAD_DIM
    column = seg_column(seg_row)
    for start in range(0, tokens, tile):
        same = column[start : start + tile] == seg_row
        outs, logs = [], []
        for head in range(heads):
            at = head * HEAD_DIM
            query = qkv[start : start + tile, at : at + HEAD_DIM] * HEAD_DIM ** (-0.5)
            keys = qkv[:, width + at : width + at + HEAD_DIM]
            values = qkv[:, 2 * width + at : 2 * width + at + HEAD_DIM]
            scores = jnp.where(same, dot_nt(query, keys), NEG)
            top = jnp.max(scores, axis=1, keepdims=True)
            expon = jnp.exp(scores - top)
            total = jnp.sum(expon, axis=1, keepdims=True)
            outs.append(dot_nn(expon.astype(BF), values) / total)
            logs.append(top + jnp.log(total))
        mixed[start : start + tile] = jnp.concatenate(outs, axis=1).astype(BF)
        logs.append(jnp.zeros((tile, lse.shape[1] - heads), F32))
        lse[start : start + tile] = jnp.concatenate(logs, axis=1)


def qkv_bias(bias_q, bias_v):
    return jnp.concatenate([bias_q, jnp.zeros_like(bias_q), bias_v], axis=1)


def attention_home(place, hidden, weight, bias, seg, mixed, ordered, qkv, lse):
    first = place[2] // 2
    tokens = hidden.shape[0]
    half = tokens // 2
    ids = []
    for i, h in enumerate((first, 1 - first)):
        at = multiple(h, half)
        ordered[i * half : (i + 1) * half] = hidden[at]
        ids.append(seg[0:1, at])
    seg_row = jnp.concatenate(ids, axis=1).astype(F32)
    qkv[...] = (dot_nt(ordered[...], weight[...]) + qkv_bias(bias[0:1], bias[1:2])).astype(BF)
    attend(qkv, seg_row, mixed, lse, half)


def put_half(part, keep, send):
    half = part.shape[0] // 2
    keep[...] = part[:half]
    send[...] = part[half:].astype(BF)


def project_first(place, mixed, mixed_got, out_w, out_got, kept, keep, send):
    native = place[3] == 1
    rows = jnp.where(native, out_w[...], out_got[...])
    values = jnp.where(native, mixed[...], mixed_got[...])
    kept[...] = values
    put_half(dot_nn(values, rows), keep, send)


def seg_of(pack, tokens):
    return pack[-EXTRA:].astype(F32)[0:1, :tokens]


def attention_again(place, pack, matrix, bias, qkv, lse, mixed):
    tokens, inner = qkv.shape
    qkv[...] = (dot_nt(pack[:tokens], matrix[:inner]) + bias[...]).astype(BF)
    attend(qkv, seg_of(pack, tokens), mixed, lse, tokens // 2)


def attention_column(place, own, got, matrix, bias, pack, qkv, mixed, lse, keep, send):
    tokens, inner = qkv.shape
    hidden = jnp.concatenate([own[...], got[...]], axis=0)
    qkv[...] = (dot_nt(hidden, matrix[:inner]) + bias[...]).astype(BF)
    attend(qkv, seg_of(pack, tokens), mixed, lse, tokens // 2)
    put_half(dot_nn(mixed[...], matrix[inner:]), keep, send)


def attend_back(qkv, lse, grad_mixed, seg_row, grad_qkv, tile):
    tokens = qkv.shape[0]
    width = qkv.shape[1] // 3
    heads = width // HEAD_DIM
    column = seg_column(seg_row)
    scale = HEAD_DIM ** (-0.5)
    grads = [[], [], []]
    for head in range(heads):
        at = head * HEAD_DIM
        keys = qkv[:, width + at : width + at + HEAD_DIM]
        values = qkv[:, 2 * width + at : 2 * width + at + HEAD_DIM]
        grad_keys = jnp.zeros((tokens, HEAD_DIM), F32)
        grad_values = jnp.zeros((tokens, HEAD_DIM), F32)
        grad_query = []
        for start in range(0, tokens, tile):
            rows = slice(start, start + tile)
            query = qkv[rows, at : at + HEAD_DIM] * scale
            grad_out = grad_mixed[rows, at : at + HEAD_DIM]
            scores = jnp.where(column[rows] == seg_row, dot_nt(query, keys), NEG)
            probs = jnp.exp(scores - lse[rows, head : head + 1])
            grad_probs = dot_nt(grad_out, values)
            inner = jnp.sum(probs * grad_probs, axis=1, keepdims=True)
            grad_scores = (probs * (grad_probs - inner)).astype(BF)
            grad_query.append(dot_nn(grad_scores, keys) * scale)
            grad_keys += dot_tn(grad_scores, query)
            grad_values += dot_tn(probs.astype(BF), grad_out)
        grads[0].append(jnp.concatenate(grad_query, axis=0))
        grads[1].append(grad_keys)
        grads[2].append(grad_values)
    grad_qkv[...] = jnp.concatenate(grads[0] + grads[1] + grads[2], axis=1).astype(BF)


def attention_back(place, own, got, matrix, qkv, lse, pack, grad_qkv, keep, send):
    tokens, inner = qkv.shape
    grad_att = jnp.concatenate([own[...], got[...]], axis=0)
    grad_mixed = dot_nt(grad_att, matrix[inner:]).astype(BF)
    attend_back(qkv, lse, grad_mixed, seg_of(pack, tokens), grad_qkv, tokens // 2)
    put_half(dot_nn(grad_qkv[...], matrix[:inner]), keep, send)


def part_rows(place, whole_a, whole_b, sums):
    features = whole_a[0].shape[1]
    for p in range(4):
        a = jnp.concatenate([whole_a[p], extra_rows(sums if p == 0 else [], features)], axis=0)
        b = jnp.concatenate([whole_b[p], extra_rows([], features)], axis=0)
        yield p, a.astype(BF), b.astype(BF)


def put_direct(place, whole_a, whole_b, sums, *refs):
    for p, a, b in part_rows(place, whole_a, whole_b, sums):
        part = jnp.concatenate([a, b], axis=0)
        for k, ref in enumerate(refs):

            @pl.when(place[0] ^ p == k)
            def _(ref=ref):
                ref[...] = part


def put_staged(place, whole_a, whole_b, sums, keep_a, send_a, keep_b, send_b):
    for p, a, b in part_rows(place, whole_a, whole_b, sums):
        offset = place[0] ^ p
        over_u, over_v = offset // 2, offset % 2

        @pl.when(over_v == 0)
        def _():
            keep_a[over_u] = a

        @pl.when(over_v == 1)
        def _():
            send_a[over_u] = a

        @pl.when(over_u == 0)
        def _():
            keep_b[over_v] = b

        @pl.when(over_u == 1)
        def _():
            send_b[over_v] = b


def head_grads(place, hidden, grad_qkv, mixed, a_own, a_got, sums, *parts):
    grad_att = jnp.concatenate([a_own[...], a_got[...]], axis=0)
    whole = jnp.concatenate([dot_tn(grad_qkv[...], hidden), dot_tn(mixed[...], grad_att)], axis=0)
    bias = jnp.sum(grad_qkv[...].astype(F32), axis=0, keepdims=True)
    rows = whole.shape[0] // 4
    cut = rows // 2
    first = [whole[p * rows : p * rows + cut] for p in range(4)]
    second = [whole[p * rows + cut : (p + 1) * rows] for p in range(4)]
    put_direct(place, first, second, [bias] + sums, *parts)


def head_grads_first(place, pack, grad_qkv, mixed, a_own, a_got, sums, got, *parts):
    total = [(sums[i : i + 1] + got[i : i + 1]) * 0.5 for i in range(sums.shape[0])]
    hidden = pack[: grad_qkv.shape[0]]
    head_grads(place, hidden, grad_qkv, mixed, a_own, a_got, total, *parts)


def head_grads_later(place, own, got, grad_qkv, mixed, a_own, a_got, *parts):
    hidden = jnp.concatenate([own[...], got[...]], axis=0)
    head_grads(place, hidden, grad_qkv, mixed, a_own, a_got, [], *parts)


def feed_forward(place, own, got, weights, bias, activ, slope, keep, send):
    hidden = jnp.concatenate([own[...], got[...]], axis=0)
    upper = dot_nn(hidden, weights[0]) + bias[...]
    cdf = 0.5 * (1.0 + lax.erf(upper * (0.5**0.5)))
    activ[...] = (upper * cdf).astype(BF)
    slope[...] = cdf + upper * jnp.exp(-0.5 * upper * upper) * 0.3989422804014327
    put_half(dot_nn(activ[...], weights[1]), keep, send)


def feed_back(place, own, got, weights, slope, grad_upper, keep, send):
    grad = jnp.concatenate([own[...], got[...]], axis=0)
    grad_upper[...] = (dot_nt(grad, weights[1]) * slope[...]).astype(BF)
    put_half(dot_nt(grad_upper[...], weights[0]), keep, send)


def unit_grads(place, x_own, x_got, g_own, g_got, activ, grad_upper, *parts):
    hidden = jnp.concatenate([x_own[...], x_got[...]], axis=0)
    grad = jnp.concatenate([g_own[...], g_got[...]], axis=0)
    up = dot_tn(hidden, grad_upper[...])
    down = dot_tn(activ[...], grad)
    bias = jnp.sum(grad_upper[...].astype(F32), axis=0, keepdims=True)
    rows = up.shape[0] // 4
    first = [up[p * rows : (p + 1) * rows] for p in range(4)]
    second = [down[p * rows : (p + 1) * rows] for p in range(4)]
    put_staged(place, first, second, [bias], *parts)


def chip_sum(place, keep, got, chip, low):
    chip[...] = keep[...] + got[...].astype(F32)
    low[...] = chip[...].astype(BF)


def combine_one(place, keep_a, got_a, keep_b, got_b, mine_a, for_a, mine_b, for_b):
    mine_a[...] = keep_a[0].astype(F32) + got_a[0].astype(F32)
    for_a[...] = (keep_a[1].astype(F32) + got_a[1].astype(F32)).astype(BF)
    mine_b[...] = keep_b[0].astype(F32) + got_b[0].astype(F32)
    for_b[...] = (keep_b[1].astype(F32) + got_b[1].astype(F32)).astype(BF)


def put_sum(place, a, b, at, mine, mixed, crossed):
    low_a, low_b = a.astype(BF), b.astype(BF)
    mine[at] = low_a
    mixed[at] = jnp.where(place[3] == 1, low_b, low_a)
    crossed[at] = low_b


def combine_staged(place, mine_a, got_a, mine_b, got_b, mine, mixed, crossed):
    a = mine_a[...] + got_a[...].astype(F32)
    b = mine_b[...] + got_b[...].astype(F32)
    put_sum(place, a, b, slice(0, a.shape[0]), mine, mixed, crossed)


def add_chips(refs):
    terms = [ref[...].astype(F32) for ref in refs]
    return (terms[0] + terms[1]) + (terms[2] + terms[3])


def combine_direct(place, own, got1, got2, got3, mine, mixed, crossed):
    total = add_chips((own, got1, got2, got3))
    half = total.shape[0] // 2
    put_sum(place, total[:half], total[half:], slice(0, half), mine, mixed, crossed)


def combine_both(place, mine_a, got_a, mine_b, got_b, own, got1, got2, got3, mine, mixed, crossed):
    a = mine_a[...] + got_a[...].astype(F32)
    b = mine_b[...] + got_b[...].astype(F32)
    rows = a.shape[0]
    put_sum(place, a, b, slice(0, rows), mine, mixed, crossed)
    total = add_chips((own, got1, got2, got3))
    half = total.shape[0] // 2
    put_sum(place, total[:half], total[half:], slice(rows, rows + half), mine, mixed, crossed)


def combine_planes(place, *refs):
    *groups, out = refs
    start = 0
    for i in range(0, len(groups), 3):
        mine, mixed, crossed = groups[i : i + 3]
        rows = mine.shape[0]
        first = jnp.where(place[3] == 1, mine[...], crossed[...])
        out[start : start + rows] = (first.astype(F32) + mixed[...].astype(F32)).astype(BF)
        start += rows


def normalize(values):
    center = values - jnp.mean(values, axis=1, keepdims=True)
    spread = jnp.mean(center * center, axis=1, keepdims=True)
    inv = lax.rsqrt(spread + EPS)
    return center * inv, inv


def norm_forward(place, base, chip, got, bias, gain, shift, total, out, low):
    values = base[...].astype(F32) + (chip[...] + got[...].astype(F32) + bias[...])
    total[...] = values
    unit, _ = normalize(values)
    result = unit * gain[...] + shift[...]
    out[...] = result
    low[...] = result.astype(BF)


def back_through(values, gain, grad):
    unit, inv = normalize(values)
    scaled = grad * gain
    first = jnp.mean(scaled, axis=1, keepdims=True)
    second = jnp.mean(scaled * unit, axis=1, keepdims=True)
    back = inv * (scaled - first - unit * second)
    low = back.astype(BF)
    sums = jnp.concatenate(
        [
            jnp.sum(low.astype(F32), axis=0, keepdims=True),
            jnp.sum(grad * unit, axis=0, keepdims=True),
            jnp.sum(grad, axis=0, keepdims=True),
        ],
        axis=0,
    )
    return back, low, sums


def norm_turn(place, base, chip, got, bias, gain, shift, pack, final, back, low, sums):
    half = base.shape[0]
    quarter = half // 2
    values = base[...] + (chip[...] + got[...].astype(F32) + bias[...])
    unit, _ = normalize(values)
    back[...] = unit * gain[...] + shift[...]
    final[...] = back[multiple(place[2] % 2, quarter)]
    grad = pack[2 * half : 3 * half].astype(F32)
    back_value, low_value, sum_value = back_through(values, gain[...], grad)
    back[...] = back_value
    low[...] = low_value
    sums[...] = sum_value


def norm_backward(place, values, base, chip, got, gain, back, low, sums):
    grad = base[...] + (chip[...] + got[...].astype(F32))
    back[...], low[...], sums[...] = back_through(values[...], gain[...], grad)


def fetch_parts(place, refs, parts, sem, start, rows):
    chip, native = place[0], place[3]

    def copies(flip):
        pairs = []
        for i in range(2):
            for k in range(4):
                ref = refs[4 * (i ^ flip) + k]
                pairs.append((ref.at[start : start + rows], parts.at[i, chip ^ k]))
        copy_all(pairs, sem)

    @pl.when(native == 1)
    def _():
        copies(0)

    @pl.when(native == 0)
    def _():
        copies(1)


def unpack_units(place, *refs, earlier, start):
    up, down, small, parts, sem = refs[8 + earlier :]
    rows = up.shape[1] // 4
    fetch_parts(place, refs[:8], parts, sem, start, rows + EXTRA)
    for p in range(4):
        at = slice(p * rows, (p + 1) * rows)
        up[0, at] = parts[0, p, 0:rows].astype(F32)
        down[0, at] = parts[1, p, 0:rows].astype(F32)
    small[...] = parts[0, 0, rows:].astype(F32)


def unpack_heads(place, *refs, earlier, start):
    qkv, out, small, parts, sem = refs[8 + earlier :]
    cut = (qkv.shape[1] + out.shape[1]) // 8
    fetch_parts(place, refs[:8], parts, sem, start, cut + EXTRA)
    for p in range(4):
        for i in range(2):
            value = parts[i, p, 0:cut].astype(F32)
            at = (2 * p + i) * cut
            if at < qkv.shape[1]:
                qkv[0, at : at + cut] = value
            else:
                at -= qkv.shape[1]
                out[0, at : at + cut] = value
    small[...] = parts[0, 0, cut:].astype(F32)


def on_device(
    hidden_in,
    out_grad,
    segment_ids,
    loss_mask,
    w_qkv,
    b_query_value,
    w_out,
    branch_bias,
    norm_gain,
    norm_shift,
    w_up,
    b_up,
    w_down,
):
    place = Place()
    at = place.vector
    layers, features = w_qkv.shape[:2]
    width = w_qkv.shape[-1]
    inner = 3 * width
    tokens = hidden_in.shape[0]
    half, quarter = tokens // 2, tokens // 4
    units = w_up.shape[-1]
    unit_rows, head_rows = features // 4, (inner + width) // 4
    w_qkv_t = jnp.transpose(w_qkv, (0, 2, 3, 1)).reshape(layers, inner, features)

    def gain_of(n, i):
        return branch_bias[n, i][None], norm_gain[n, i][None], norm_shift[n, i][None]

    half_f = ((half, features), F32)
    half_b = ((half, features), BF)
    sums_of = ((3, features), F32)
    unit_piece = ((2 * unit_rows + EXTRA, features), BF)
    head_piece = ((head_rows + EXTRA, features), BF)
    sem = pltpu.SemaphoreType.DMA((9,))
    tail = pltpu.VMEM((EXTRA, features), BF)

    def spread_chips(values):
        return [values] + [place.chip(values, k, native=False) for k in (1, 2, 3)]

    def unit_weights(n, pieces, after=()):
        return run(
            "choose_units",
            functools.partial(choose_units, n=n),
            [((2, units, features), BF), ((1, units), F32)],
            at, w_up, w_down, b_up, *pieces,
            scratch=[tail, sem],
            hbm=(1, 2, 4, 5, 6, 7),
            hbm_out=(0,),
            after=after,
        )

    def unit_pack(n, after=()):
        return run(
            "pack_units",
            functools.partial(pack_units, n=n),
            [unit_piece],
            at, w_up, w_down, b_up,
            scratch=[tail, sem],
            hbm=(1, 2),
            hbm_out=(0,),
            after=after,
        )[0]

    def quad_sum(keep, send):
        chip = keep + place.core(send).astype(F32)
        return chip, place.side(chip.astype(BF))

    units1 = unit_pack(0)
    early = units1
    out_got = place.cross(w_out[0])
    units1 = place.cross(units1)
    row_pack = ((tokens + half + EXTRA, features), BF)
    pack_own, pack_other = run(
        "pack_rows",
        pack_rows,
        [row_pack, row_pack],
        at, hidden_in, out_grad, segment_ids, loss_mask,
        after=[early],
    )
    (mixed_home,) = run(
        "attention_home",
        attention_home,
        [((tokens, width), BF)],
        at, hidden_in, Layer(w_qkv_t, 0), Layer(b_query_value, 0), segment_ids,
        scratch=[
            pltpu.VMEM((tokens, features), BF),
            pltpu.VMEM((tokens, inner), BF),
            pltpu.VMEM((tokens, 128), F32),
        ],
        after=[pack_own],
    )
    mixed_got = place.cross(mixed_home)
    pack = jnp.where(place.native, pack_own, place.to_foreign(pack_other))

    def head_pack(n, after):
        return run(
            "pack_heads",
            functools.partial(pack_heads, n=n),
            [head_piece],
            at, w_qkv_t, w_out, Layer(b_query_value, n),
            scratch=[tail, sem],
            hbm=(1, 2),
            hbm_out=(0,),
            after=after,
        )[0]

    mixed1, keep, send = run(
        "project_first",
        project_first,
        [((tokens, width), BF), half_f, half_b],
        at, mixed_home, mixed_got, Layer(w_out, 0), out_got,
        after=[units1],
    )
    chip, low = run(
        "chip_sum",
        chip_sum,
        [half_f, half_b],
        at, keep, place.core(send),
    )
    others = place.side(low)
    heads2 = place.cross(head_pack(1, [low]))
    sum11, norm11, low11 = run(
        "norm_forward",
        norm_forward,
        [half_f, half_f, half_b],
        at, pack[:half], chip, others, *gain_of(0, 0),
    )
    got11 = place.core(low11)
    weights1, b_up1 = unit_weights(0, spread_chips(units1), after=[low11])
    ffn_outs = [((tokens, units), BF), ((tokens, units), F32), half_f, half_b]
    activ1, slope1, keep, send = run(
        "feed_forward",
        feed_forward,
        ffn_outs,
        at, low11, got11, weights1, b_up1,
        after=[heads2],
    )
    matrix_of = ((inner + width, features), BF)
    matrix2, bias2 = run(
        "choose_heads",
        functools.partial(choose_heads, n=1),
        [matrix_of, ((1, inner), F32)],
        at, w_qkv_t, w_out, Layer(b_query_value, 1), *spread_chips(heads2),
        scratch=[tail, sem],
        hbm=(1, 2, 4, 5, 6, 7),
        hbm_out=(0,),
    )
    units2 = place.cross(unit_pack(1, [send]))
    chip, others = quad_sum(keep, send)
    sum12, norm12, low12 = run(
        "norm_forward",
        norm_forward,
        [half_f, half_f, half_b],
        at, norm11, chip, others, *gain_of(0, 1),
        after=[matrix2, units2],
    )
    got12 = place.core(low12)
    lse_of = ((tokens, 128), F32)
    qkv2, mixed2, lse2, keep, send = run(
        "attention_column",
        attention_column,
        [((tokens, inner), BF), ((tokens, width), BF), lse_of, half_f, half_b],
        at, low12, got12, matrix2, bias2, pack,
    )
    weights2, b_up2 = unit_weights(1, spread_chips(units2))
    (inner1,) = run(
        "pack_inner",
        pack_inner,
        [((inner + EXTRA, features), BF)],
        at, w_qkv_t, Layer(b_query_value, 0),
        scratch=[tail, sem],
        hbm=(1,),
        hbm_out=(0,),
        after=[low12],
    )
    inner_got = place.cross(inner1)
    chip, others = quad_sum(keep, send)
    sum21, norm21, low21 = run(
        "norm_forward",
        norm_forward,
        [half_f, half_f, half_b],
        at, low12, chip, others, *gain_of(1, 0),
        after=[weights2, inner_got],
    )
    got21 = place.core(low21)
    activ2, slope2, keep, send = run(
        "feed_forward", feed_forward, ffn_outs, at, low21, got21, weights2, b_up2
    )
    matrix1, bias1 = run(
        "choose_first",
        choose_first,
        [matrix_of, ((1, inner), F32)],
        at, w_qkv_t, w_out, Layer(b_query_value, 0), inner_got, out_got,
        scratch=[tail, sem],
        hbm=(1, 2, 4, 5),
        hbm_out=(0,),
        after=[low21],
    )
    qkv1, lse1, _ = run(
        "attention_again",
        attention_again,
        [((tokens, inner), BF), lse_of, ((tokens, width), BF)],
        at, pack, matrix1, bias1,
        after=[send],
    )
    chip, others = quad_sum(keep, send)
    final, back, low, sums22 = run(
        "norm_turn",
        norm_turn,
        [((quarter, features), F32), half_f, half_b, sums_of],
        at, norm21, chip, others, *gain_of(1, 1), pack,
        after=[lse1],
    )
    final_got = place.cross(final)
    final_out = jnp.where(place.native, final, final_got)

    unit_half, head_half = unit_rows + EXTRA, head_rows // 2 + EXTRA
    unit_parts = [((2, unit_half, features), BF)] * 4
    head_parts = [((2 * head_half, features), BF)] * 4

    def send_direct(parts):
        return [parts[0]] + [place.chip(parts[k], k) for k in (1, 2, 3)]

    def send_staged(keep_a, send_a, keep_b, send_b):
        return keep_a, place.chip(send_a, 1), keep_b, place.chip(send_b, 2)

    def next_stage(parts, after=()):
        of = (unit_half, features)
        mine_a, for_a, mine_b, for_b = run(
            "combine_one",
            combine_one,
            [(of, F32), (of, BF), (of, F32), (of, BF)],
            at, *parts,
            after=after,
        )
        return mine_a, place.chip(for_a, 2), mine_b, place.chip(for_b, 1)

    def sum_chips(kernel, parts, rows, after=()):
        half_rows = ((rows, features), BF)
        mine, mixed, crossed = run(
            kernel.__name__, kernel, [half_rows] * 3, at, *parts, after=after
        )
        return mine, place.mix(mixed), place.cross(crossed)

    def sum_planes(groups, after=()):
        rows = sum(group[0].shape[0] for group in groups)
        (piece,) = run(
            "combine_planes",
            combine_planes,
            [((rows, features), BF)],
            at, *[part for group in groups for part in group],
            after=after,
        )
        piece = place.add_far(piece)
        pieces = [piece] + [place.chip(piece, k) for k in (1, 2, 3)]
        got = place.core(jnp.stack(pieces))
        return pieces + [got[k] for k in range(4)]

    grad_of = [((tokens, units), BF), half_f, half_b]
    back_of = [half_f, half_b, sums_of]
    inner_of = [((tokens, inner), BF), half_f, half_b]

    got = place.core(low)
    grad_upper2, keep, send = run(
        "feed_back", feed_back, grad_of, at, low, got, weights2, slope2
    )
    chip, others = quad_sum(keep, send)
    units2 = run(
        "unit_grads",
        unit_grads,
        unit_parts,
        at, low21, got21, low, got, activ2, grad_upper2,
        after=[send],
    )
    early = units2[0]
    units2 = send_staged(*units2)
    back, low, sums21 = run(
        "norm_backward",
        norm_backward,
        back_of,
        at, sum21, back, chip, others, norm_gain[1, 0][None],
        after=[early],
    )
    got = place.core(low)
    grad_qkv2, keep, send = run(
        "attention_back",
        attention_back,
        inner_of,
        at, low, got, matrix2, qkv2, lse2, pack,
        after=[final_got, units2[1], units2[3]],
    )
    chip, others = quad_sum(keep, send)
    heads2 = run(
        "head_grads",
        head_grads_later,
        head_parts,
        at, low12, got12, grad_qkv2, mixed2, low, got,
        after=[send],
    )
    units2 = next_stage(units2, after=[send])
    early = heads2[0]
    heads2 = send_direct(heads2)
    back, low, sums12 = run(
        "norm_backward",
        norm_backward,
        back_of,
        at, sum12, back, chip, others, norm_gain[0, 1][None],
        after=[early, units2[1], units2[3]],
    )
    got = place.core(low)
    grad_upper1, keep, send = run(
        "feed_back", feed_back, grad_of, at, low, got, weights1, slope1
    )
    chip, others = quad_sum(keep, send)
    units1 = run(
        "unit_grads",
        unit_grads,
        unit_parts,
        at, low11, got11, low, got, activ1, grad_upper1,
        after=[send],
    )
    early = units1[0]
    units1 = send_staged(*units1)
    later = sum_chips(combine_both, (*units2, *heads2), unit_half + head_half, after=[send])
    back, low, sums11 = run(
        "norm_backward",
        norm_backward,
        back_of,
        at, sum11, back, chip, others, norm_gain[0, 0][None],
        after=[early, later[0]],
    )
    got = place.core(low)
    sums = jnp.concatenate([sums11, sums12, sums21, sums22])
    sums = sums + place.core(sums)
    grad_qkv1, keep, send = run(
        "attention_back",
        attention_back,
        inner_of,
        at, low, got, matrix1, qkv1, lse1, pack,
        after=[units1[1], units1[3], sums],
    )
    heads1 = run(
        "head_grads",
        head_grads_first,
        head_parts,
        at, pack, grad_qkv1, mixed1, low, got, sums, place.side(sums),
        after=[send],
    )
    units1 = next_stage(units1, after=[send])
    early = heads1[0]
    heads1 = send_direct(heads1)
    chip = keep + place.core(send).astype(F32)
    chip = chip.reshape(2, quarter, features)
    mine = lax.dynamic_index_in_dim(chip, place.z % 2, 0, keepdims=False)
    other = lax.dynamic_index_in_dim(chip, 1 - place.z % 2, 0, keepdims=False)
    mine += lax.dynamic_index_in_dim(
        back.reshape(chip.shape), place.z % 2, 0, keepdims=False
    )
    rows = mine + place.side(other.astype(BF)).astype(F32)
    input_grad = jnp.where(place.native, rows, place.cross(rows))

    units1 = sum_chips(combine_staged, units1, unit_half, after=[early])
    later = sum_planes([later], after=[units1[0]])
    heads1 = sum_chips(combine_direct, heads1, head_half)
    first = sum_planes([units1, heads1])

    def write_layer(name, kernel, n, shapes, rows, given, earlier, start):
        return pl.pallas_call(
            functools.partial(kernel, earlier=len(earlier), start=start),
            name=name,
            grid=(1,),
            out_shape=[jax.ShapeDtypeStruct(s, F32) for s in shapes + [(EXTRA, features)]],
            in_specs=[pl.BlockSpec(memory_space=pltpu.SMEM)]
            + [pl.BlockSpec(memory_space=pl.ANY)] * (8 + len(earlier)),
            out_specs=[pl.BlockSpec((1,) + s[1:], lambda i: (n, 0, 0)) for s in shapes]
            + [pl.BlockSpec(memory_space=pltpu.VMEM)],
            input_output_aliases={9 + i: i for i in range(len(earlier))},
            scratch_shapes=[
                pltpu.VMEM((2, 4, rows, features), BF),
                pltpu.SemaphoreType.DMA((8,)),
            ],
            compiler_params=pltpu.CompilerParams(vmem_limit_bytes=VMEM_BYTES),
        )(at, *given, *earlier)

    unit_shapes = [(layers, features, units), (layers, units, features)]
    head_shapes = [(layers, inner, features), (layers, width, features)]

    def unpack(n, given, earlier):
        *ffn, ffn_small = write_layer(
            "unpack_units", unpack_units, n, unit_shapes, unit_half, given, earlier[:2], 0
        )
        *heads, head_small = write_layer(
            "unpack_heads", unpack_heads, n, head_shapes, head_half, given, earlier[2:], unit_half
        )
        return ffn + heads, ffn_small, head_small

    grads, small_u2, small_h2 = unpack(1, later, [])
    (up, down, qkv, out), small_u1, small_h1 = unpack(0, first, grads)
    total = small_h1[1:13].reshape(layers, 2, 3, features)
    small = jnp.stack([small_h1[0], small_h2[0]])
    sums = small[:, :inner].reshape(layers, 3, width)
    return (
        final_out,
        input_grad,
        jnp.transpose(qkv.reshape(layers, 3, width, features), (0, 3, 1, 2)),
        jnp.stack([sums[:, 0], sums[:, 2]], axis=1),
        out,
        total[:, :, 0],
        total[:, :, 1],
        total[:, :, 2],
        up,
        jnp.stack([small_u1[0], small_u2[0]]),
        down,
    )


def solution(mesh):
    columns = Mesh(mesh.devices.reshape(-1, 2, 2, 2, mesh.shape["tp"]), AXES)
    rows = P(AXES[:4], None)
    return jax.shard_map(
        on_device,
        mesh=columns,
        in_specs=(
            rows,
            rows,
            rows,
            rows,
            P(None, None, None, "tp"),
            P(None, None, "tp"),
            P(None, "tp", None),
            P(),
            P(),
            P(),
            P(None, None, "tp"),
            P(None, "tp"),
            P(None, "tp", None),
        ),
        out_specs=(
            P(AXES, None),
            P(AXES, None),
            P(None, None, None, "tp"),
            P(None, None, "tp"),
            P(None, "tp", None),
            P(),
            P(),
            P(),
            P(None, None, "tp"),
            P(None, "tp"),
            P(None, "tp", None),
        ),
        check_vma=False,
    )
```

```python
import functools

import jax
import jax.numpy as jnp
from jax import lax
from jax.experimental import pallas as pl
from jax.experimental.pallas import tpu as pltpu
from jax.sharding import Mesh
from jax.sharding import PartitionSpec as P

HEAD_DIM = 64
EPS = 1e-06
NEG = -1e30
EXTRA = 16
AXES = ("far", "u", "v", "c", "tp")
BF = jnp.bfloat16
F32 = jnp.float32
VMEM_BYTES = 48 << 20


class Place:
    def __init__(self):
        self.fars = lax.axis_size("far")
        self.core_no = lax.axis_index("c")
        self.z = lax.axis_index("tp")
        self.native = self.core_no == self.z // 2
        chip = lax.axis_index("u") * 2 + lax.axis_index("v")
        self.vector = jnp.stack(
            [chip, self.core_no, self.z, self.native.astype(jnp.int32)]
        ).astype(jnp.int32)

    def move(self, values, where):
        pairs = []
        for far in range(self.fars):
            for chip in range(4):
                for c in range(2):
                    for z in range(4):
                        to = where(chip, c, z)
                        if to is not None:
                            base = far * 4
                            source = ((base + chip) * 2 + c) * 4 + z
                            target = ((base + to[0]) * 2 + to[1]) * 4 + to[2]
                            pairs.append((source, target))
        return lax.ppermute(values, AXES, pairs)

    def core(self, values):
        return self.move(values, lambda i, c, z: (i, c ^ 1, z))

    def to_foreign(self, values):
        return self.move(values, lambda i, c, z: (i, c ^ 1, z) if c == z // 2 else None)

    def side(self, values):
        return self.move(values, lambda i, c, z: (i, c, z ^ 1))

    def cross(self, values):
        return self.move(values, lambda i, c, z: (i, c ^ 1, z ^ 2) if c != z // 2 else None)

    def mix(self, values):
        def where(i, c, z):
            return (i, c ^ 1, z) if c == z // 2 else (i, c, z ^ 2)

        return self.move(values, where)

    def chip(self, values, k, native=None):
        def where(i, c, z):
            if native is None or native == (c == z // 2):
                return (i ^ k, c, z)
            return None

        return self.move(values, where)

    def add_far(self, values):
        step = 1
        while step < self.fars:
            pairs = []
            for far in range(self.fars):
                pairs += [(far * 32 + i, (far ^ step) * 32 + i) for i in range(32)]
            got = lax.ppermute(values, AXES, pairs)
            values = (values.astype(F32) + got.astype(F32)).astype(values.dtype)
            step *= 2
        return values


class Layer:
    def __init__(self, whole, n):
        self.whole, self.n = whole, n


def run(name, kernel, outs, *args, scratch=(), after=(), hbm=(), hbm_out=(), cost=0):
    n = len(args)

    def body(*refs):
        kernel(*refs[:n], *refs[n + len(after) :])

    anywhere = pl.BlockSpec(memory_space=pl.ANY)
    vmem = pl.BlockSpec(memory_space=pltpu.VMEM)
    in_specs, given = [pl.BlockSpec(memory_space=pltpu.SMEM)], [args[0]]
    for i in range(1, n):
        arg = args[i]
        if isinstance(arg, Layer):
            block = (None,) + arg.whole.shape[1:]
            zeros = (0,) * (arg.whole.ndim - 1)
            in_specs.append(pl.BlockSpec(block, lambda i, at=(arg.n,) + zeros: at))
            given.append(arg.whole)
        else:
            in_specs.append(anywhere if i in hbm else vmem)
            given.append(arg)
    in_specs += [anywhere] * len(after)
    return pl.pallas_call(
        body,
        name=name,
        grid=(1,) if any(isinstance(arg, Layer) for arg in args) else (),
        out_shape=[jax.ShapeDtypeStruct(s, d) for s, d in outs],
        in_specs=in_specs,
        out_specs=[anywhere if i in hbm_out else vmem for i in range(len(outs))],
        scratch_shapes=list(scratch),
        cost_estimate=pl.CostEstimate(
            flops=cost * 10**9, bytes_accessed=0, transcendentals=0
        ),
        compiler_params=pltpu.CompilerParams(vmem_limit_bytes=VMEM_BYTES),
    )(*given, *after)


def dot_nn(a, b):
    return lax.dot_general(a, b, (((1,), (0,)), ((), ())), preferred_element_type=F32)


def dot_nt(a, b):
    return lax.dot_general(a, b, (((1,), (1,)), ((), ())), preferred_element_type=F32)


def dot_tn(a, b):
    return lax.dot_general(a, b, (((0,), (0,)), ((), ())), preferred_element_type=F32)


def thirds(value):
    hi = value.astype(BF).astype(F32)
    mid = (value - hi).astype(BF).astype(F32)
    return hi, mid, value - hi - mid


def extra_rows(rows, columns):
    padded = [
        jnp.concatenate([r, jnp.zeros((1, columns - r.shape[1]), F32)], axis=1)
        if r.shape[1] < columns
        else r
        for r in rows
    ]
    return jnp.concatenate(padded + [jnp.zeros((EXTRA - len(rows), columns), F32)], axis=0)


def multiple(index, size):
    return pl.ds(pl.multiple_of(index * size, size), size)


def copy_all(pairs, sem):
    copies = [pltpu.make_async_copy(a, b, sem.at[i]) for i, (a, b) in enumerate(pairs)]
    for copy in copies:
        copy.start()
    for copy in copies:
        copy.wait()


def pack_units(place, up, down, bias, piece, tail, sem, n, whole):
    rows = up.shape[1] if whole else up.shape[1] // 4
    at = slice(0, rows) if whole else multiple(place[0], rows)
    tail[...] = extra_rows(thirds(bias[n : n + 1]), up.shape[2]).astype(BF)
    copy_all(
        [
            (up.at[n, at], piece.at[0:rows]),
            (down.at[n, at], piece.at[rows : 2 * rows]),
            (tail, piece.at[2 * rows :]),
        ],
        sem,
    )


def head_biases(bias):
    both = jnp.concatenate([bias[0:1], bias[1:2]], axis=1)
    return extra_rows(thirds(both), 4 * bias.shape[1]).astype(BF)


def pack_heads(place, qkv_w, out_w, bias, pack, tail, sem):
    chip = place[0]
    rows, fewer = out_w.shape[1], qkv_w.shape[1] // 4
    inner = qkv_w.shape[1] // rows
    for n in range(2):
        tail[n] = head_biases(bias[n])
    second = rows + EXTRA

    @pl.when(chip < inner)
    def _():
        copy_all([(qkv_w.at[1, multiple(chip, rows)], pack.at[0:rows])], sem)

    @pl.when(chip >= inner)
    def _():
        copy_all([(out_w.at[1], pack.at[0:rows])], sem)

    copy_all(
        [
            (qkv_w.at[0, multiple(chip, fewer)], pack.at[second : second + fewer]),
            (tail.at[1], pack.at[rows:second]),
            (tail.at[0], pack.at[second + fewer :]),
        ],
        sem,
    )


def pack_rows(place, hidden, grad, seg, mask, own, other):
    c = place[1]
    tokens, features = hidden.shape
    half = tokens // 2
    for ref, first in ((own, c), (other, 1 - c)):
        ids = []
        for i, h in enumerate((first, 1 - first)):
            at = multiple(h, half)
            ref[i * half : (i + 1) * half] = hidden[at]
            ids.append(seg[0:1, at])
        at = multiple(first, half)
        scale = seg_column(mask[0:1, at].astype(F32))
        ref[tokens : tokens + half] = (grad[at].astype(F32) * scale).astype(BF)
        ids = jnp.concatenate(ids, axis=1).astype(F32)
        ref[tokens + half :] = extra_rows([ids], features).astype(BF)


def choose_units(place, up, down, bias, *refs, n):
    *pieces, both, bias_out, tail, sem = refs
    chip, native = place[0], place[3]
    rows = up.shape[1] // len(pieces)

    @pl.when(native == 1)
    def _():
        copy_all([(up.at[n], both.at[0]), (down.at[n], both.at[1])], sem)
        bias_out[...] = bias[n : n + 1]

    @pl.when(native == 0)
    def _():
        pairs = [(pieces[0].at[2 * rows :], tail)]
        for k, ref in enumerate(pieces):
            to = slice(0, rows) if len(pieces) == 1 else multiple(chip ^ k, rows)
            for m in range(2):
                pairs.append((ref.at[m * rows : (m + 1) * rows], both.at[m, to]))
        copy_all(pairs, sem)
        parts = tail[...].astype(F32)
        bias_out[...] = parts[0:1] + parts[1:2] + parts[2:3]


def choose_heads(place, qkv_w, out_w, bias, *refs, n):
    *pieces, matrix, bias_out, tail, sem = refs
    chip, native = place[0], place[3]
    width, inner = out_w.shape[1], qkv_w.shape[1]

    @pl.when(native == 1)
    def _():
        copy_all([(qkv_w.at[n], matrix.at[0:inner]), (out_w.at[n], matrix.at[inner:])], sem)
        bias_out[...] = qkv_bias(bias[0:1], bias[1:2])

    @pl.when(native == 0)
    def _():
        start, rows = (0, width) if n else (width + EXTRA, inner // 4)
        pairs = [(pieces[0].at[start + rows : start + rows + EXTRA], tail)]
        for k in range(4):
            pairs.append(
                (pieces[k].at[start : start + rows], matrix.at[multiple(chip ^ k, rows)])
            )
        if n == 0:
            pairs.append((pieces[4], matrix.at[inner:]))
        copy_all(pairs, sem)
        parts = tail[...].astype(F32)
        row = parts[0:1] + parts[1:2] + parts[2:3]
        bias_out[...] = qkv_bias(row[:, :width], row[:, width : 2 * width])


def seg_column(seg_row):
    n = seg_row.shape[1]
    parts = [
        jnp.broadcast_to(seg_row[:, i : i + 128], (128, 128)).T[:, 0:1] for i in range(0, n, 128)
    ]
    return jnp.concatenate(parts, axis=0)


def attend(qkv, seg_row, mixed, lse, tile):
    tokens = qkv.shape[0]
    width = qkv.shape[1] // 3
    heads = width // HEAD_DIM
    column = seg_column(seg_row)
    for start in range(0, tokens, tile):
        same = column[start : start + tile] == seg_row
        outs, logs = [], []
        for head in range(heads):
            at = head * HEAD_DIM
            query = qkv[start : start + tile, at : at + HEAD_DIM] * HEAD_DIM ** (-0.5)
            keys = qkv[:, width + at : width + at + HEAD_DIM]
            values = qkv[:, 2 * width + at : 2 * width + at + HEAD_DIM]
            scores = jnp.where(same, dot_nt(query, keys), NEG)
            top = jnp.max(scores, axis=1, keepdims=True)
            expon = jnp.exp(scores - top)
            total = jnp.sum(expon, axis=1, keepdims=True)
            outs.append(dot_nn(expon.astype(BF), values) / total)
            logs.append(top + jnp.log(total))
        mixed[start : start + tile] = jnp.concatenate(outs, axis=1).astype(BF)
        logs.append(jnp.zeros((tile, lse.shape[1] - heads), F32))
        lse[start : start + tile] = jnp.concatenate(logs, axis=1)


def qkv_bias(bias_q, bias_v):
    return jnp.concatenate([bias_q, jnp.zeros_like(bias_q), bias_v], axis=1)


def attention_home(place, hidden, weight, bias, seg, mixed, ordered, qkv, lse):
    first = place[2] // 2
    tokens = hidden.shape[0]
    half = tokens // 2
    ids = []
    for i, h in enumerate((first, 1 - first)):
        at = multiple(h, half)
        ordered[i * half : (i + 1) * half] = hidden[at]
        ids.append(seg[0:1, at])
    seg_row = jnp.concatenate(ids, axis=1).astype(F32)
    qkv[...] = (dot_nt(ordered[...], weight[...]) + qkv_bias(bias[0:1], bias[1:2])).astype(BF)
    attend(qkv, seg_row, mixed, lse, half)


def put_half(part, keep, send):
    half = part.shape[0] // 2
    keep[...] = part[:half]
    send[...] = part[half:].astype(BF)


def project_first(place, mixed, mixed_got, out_w, out_got, kept, keep, send):
    native = place[3] == 1
    rows = jnp.where(native, out_w[...], out_got[...])
    values = jnp.where(native, mixed[...], mixed_got[...])
    kept[...] = values
    put_half(dot_nn(values, rows), keep, send)


def seg_of(pack, tokens):
    return pack[-EXTRA:].astype(F32)[0:1, :tokens]


def attention_again(place, pack, matrix, bias, qkv, lse, mixed):
    tokens, inner = qkv.shape
    qkv[...] = (dot_nt(pack[:tokens], matrix[:inner]) + bias[...]).astype(BF)
    attend(qkv, seg_of(pack, tokens), mixed, lse, tokens // 2)


def attention_column(place, own, got, matrix, bias, pack, qkv, mixed, lse, keep, send):
    tokens, inner = qkv.shape
    hidden = jnp.concatenate([own[...], got[...]], axis=0)
    qkv[...] = (dot_nt(hidden, matrix[:inner]) + bias[...]).astype(BF)
    attend(qkv, seg_of(pack, tokens), mixed, lse, tokens // 2)
    put_half(dot_nn(mixed[...], matrix[inner:]), keep, send)


def attend_back(qkv, lse, grad_mixed, seg_row, grad_qkv, tile):
    tokens = qkv.shape[0]
    width = qkv.shape[1] // 3
    heads = width // HEAD_DIM
    column = seg_column(seg_row)
    scale = HEAD_DIM ** (-0.5)
    grads = [[], [], []]
    for head in range(heads):
        at = head * HEAD_DIM
        keys = qkv[:, width + at : width + at + HEAD_DIM]
        values = qkv[:, 2 * width + at : 2 * width + at + HEAD_DIM]
        grad_keys = jnp.zeros((tokens, HEAD_DIM), F32)
        grad_values = jnp.zeros((tokens, HEAD_DIM), F32)
        grad_query = []
        for start in range(0, tokens, tile):
            rows = slice(start, start + tile)
            query = qkv[rows, at : at + HEAD_DIM] * scale
            grad_out = grad_mixed[rows, at : at + HEAD_DIM]
            scores = jnp.where(column[rows] == seg_row, dot_nt(query, keys), NEG)
            probs = jnp.exp(scores - lse[rows, head : head + 1])
            grad_probs = dot_nt(grad_out, values)
            inner = jnp.sum(probs * grad_probs, axis=1, keepdims=True)
            grad_scores = (probs * (grad_probs - inner)).astype(BF)
            grad_query.append(dot_nn(grad_scores, keys) * scale)
            grad_keys += dot_tn(grad_scores, query)
            grad_values += dot_tn(probs.astype(BF), grad_out)
        grads[0].append(jnp.concatenate(grad_query, axis=0))
        grads[1].append(grad_keys)
        grads[2].append(grad_values)
    grad_qkv[...] = jnp.concatenate(grads[0] + grads[1] + grads[2], axis=1).astype(BF)


def join_grads(own, got):
    return jnp.concatenate([own[:-EXTRA], got[:-EXTRA]], axis=0)


def attention_back(place, own, got, matrix, qkv, lse, pack, grad_qkv, keep, send):
    tokens, inner = qkv.shape
    grad_att = join_grads(own, got)
    grad_mixed = dot_nt(grad_att, matrix[inner:]).astype(BF)
    attend_back(qkv, lse, grad_mixed, seg_of(pack, tokens), grad_qkv, tokens // 2)
    put_half(dot_nn(grad_qkv[...], matrix[:inner]), keep, send)


def part_rows(place, whole_a, whole_b, sums):
    features = whole_a[0].shape[1]
    for p in range(4):
        a = jnp.concatenate([whole_a[p], extra_rows(sums if p == 0 else [], features)], axis=0)
        b = jnp.concatenate([whole_b[p], extra_rows([], features)], axis=0)
        yield p, a.astype(BF), b.astype(BF)


def put_direct(place, whole_a, whole_b, sums, *refs):
    for p, a, b in part_rows(place, whole_a, whole_b, sums):
        part = jnp.concatenate([a, b], axis=0)
        for k, ref in enumerate(refs):

            @pl.when(place[0] ^ p == k)
            def _(ref=ref):
                ref[...] = part


def put_staged(place, whole_a, whole_b, sums, keep_a, send_a, keep_b, send_b):
    for p, a, b in part_rows(place, whole_a, whole_b, sums):
        offset = place[0] ^ p
        over_u, over_v = offset // 2, offset % 2

        @pl.when(over_v == 0)
        def _():
            keep_a[over_u] = a

        @pl.when(over_v == 1)
        def _():
            send_a[over_u] = a

        @pl.when(over_u == 0)
        def _():
            keep_b[over_v] = b

        @pl.when(over_u == 1)
        def _():
            send_b[over_v] = b


def head_grads(place, hidden, grad_qkv, mixed, a_own, a_got, sums, *parts):
    grad_att = join_grads(a_own, a_got)
    whole = jnp.concatenate([dot_tn(grad_qkv[...], hidden), dot_tn(mixed[...], grad_att)], axis=0)
    bias = jnp.sum(grad_qkv[...].astype(F32), axis=0, keepdims=True)
    rows = whole.shape[0] // 4
    cut = rows // 2
    first = [whole[p * rows : p * rows + cut] for p in range(4)]
    second = [whole[p * rows + cut : (p + 1) * rows] for p in range(4)]
    put_direct(place, first, second, [bias] + sums, *parts)


def head_grads_first(place, pack, grad_qkv, mixed, a_own, a_got, *refs):
    *parts, rows, sem = refs[8:]
    copy_all([(ref.at[ref.shape[0] - EXTRA :], rows.at[i]) for i, ref in enumerate(refs[:8])], sem)
    total = []
    for i in range(4):
        both = rows[2 * i].astype(F32) + rows[2 * i + 1].astype(F32)
        total += [both[j : j + 1] for j in range(3)]
    hidden = pack[: grad_qkv.shape[0]]
    head_grads(place, hidden, grad_qkv, mixed, a_own, a_got, total, *parts)


def head_grads_later(place, own, got, grad_qkv, mixed, a_own, a_got, *parts):
    hidden = jnp.concatenate([own[...], got[...]], axis=0)
    head_grads(place, hidden, grad_qkv, mixed, a_own, a_got, [], *parts)


def feed_forward(place, own, got, weights, bias, activ, slope, keep, send):
    hidden = jnp.concatenate([own[...], got[...]], axis=0)
    upper = dot_nn(hidden, weights[0]) + bias[...]
    cdf = 0.5 * (1.0 + lax.erf(upper * (0.5**0.5)))
    activ[...] = (upper * cdf).astype(BF)
    slope[...] = cdf + upper * jnp.exp(-0.5 * upper * upper) * 0.3989422804014327
    put_half(dot_nn(activ[...], weights[1]), keep, send)


def feed_back(place, own, got, weights, slope, grad_upper, keep, send):
    grad = join_grads(own, got)
    grad_upper[...] = (dot_nt(grad, weights[1]) * slope[...]).astype(BF)
    put_half(dot_nt(grad_upper[...], weights[0]), keep, send)


def unit_grads(place, x_own, x_got, g_own, g_got, activ, grad_upper, *parts):
    hidden = jnp.concatenate([x_own[...], x_got[...]], axis=0)
    grad = join_grads(g_own, g_got)
    up = dot_tn(hidden, grad_upper[...])
    down = dot_tn(activ[...], grad)
    bias = jnp.sum(grad_upper[...].astype(F32), axis=0, keepdims=True)
    rows = up.shape[0] // 4
    first = [up[p * rows : (p + 1) * rows] for p in range(4)]
    second = [down[p * rows : (p + 1) * rows] for p in range(4)]
    put_staged(place, first, second, [bias], *parts)


def chip_sum(place, keep, got, chip, low):
    chip[...] = keep[...] + got[...].astype(F32)
    low[...] = chip[...].astype(BF)


def combine_one(place, keep_a, got_a, keep_b, got_b, mine_a, for_a, mine_b, for_b):
    mine_a[...] = keep_a[0].astype(F32) + got_a[0].astype(F32)
    for_a[...] = (keep_a[1].astype(F32) + got_a[1].astype(F32)).astype(BF)
    mine_b[...] = keep_b[0].astype(F32) + got_b[0].astype(F32)
    for_b[...] = (keep_b[1].astype(F32) + got_b[1].astype(F32)).astype(BF)


def put_sum(place, a, b, at, mine, mixed, crossed):
    low_a, low_b = a.astype(BF), b.astype(BF)
    mine[at] = low_a
    mixed[at] = jnp.where(place[3] == 1, low_b, low_a)
    crossed[at] = low_b


def combine_staged(place, mine_a, got_a, mine_b, got_b, mine, mixed, crossed):
    a = mine_a[...] + got_a[...].astype(F32)
    b = mine_b[...] + got_b[...].astype(F32)
    put_sum(place, a, b, slice(0, a.shape[0]), mine, mixed, crossed)


def add_chips(refs):
    terms = [ref[...].astype(F32) for ref in refs]
    return (terms[0] + terms[1]) + (terms[2] + terms[3])


def combine_direct(place, own, got1, got2, got3, mine, mixed, crossed):
    total = add_chips((own, got1, got2, got3))
    half = total.shape[0] // 2
    put_sum(place, total[:half], total[half:], slice(0, half), mine, mixed, crossed)


def combine_both(place, mine_a, got_a, mine_b, got_b, own, got1, got2, got3, mine, mixed, crossed):
    a = mine_a[...] + got_a[...].astype(F32)
    b = mine_b[...] + got_b[...].astype(F32)
    rows = a.shape[0]
    put_sum(place, a, b, slice(0, rows), mine, mixed, crossed)
    total = add_chips((own, got1, got2, got3))
    half = total.shape[0] // 2
    put_sum(place, total[:half], total[half:], slice(rows, rows + half), mine, mixed, crossed)


def combine_planes(place, *refs):
    *groups, out = refs
    start = 0
    for i in range(0, len(groups), 3):
        mine, mixed, crossed = groups[i : i + 3]
        rows = mine.shape[0]
        first = jnp.where(place[3] == 1, mine[...], crossed[...])
        out[start : start + rows] = (first.astype(F32) + mixed[...].astype(F32)).astype(BF)
        start += rows


def tail_one(place, keep, got, back, mine, other):
    s = place[2] % 2
    rows = mine.shape[0]
    at, away = multiple(s, rows), multiple(1 - s, rows)
    mine[...] = keep[at] + got[at].astype(F32) + back[at]
    other[...] = (keep[away] + got[away].astype(F32)).astype(BF)


def tail_two(place, mine, got, final, rows, both):
    rows[...] = mine[...] + got[...].astype(F32)
    both[0] = final[...].astype(BF)
    both[1] = rows[...].astype(BF)


def normalize(values):
    center = values - jnp.mean(values, axis=1, keepdims=True)
    spread = jnp.mean(center * center, axis=1, keepdims=True)
    inv = lax.rsqrt(spread + EPS)
    return center * inv, inv


def norm_forward(place, base, chip, got, bias, gain, shift, total, out, low):
    values = base[...].astype(F32) + (chip[...].astype(BF).astype(F32) + got[...].astype(F32) + bias[...])
    total[...] = values
    unit, _ = normalize(values)
    result = unit * gain[...] + shift[...]
    out[...] = result
    low[...] = result.astype(BF)


def back_through(values, gain, grad):
    unit, inv = normalize(values)
    scaled = grad * gain
    first = jnp.mean(scaled, axis=1, keepdims=True)
    second = jnp.mean(scaled * unit, axis=1, keepdims=True)
    back = inv * (scaled - first - unit * second)
    low = back.astype(BF)
    sums = [
        jnp.sum(low.astype(F32), axis=0, keepdims=True),
        jnp.sum(grad * unit, axis=0, keepdims=True),
        jnp.sum(grad, axis=0, keepdims=True),
    ]
    return back, jnp.concatenate([low, extra_rows(sums, low.shape[1]).astype(BF)], axis=0)


def norm_turn(place, base, chip, got, bias, gain, shift, pack, final, back, low):
    half = base.shape[0]
    quarter = half // 2
    values = base[...] + (chip[...].astype(BF).astype(F32) + got[...].astype(F32) + bias[...])
    unit, _ = normalize(values)
    back[...] = unit * gain[...] + shift[...]
    final[...] = back[multiple(place[2] % 2, quarter)]
    grad = pack[2 * half : 3 * half].astype(F32)
    back[...], low[...] = back_through(values, gain[...], grad)


def norm_backward(place, values, base, chip, got, gain, back, low):
    grad = base[...] + (chip[...].astype(BF).astype(F32) + got[...].astype(F32))
    back[...], low[...] = back_through(values[...], gain[...], grad)


def join_pieces(place, p0, p1, p2, p3, mine, sem):
    copy_all([(ref, mine.at[k]) for k, ref in enumerate((p0, p1, p2, p3))], sem)


def unpack_layer(place, mine, got, *refs, earlier, unit_half):
    up, down, qkv, out, small_u, small_h, parts, sem = refs[earlier:]
    chip, native = place[0], place[3]
    p = pl.program_id(0)

    def copy(ref, i, k):
        return pltpu.make_async_copy(ref.at[k], parts.at[i, chip ^ k], sem.at[i, k])

    for flip, refs in enumerate(((got, mine), (mine, got))):

        @pl.when(native == flip)
        def _(refs=refs):
            @pl.when(p == 0)
            def _():
                for i in range(2):
                    for k in range(4):
                        copy(refs[i], i, k).start()

            for k in range(4):

                @pl.when(chip ^ k == p)
                def _(k=k):
                    for i in range(2):
                        copy(refs[i], i, k).wait()

    rows = up.shape[1]
    cut = out.shape[1] // 2
    up[0] = parts[0, p, 0:rows].astype(F32)
    down[0] = parts[1, p, 0:rows].astype(F32)
    heads = [parts[i, p, unit_half : unit_half + cut].astype(F32) for i in range(2)]

    @pl.when(p < 3)
    def _():
        for i in range(2):
            qkv[0, i * cut : (i + 1) * cut] = heads[i]

    @pl.when(p == 3)
    def _():
        for i in range(2):
            out[0, i * cut : (i + 1) * cut] = heads[i]

    @pl.when(p == 0)
    def _():
        small_u[...] = parts[0, 0, rows:unit_half].astype(F32)
        small_h[...] = parts[0, 0, unit_half + cut :].astype(F32)


def write_small(place, u1, h1, u2, h2, bup, bqv, bias, gain, shift):
    width = bqv.shape[2]
    for n, (u, h) in enumerate(((u1, h1), (u2, h2))):
        bup[n : n + 1] = u[0:1]
        bqv[n, 0:1] = h[0:1, 0:width]
        bqv[n, 1:2] = h[0:1, 2 * width : 3 * width]
        for i in range(2):
            for ref, at in ((bias, 0), (gain, 1), (shift, 2)):
                row = 1 + (2 * n + i) * 3 + at
                ref[n, i : i + 1] = h1[row : row + 1]


def on_device(
    hidden_in,
    out_grad,
    segment_ids,
    loss_mask,
    w_qkv,
    b_query_value,
    w_out,
    branch_bias,
    norm_gain,
    norm_shift,
    w_up,
    b_up,
    w_down,
):
    place = Place()
    at = place.vector
    layers, features = w_qkv.shape[:2]
    width = w_qkv.shape[-1]
    inner = 3 * width
    tokens = hidden_in.shape[0]
    half, quarter = tokens // 2, tokens // 4
    units = w_up.shape[-1]
    unit_rows, head_rows = features // 4, (inner + width) // 4
    w_qkv_t = jnp.transpose(w_qkv, (0, 2, 3, 1)).reshape(layers, inner, features)

    def gain_of(n, i):
        return branch_bias[n, i][None], norm_gain[n, i][None], norm_shift[n, i][None]

    half_f = ((half, features), F32)
    half_b = ((half, features), BF)
    half_e = ((half + EXTRA, features), BF)
    unit_piece = ((2 * unit_rows + EXTRA, features), BF)
    head_piece = ((head_rows + EXTRA, features), BF)
    row_quarter_f = ((quarter, features), F32)
    sem = pltpu.SemaphoreType.DMA((9,))
    tail = pltpu.VMEM((EXTRA, features), BF)

    def spread_chips(values):
        return [values] + [place.chip(values, k, native=False) for k in (1, 2, 3)]

    def unit_weights(n, pieces, after=()):
        return run(
            "choose_units",
            functools.partial(choose_units, n=n),
            [((2, units, features), BF), ((1, units), F32)],
            at, w_up, w_down, b_up, *pieces,
            scratch=[tail, sem],
            hbm=(1, 2, *range(4, 4 + len(pieces))),
            hbm_out=(0,),
            after=after,
        )

    def unit_pack(n, whole, after=()):
        rows = 2 * (units if whole else unit_rows) + EXTRA
        return run(
            "pack_units",
            functools.partial(pack_units, n=n, whole=whole),
            [((rows, features), BF)],
            at, w_up, w_down, b_up,
            scratch=[tail, sem],
            hbm=(1, 2),
            hbm_out=(0,),
            after=after,
        )[0]

    def head_weights(n, pieces, after=()):
        return run(
            "choose_heads",
            functools.partial(choose_heads, n=n),
            [((inner + width, features), BF), ((1, inner), F32)],
            at, w_qkv_t, w_out, Layer(b_query_value, n), *pieces,
            scratch=[tail, sem],
            hbm=(1, 2, *range(4, 4 + len(pieces))),
            hbm_out=(0,),
            after=after,
        )

    def quad_sum(keep, send, after=()):
        chip, low = run(
            "chip_sum", chip_sum, [half_f, half_b], at, keep, place.core(send), after=after
        )
        return chip, place.side(low)

    units1 = unit_pack(0, False)
    early = units1
    out_got = place.cross(w_out[0])
    units1 = place.cross(units1)
    row_pack = ((tokens + half + EXTRA, features), BF)
    pack_own, pack_other = run(
        "pack_rows",
        pack_rows,
        [row_pack, row_pack],
        at, hidden_in, out_grad, segment_ids, loss_mask,
        after=[early],
    )
    (mixed_home,) = run(
        "attention_home",
        attention_home,
        [((tokens, width), BF)],
        at, hidden_in, Layer(w_qkv_t, 0), Layer(b_query_value, 0), segment_ids,
        scratch=[
            pltpu.VMEM((tokens, features), BF),
            pltpu.VMEM((tokens, inner), BF),
            pltpu.VMEM((tokens, 128), F32),
        ],
        after=[pack_own],
    )
    mixed_got = place.cross(mixed_home)
    pack = jnp.where(place.native, pack_own, place.to_foreign(pack_other))

    mixed1, keep, send = run(
        "project_first",
        project_first,
        [((tokens, width), BF), half_f, half_b],
        at, mixed_home, mixed_got, Layer(w_out, 0), out_got,
        after=[units1],
    )
    chip, others = quad_sum(keep, send)
    head_pack_rows = width + inner // 4 + 2 * EXTRA
    (heads,) = run(
        "pack_heads",
        pack_heads,
        [((head_pack_rows, features), BF)],
        at, w_qkv_t, w_out, b_query_value,
        scratch=[pltpu.VMEM((2, EXTRA, features), BF), sem],
        hbm=(1, 2),
        hbm_out=(0,),
        after=[chip],
    )
    heads = place.cross(heads)
    sum11, norm11, low11 = run(
        "norm_forward",
        norm_forward,
        [half_f, half_f, half_b],
        at, pack[:half], chip, others, *gain_of(0, 0),
    )
    got11 = place.core(low11)
    weights1, b_up1 = unit_weights(0, spread_chips(units1), after=[low11])
    ffn_outs = [((tokens, units), BF), ((tokens, units), F32), half_f, half_b]
    activ1, slope1, keep, send = run(
        "feed_forward",
        feed_forward,
        ffn_outs,
        at, low11, got11, weights1, b_up1,
    )
    matrix_of = ((inner + width, features), BF)
    chip, others = quad_sum(keep, send, [heads])
    units2 = place.cross(unit_pack(1, False, [chip]))
    sum12, norm12, low12 = run(
        "norm_forward",
        norm_forward,
        [half_f, half_f, half_b],
        at, norm11, chip, others, *gain_of(0, 1),
    )
    got12 = place.core(low12)
    heads = spread_chips(heads)
    matrix2, bias2 = head_weights(1, heads, [low12])
    lse_of = ((tokens, 128), F32)
    qkv2, mixed2, lse2, keep, send = run(
        "attention_column",
        attention_column,
        [((tokens, inner), BF), ((tokens, width), BF), lse_of, half_f, half_b],
        at, low12, got12, matrix2, bias2, pack,
    )
    chip, others = quad_sum(keep, send, [units2])
    sum21, norm21, low21 = run(
        "norm_forward",
        norm_forward,
        [half_f, half_f, half_b],
        at, low12, chip, others, *gain_of(1, 0),
    )
    got21 = place.core(low21)
    weights2, b_up2 = unit_weights(1, spread_chips(units2), after=[low21])
    activ2, slope2, keep, send = run(
        "feed_forward", feed_forward, ffn_outs, at, low21, got21, weights2, b_up2
    )
    matrix1, bias1 = head_weights(0, [*heads, out_got], [low21])
    chip, others = quad_sum(keep, send)
    final, back, low = run(
        "norm_turn",
        norm_turn,
        [row_quarter_f, half_f, half_e],
        at, norm21, chip, others, *gain_of(1, 1), pack,
    )

    shapes = [
        (layers, features, units),
        (layers, units, features),
        (layers, inner, features),
        (layers, width, features),
    ]

    def unpack(n, given, earlier, after=()):
        extra = (EXTRA, features)
        *grads, small_u, small_h = pl.pallas_call(
            functools.partial(
                unpack_layer, earlier=len(earlier) + len(after), unit_half=unit_half
            ),
            name="unpack_layer",
            grid=(4,),
            out_shape=[jax.ShapeDtypeStruct(s, F32) for s in shapes + [extra, extra]],
            in_specs=[pl.BlockSpec(memory_space=pltpu.SMEM)]
            + [pl.BlockSpec(memory_space=pl.ANY)] * (2 + len(earlier) + len(after)),
            out_specs=[
                pl.BlockSpec((1, unit_rows, units), lambda p: (n, p, 0)),
                pl.BlockSpec((1, units // 4, features), lambda p: (n, p, 0)),
                pl.BlockSpec((1, head_rows, features), lambda p: (n, jnp.minimum(p, 2), 0)),
                pl.BlockSpec((1, head_rows, features), lambda p: (n, 0, 0)),
                pl.BlockSpec(extra, lambda p: (0, 0)),
                pl.BlockSpec(extra, lambda p: (0, 0)),
            ],
            input_output_aliases={3 + i: i for i in range(len(earlier))},
            scratch_shapes=[
                pltpu.VMEM((2, 4, unit_half + head_half, features), BF),
                pltpu.SemaphoreType.DMA((2, 4)),
            ],
            cost_estimate=pl.CostEstimate(flops=0, bytes_accessed=0, transcendentals=0),
            compiler_params=pltpu.CompilerParams(
                vmem_limit_bytes=VMEM_BYTES, dimension_semantics=("arbitrary",)
            ),
        )(at, *given, *earlier, *after)
        return grads, (small_u, small_h)

    unit_half, head_half = unit_rows + EXTRA, head_rows // 2 + EXTRA
    unit_parts = [((2, unit_half, features), BF)] * 4
    head_parts = [((2 * head_half, features), BF)] * 4

    def send_direct(parts):
        return [parts[0]] + [place.chip(parts[k], k) for k in (1, 2, 3)]

    def send_staged(keep_a, send_a, keep_b, send_b):
        return keep_a, place.chip(send_a, 1), keep_b, place.chip(send_b, 2)

    def next_stage(parts, after=()):
        of = (unit_half, features)
        mine_a, for_a, mine_b, for_b = run(
            "combine_one",
            combine_one,
            [(of, F32), (of, BF), (of, F32), (of, BF)],
            at, *parts,
            after=after,
        )
        return mine_a, place.chip(for_a, 2), mine_b, place.chip(for_b, 1)

    def sum_chips(kernel, parts, rows, after=()):
        half_rows = ((rows, features), BF)
        mine, mixed, crossed = run(
            kernel.__name__, kernel, [half_rows] * 3, at, *parts, after=after
        )
        return mine, place.mix(mixed), place.cross(crossed)

    def sum_planes(groups, after=()):
        rows = sum(group[0].shape[0] for group in groups)
        (piece,) = run(
            "combine_planes",
            combine_planes,
            [((rows, features), BF)],
            at, *[part for group in groups for part in group],
            after=after,
        )
        piece = place.add_far(piece)
        return [piece] + [place.chip(piece, k) for k in (1, 2, 3)]

    def with_partner(pieces, after=()):
        (mine,) = run(
            "join_pieces",
            join_pieces,
            [((4,) + pieces[0].shape, BF)],
            at, *pieces,
            scratch=[sem],
            hbm=(1, 2, 3, 4),
            hbm_out=(0,),
            after=after,
        )
        return mine, place.core(mine)

    grad_of = [((tokens, units), BF), half_f, half_b]
    back_of = [half_f, half_e]
    inner_of = [((tokens, inner), BF), half_f, half_b]

    got = place.core(low)
    grad_upper2, keep, send = run(
        "feed_back", feed_back, grad_of, at, low, got, weights2, slope2
    )
    chip, others = quad_sum(keep, send)
    units2 = run(
        "unit_grads",
        unit_grads,
        unit_parts,
        at, low21, got21, low, got, activ2, grad_upper2,
        after=[send],
    )
    early = units2[0]
    units2 = send_staged(*units2)
    sums = [low, got]
    back, low = run(
        "norm_backward",
        norm_backward,
        back_of,
        at, sum21, back, chip, others, norm_gain[1, 0][None],
        after=[early],
    )
    got = place.core(low)
    grad_qkv2, keep, send = run(
        "attention_back",
        attention_back,
        inner_of,
        at, low, got, matrix2, qkv2, lse2, pack,
        after=[units2[1], units2[3]],
    )
    qkv1, lse1, _ = run(
        "attention_again",
        attention_again,
        [((tokens, inner), BF), lse_of, ((tokens, width), BF)],
        at, pack, matrix1, bias1,
        after=[send],
    )
    chip, others = quad_sum(keep, send)
    heads2 = run(
        "head_grads",
        head_grads_later,
        head_parts,
        at, low12, got12, grad_qkv2, mixed2, low, got,
        after=[send],
    )
    units2 = next_stage(units2, after=[send])
    early = heads2[0]
    heads2 = send_direct(heads2)
    sums = [low, got] + sums
    back, low = run(
        "norm_backward",
        norm_backward,
        back_of,
        at, sum12, back, chip, others, norm_gain[0, 1][None],
        after=[early, lse1, units2[1], units2[3]],
    )
    got = place.core(low)
    grad_upper1, keep, send = run(
        "feed_back", feed_back, grad_of, at, low, got, weights1, slope1
    )
    chip, others = quad_sum(keep, send)
    units1 = run(
        "unit_grads",
        unit_grads,
        unit_parts,
        at, low11, got11, low, got, activ1, grad_upper1,
        after=[send],
    )
    early = units1[0]
    units1 = send_staged(*units1)
    sums = [low, got] + sums
    back, low = run(
        "norm_backward",
        norm_backward,
        back_of,
        at, sum11, back, chip, others, norm_gain[0, 0][None],
        after=[early, *heads2[1:]],
    )
    got = place.core(low)
    sums = [low, got] + sums
    grad_qkv1, keep, send = run(
        "attention_back",
        attention_back,
        inner_of,
        at, low, got, matrix1, qkv1, lse1, pack,
    )
    later = sum_chips(combine_both, (*units2, *heads2), unit_half + head_half, after=[send])
    units1 = next_stage(units1, after=[later[0]])
    heads1 = run(
        "head_grads",
        head_grads_first,
        head_parts,
        at, pack, grad_qkv1, mixed1, low, got, *sums,
        scratch=[pltpu.VMEM((8, EXTRA, features), BF), pltpu.SemaphoreType.DMA((8,))],
        hbm=range(6, 14),
        after=[units1[0]],
    )
    early = heads1[0]
    heads1 = send_direct(heads1)
    row_quarter = (quarter, features)
    mine, other = run(
        "tail_one",
        tail_one,
        [(row_quarter, F32), (row_quarter, BF)],
        at, keep, place.core(send), back,
        after=[early],
    )
    units1 = sum_chips(combine_staged, units1, unit_half, after=[mine, *later[1:]])
    rows, both = run(
        "tail_two",
        tail_two,
        [row_quarter_f, ((2, quarter, features), BF)],
        at, mine, place.side(other), final,
        after=[units1[0]],
    )
    both = place.cross(both)
    final_out, input_grad = (
        jnp.where(place.native, own, got.astype(F32)) for own, got in zip((final, rows), both)
    )
    later = sum_planes([later], after=[rows])
    early = later[0]
    heads1 = sum_chips(combine_direct, heads1, head_half, after=[early, *units1[1:]])
    first = sum_planes([units1, heads1], after=[early])
    later = with_partner(later, [first[0]])
    grads, small2 = unpack(1, later, [], [both])
    first = with_partner(first, grads[:1])

    (up, down, qkv, out), small1 = unpack(0, first, grads)
    pairs = (layers, 2, features)
    bup, bqv, bias, gain, shift = run(
        "write_small",
        write_small,
        [((layers, units), F32), ((layers, 2, width), F32)] + [(pairs, F32)] * 3,
        at, *small1, *small2,
    )
    return (
        final_out,
        input_grad,
        jnp.transpose(qkv.reshape(layers, 3, width, features), (0, 3, 1, 2)),
        bqv,
        out,
        bias,
        gain,
        shift,
        up,
        bup,
        down,
    )


def solution(mesh):
    columns = Mesh(mesh.devices.reshape(-1, 2, 2, 2, mesh.shape["tp"]), AXES)
    rows = P(AXES[:4], None)
    return jax.shard_map(
        on_device,
        mesh=columns,
        in_specs=(
            rows,
            rows,
            rows,
            rows,
            P(None, None, None, "tp"),
            P(None, None, "tp"),
            P(None, "tp", None),
            P(),
            P(),
            P(),
            P(None, None, "tp"),
            P(None, "tp"),
            P(None, "tp", None),
        ),
        out_specs=(
            P(AXES, None),
            P(AXES, None),
            P(None, None, None, "tp"),
            P(None, None, "tp"),
            P(None, "tp", None),
            P(),
            P(),
            P(),
            P(None, None, "tp"),
            P(None, "tp"),
            P(None, "tp", None),
        ),
        check_vma=False,
    )
```

```python
import functools

import jax
import jax.numpy as jnp
from jax import lax
from jax.experimental import pallas as pl
from jax.experimental.pallas import tpu as pltpu
from jax.sharding import Mesh
from jax.sharding import PartitionSpec as P

HEAD_DIM = 64
EPS = 1e-06
NEG = -1e30
EXTRA = 16
AXES = ("far", "u", "v", "c", "tp")
BF = jnp.bfloat16
F32 = jnp.float32
VMEM_BYTES = 24 << 20


class Place:
    def __init__(self):
        self.fars = lax.axis_size("far")
        self.core_no = lax.axis_index("c")
        self.z = lax.axis_index("tp")
        self.native = self.core_no == self.z // 2
        chip = lax.axis_index("u") * 2 + lax.axis_index("v")
        self.vector = jnp.stack(
            [chip, self.core_no, self.z, self.native.astype(jnp.int32)]
        ).astype(jnp.int32)

    def move(self, values, where):
        pairs = []
        for far in range(self.fars):
            for chip in range(4):
                for c in range(2):
                    for z in range(4):
                        to = where(chip, c, z)
                        if to is not None:
                            base = far * 4
                            source = ((base + chip) * 2 + c) * 4 + z
                            target = ((base + to[0]) * 2 + to[1]) * 4 + to[2]
                            pairs.append((source, target))
        return lax.ppermute(values, AXES, pairs)

    def core(self, values):
        return self.move(values, lambda i, c, z: (i, c ^ 1, z))

    def to_foreign(self, values):
        return self.move(values, lambda i, c, z: (i, c ^ 1, z) if c == z // 2 else None)

    def side(self, values):
        return self.move(values, lambda i, c, z: (i, c, z ^ 1))

    def cross(self, values):
        return self.move(values, lambda i, c, z: (i, c ^ 1, z ^ 2) if c != z // 2 else None)

    def mix(self, values):
        def where(i, c, z):
            return (i, c ^ 1, z) if c == z // 2 else (i, c, z ^ 2)

        return self.move(values, where)

    def chip(self, values, k, native=None):
        def where(i, c, z):
            if native is None or native == (c == z // 2):
                return (i ^ k, c, z)
            return None

        return self.move(values, where)

    def add_far(self, values):
        step = 1
        while step < self.fars:
            pairs = []
            for far in range(self.fars):
                pairs += [(far * 32 + i, (far ^ step) * 32 + i) for i in range(32)]
            got = lax.ppermute(values, AXES, pairs)
            values = (values.astype(F32) + got.astype(F32)).astype(values.dtype)
            step *= 2
        return values


class Layer:
    def __init__(self, whole, n):
        self.whole, self.n = whole, n


class Argument:
    def __init__(self, whole):
        self.whole = whole


def run(name, kernel, outs, *args, scratch=(), after=(), hbm=(), hbm_out=(), cost=0):
    n = len(args)

    def body(*refs):
        kernel(*refs[:n], *refs[n + len(after) :])

    anywhere = pl.BlockSpec(memory_space=pl.ANY)
    vmem = pl.BlockSpec(memory_space=pltpu.VMEM)
    in_specs, given = [pl.BlockSpec(memory_space=pltpu.SMEM)], [args[0]]
    for i in range(1, n):
        arg = args[i]
        if isinstance(arg, Layer):
            block = (None,) + arg.whole.shape[1:]
            zeros = (0,) * (arg.whole.ndim - 1)
            in_specs.append(pl.BlockSpec(block, lambda i, at=(arg.n,) + zeros: at))
            given.append(arg.whole)
        else:
            pinned = isinstance(arg, Argument)
            space = pltpu.HBM if pinned else pl.ANY if i in hbm else pltpu.VMEM
            in_specs.append(pl.BlockSpec(memory_space=space))
            given.append(arg.whole if pinned else arg)
    in_specs += [anywhere] * len(after)
    return pl.pallas_call(
        body,
        name=name,
        grid=(1,) if any(isinstance(arg, Layer) for arg in args) else (),
        out_shape=[jax.ShapeDtypeStruct(s, d) for s, d in outs],
        in_specs=in_specs,
        out_specs=[anywhere if i in hbm_out else vmem for i in range(len(outs))],
        scratch_shapes=list(scratch),
        cost_estimate=pl.CostEstimate(
            flops=cost * 10**9, bytes_accessed=0, transcendentals=0
        ),
        compiler_params=pltpu.CompilerParams(vmem_limit_bytes=VMEM_BYTES),
    )(*given, *after)


def dot_nn(a, b):
    return lax.dot_general(a, b, (((1,), (0,)), ((), ())), preferred_element_type=F32)


def dot_nt(a, b):
    return lax.dot_general(a, b, (((1,), (1,)), ((), ())), preferred_element_type=F32)


def dot_tn(a, b):
    return lax.dot_general(a, b, (((0,), (0,)), ((), ())), preferred_element_type=F32)


def thirds(value):
    hi = value.astype(BF).astype(F32)
    mid = (value - hi).astype(BF).astype(F32)
    return hi, mid, value - hi - mid


def extra_rows(rows, columns):
    padded = [
        jnp.concatenate([r, jnp.zeros((1, columns - r.shape[1]), F32)], axis=1)
        if r.shape[1] < columns
        else r
        for r in rows
    ]
    return jnp.concatenate(padded + [jnp.zeros((EXTRA - len(rows), columns), F32)], axis=0)


def multiple(index, size):
    return pl.ds(pl.multiple_of(index * size, size), size)


def bias_rows(place, bias, rows):
    rows[...] = extra_rows(thirds(bias[0:1]), rows.shape[1]).astype(BF)


def copy_all(pairs, sem):
    copies = [pltpu.make_async_copy(a, b, sem.at[i]) for i, (a, b) in enumerate(pairs)]
    for copy in copies:
        copy.start()
    for copy in copies:
        copy.wait()


def pack_units(place, up, down, bias, piece, tail, sem, n, whole):
    rows = up.shape[1] if whole else up.shape[1] // 4
    at = slice(0, rows) if whole else multiple(place[0], rows)
    tail[...] = extra_rows(thirds(bias[n : n + 1]), up.shape[2]).astype(BF)
    copy_all(
        [
            (up.at[n, at], piece.at[0:rows]),
            (down.at[n, at], piece.at[rows : 2 * rows]),
            (tail, piece.at[2 * rows :]),
        ],
        sem,
    )


def head_biases(bias):
    both = jnp.concatenate([bias[0:1], bias[1:2]], axis=1)
    return extra_rows(thirds(both), 4 * bias.shape[1]).astype(BF)


def pack_heads(place, qkv_w, out_w, bias, pack, tail, sem):
    chip = place[0]
    rows, fewer = out_w.shape[1], qkv_w.shape[1] // 4
    inner = qkv_w.shape[1] // rows
    for n in range(2):
        tail[n] = head_biases(bias[n])
    second = rows + EXTRA

    @pl.when(chip < inner)
    def _():
        copy_all([(qkv_w.at[1, multiple(chip, rows)], pack.at[0:rows])], sem)

    @pl.when(chip >= inner)
    def _():
        copy_all([(out_w.at[1], pack.at[0:rows])], sem)

    copy_all(
        [
            (qkv_w.at[0, multiple(chip, fewer)], pack.at[second : second + fewer]),
            (tail.at[1], pack.at[rows:second]),
            (tail.at[0], pack.at[second + fewer :]),
        ],
        sem,
    )


def pack_rows(place, hidden, grad, seg, mask, own, other):
    c = place[1]
    tokens, features = hidden.shape
    half = tokens // 2
    for ref, first in ((own, c), (other, 1 - c)):
        ids = []
        for i, h in enumerate((first, 1 - first)):
            at = multiple(h, half)
            ref[i * half : (i + 1) * half] = hidden[at]
            ids.append(seg[0:1, at])
        at = multiple(first, half)
        scale = seg_column(mask[0:1, at].astype(F32))
        ref[tokens : tokens + half] = (grad[at].astype(F32) * scale).astype(BF)
        ids = jnp.concatenate(ids, axis=1).astype(F32)
        ref[tokens + half :] = extra_rows([ids], features).astype(BF)


def choose_units(place, up, down, bias, *refs, n):
    *pieces, both, bias_out, tail, sem = refs
    chip, native = place[0], place[3]
    rows = up.shape[1] // len(pieces)

    @pl.when(native == 1)
    def _():
        copy_all([(up.at[n], both.at[0]), (down.at[n], both.at[1])], sem)
        bias_out[...] = bias[n : n + 1]

    @pl.when(native == 0)
    def _():
        pairs = [(pieces[0].at[2 * rows :], tail)]
        for k, ref in enumerate(pieces):
            to = slice(0, rows) if len(pieces) == 1 else multiple(chip ^ k, rows)
            for m in range(2):
                pairs.append((ref.at[m * rows : (m + 1) * rows], both.at[m, to]))
        copy_all(pairs, sem)
        parts = tail[...].astype(F32)
        bias_out[...] = parts[0:1] + parts[1:2] + parts[2:3]


def choose_heads(place, qkv_w, out_w, bias, *refs, n):
    *pieces, matrix, bias_out, tail, sem = refs
    chip, native = place[0], place[3]
    width, inner = out_w.shape[1], qkv_w.shape[1]

    @pl.when(native == 1)
    def _():
        copy_all([(qkv_w.at[n], matrix.at[0:inner]), (out_w.at[n], matrix.at[inner:])], sem)
        bias_out[...] = qkv_bias(bias[0:1], bias[1:2])

    @pl.when(native == 0)
    def _():
        start, rows = (0, width) if n else (width + EXTRA, inner // 4)
        pairs = [(pieces[0].at[start + rows : start + rows + EXTRA], tail)]
        for k in range(4):
            pairs.append(
                (pieces[k].at[start : start + rows], matrix.at[multiple(chip ^ k, rows)])
            )
        if n == 0:
            pairs.append((pieces[4], matrix.at[inner:]))
        copy_all(pairs, sem)
        parts = tail[...].astype(F32)
        row = parts[0:1] + parts[1:2] + parts[2:3]
        bias_out[...] = qkv_bias(row[:, :width], row[:, width : 2 * width])


def seg_column(seg_row):
    n = seg_row.shape[1]
    parts = [
        jnp.broadcast_to(seg_row[:, i : i + 128], (128, 128)).T[:, 0:1] for i in range(0, n, 128)
    ]
    return jnp.concatenate(parts, axis=0)


def attend(qkv, seg_row, mixed, lse, tile):
    tokens = qkv.shape[0]
    width = qkv.shape[1] // 3
    heads = width // HEAD_DIM
    column = seg_column(seg_row)
    for start in range(0, tokens, tile):
        same = column[start : start + tile] == seg_row
        outs, logs = [], []
        for head in range(heads):
            at = head * HEAD_DIM
            query = qkv[start : start + tile, at : at + HEAD_DIM] * HEAD_DIM ** (-0.5)
            keys = qkv[:, width + at : width + at + HEAD_DIM]
            values = qkv[:, 2 * width + at : 2 * width + at + HEAD_DIM]
            scores = jnp.where(same, dot_nt(query, keys), NEG)
            top = jnp.max(scores, axis=1, keepdims=True)
            expon = jnp.exp(scores - top)
            total = jnp.sum(expon, axis=1, keepdims=True)
            outs.append(dot_nn(expon.astype(BF), values) / total)
            logs.append(top + jnp.log(total))
        mixed[start : start + tile] = jnp.concatenate(outs, axis=1).astype(BF)
        logs.append(jnp.zeros((tile, lse.shape[1] - heads), F32))
        lse[start : start + tile] = jnp.concatenate(logs, axis=1)


def qkv_bias(bias_q, bias_v):
    return jnp.concatenate([bias_q, jnp.zeros_like(bias_q), bias_v], axis=1)


def attention_home(place, hidden, weight, bias, seg, mixed, ordered, qkv, lse):
    first = place[2] // 2
    tokens = hidden.shape[0]
    half = tokens // 2
    ids = []
    for i, h in enumerate((first, 1 - first)):
        at = multiple(h, half)
        ordered[i * half : (i + 1) * half] = hidden[at]
        ids.append(seg[0:1, at])
    seg_row = jnp.concatenate(ids, axis=1).astype(F32)
    qkv[...] = (dot_nt(ordered[...], weight[...]) + qkv_bias(bias[0:1], bias[1:2])).astype(BF)
    attend(qkv, seg_row, mixed, lse, half)


def put_half(part, keep, send):
    half = part.shape[0] // 2
    keep[...] = part[:half]
    send[...] = part[half:].astype(BF)


def project_first(place, mixed, mixed_got, out_w, out_got, kept, keep, send):
    native = place[3] == 1
    rows = jnp.where(native, out_w[...], out_got[...])
    values = jnp.where(native, mixed[...], mixed_got[...])
    kept[...] = values
    put_half(dot_nn(values, rows), keep, send)


def seg_of(pack, tokens):
    return pack[-EXTRA:].astype(F32)[0:1, :tokens]


def attention_again(place, pack, matrix, bias, qkv, lse, mixed):
    tokens, inner = qkv.shape
    qkv[...] = (dot_nt(pack[:tokens], matrix[:inner]) + bias[...]).astype(BF)
    attend(qkv, seg_of(pack, tokens), mixed, lse, tokens // 2)


def attention_column(place, own, got, matrix, bias, pack, qkv, mixed, lse, keep, send):
    tokens, inner = qkv.shape
    hidden = jnp.concatenate([own[...], got[...]], axis=0)
    qkv[...] = (dot_nt(hidden, matrix[:inner]) + bias[...]).astype(BF)
    attend(qkv, seg_of(pack, tokens), mixed, lse, tokens // 2)
    put_half(dot_nn(mixed[...], matrix[inner:]), keep, send)


def attend_back(qkv, lse, grad_mixed, seg_row, grad_qkv, tile):
    tokens = qkv.shape[0]
    width = qkv.shape[1] // 3
    heads = width // HEAD_DIM
    column = seg_column(seg_row)
    scale = HEAD_DIM ** (-0.5)
    grads = [[], [], []]
    for head in range(heads):
        at = head * HEAD_DIM
        keys = qkv[:, width + at : width + at + HEAD_DIM]
        values = qkv[:, 2 * width + at : 2 * width + at + HEAD_DIM]
        grad_keys = jnp.zeros((tokens, HEAD_DIM), F32)
        grad_values = jnp.zeros((tokens, HEAD_DIM), F32)
        grad_query = []
        for start in range(0, tokens, tile):
            rows = slice(start, start + tile)
            query = qkv[rows, at : at + HEAD_DIM] * scale
            grad_out = grad_mixed[rows, at : at + HEAD_DIM]
            scores = jnp.where(column[rows] == seg_row, dot_nt(query, keys), NEG)
            probs = jnp.exp(scores - lse[rows, head : head + 1])
            grad_probs = dot_nt(grad_out, values)
            inner = jnp.sum(probs * grad_probs, axis=1, keepdims=True)
            grad_scores = (probs * (grad_probs - inner)).astype(BF)
            grad_query.append(dot_nn(grad_scores, keys) * scale)
            grad_keys += dot_tn(grad_scores, query)
            grad_values += dot_tn(probs.astype(BF), grad_out)
        grads[0].append(jnp.concatenate(grad_query, axis=0))
        grads[1].append(grad_keys)
        grads[2].append(grad_values)
    grad_qkv[...] = jnp.concatenate(grads[0] + grads[1] + grads[2], axis=1).astype(BF)


def join_grads(own, got):
    return jnp.concatenate([own[:-EXTRA], got[:-EXTRA]], axis=0)


def attention_back(place, own, got, matrix, qkv, lse, pack, grad_qkv, keep, send):
    tokens, inner = qkv.shape
    grad_att = join_grads(own, got)
    grad_mixed = dot_nt(grad_att, matrix[inner:]).astype(BF)
    attend_back(qkv, lse, grad_mixed, seg_of(pack, tokens), grad_qkv, tokens // 2)
    put_half(dot_nn(grad_qkv[...], matrix[:inner]), keep, send)


def part_rows(place, whole_a, whole_b, sums):
    features = whole_a[0].shape[1]
    for p in range(4):
        a = jnp.concatenate([whole_a[p], extra_rows(sums if p == 0 else [], features)], axis=0)
        b = jnp.concatenate([whole_b[p], extra_rows([], features)], axis=0)
        yield p, a.astype(BF), b.astype(BF)


def put_direct(place, whole_a, whole_b, sums, *refs):
    for p, a, b in part_rows(place, whole_a, whole_b, sums):
        part = jnp.concatenate([a, b], axis=0)
        for k, ref in enumerate(refs):

            @pl.when(place[0] ^ p == k)
            def _(ref=ref):
                ref[...] = part


def put_staged(place, whole_a, whole_b, sums, keep_a, send_a, keep_b, send_b):
    for p, a, b in part_rows(place, whole_a, whole_b, sums):
        offset = place[0] ^ p
        over_u, over_v = offset // 2, offset % 2

        @pl.when(over_v == 0)
        def _():
            keep_a[over_u] = a

        @pl.when(over_v == 1)
        def _():
            send_a[over_u] = a

        @pl.when(over_u == 0)
        def _():
            keep_b[over_v] = b

        @pl.when(over_u == 1)
        def _():
            send_b[over_v] = b


def head_grads(place, hidden, grad_qkv, mixed, a_own, a_got, sums, *parts):
    grad_att = join_grads(a_own, a_got)
    whole = jnp.concatenate([dot_tn(grad_qkv[...], hidden), dot_tn(mixed[...], grad_att)], axis=0)
    bias = jnp.sum(grad_qkv[...].astype(F32), axis=0, keepdims=True)
    rows = whole.shape[0] // 4
    cut = rows // 2
    first = [whole[p * rows : p * rows + cut] for p in range(4)]
    second = [whole[p * rows + cut : (p + 1) * rows] for p in range(4)]
    put_direct(place, first, second, [bias] + sums, *parts)


def head_grads_first(place, pack, grad_qkv, mixed, a_own, a_got, *refs):
    *parts, rows, sem = refs[8:]
    copy_all([(ref.at[ref.shape[0] - EXTRA :], rows.at[i]) for i, ref in enumerate(refs[:8])], sem)
    total = []
    for i in range(4):
        both = rows[2 * i].astype(F32) + rows[2 * i + 1].astype(F32)
        total += [both[j : j + 1] for j in range(3)]
    hidden = pack[: grad_qkv.shape[0]]
    head_grads(place, hidden, grad_qkv, mixed, a_own, a_got, total, *parts)


def head_grads_later(place, own, got, grad_qkv, mixed, a_own, a_got, *parts):
    hidden = jnp.concatenate([own[...], got[...]], axis=0)
    head_grads(place, hidden, grad_qkv, mixed, a_own, a_got, [], *parts)


def feed_forward(place, own, got, weights, bias, activ, slope, keep, send):
    hidden = jnp.concatenate([own[...], got[...]], axis=0)
    upper = dot_nn(hidden, weights[0]) + bias[...]
    cdf = 0.5 * (1.0 + lax.erf(upper * (0.5**0.5)))
    activ[...] = (upper * cdf).astype(BF)
    slope[...] = cdf + upper * jnp.exp(-0.5 * upper * upper) * 0.3989422804014327
    put_half(dot_nn(activ[...], weights[1]), keep, send)


def feed_back(place, own, got, weights, slope, grad_upper, keep, send):
    grad = join_grads(own, got)
    grad_upper[...] = (dot_nt(grad, weights[1]) * slope[...]).astype(BF)
    put_half(dot_nt(grad_upper[...], weights[0]), keep, send)


def unit_grads(place, x_own, x_got, g_own, g_got, activ, grad_upper, *parts):
    hidden = jnp.concatenate([x_own[...], x_got[...]], axis=0)
    grad = join_grads(g_own, g_got)
    up = dot_tn(hidden, grad_upper[...])
    down = dot_tn(activ[...], grad)
    bias = jnp.sum(grad_upper[...].astype(F32), axis=0, keepdims=True)
    rows = up.shape[0] // 4
    first = [up[p * rows : (p + 1) * rows] for p in range(4)]
    second = [down[p * rows : (p + 1) * rows] for p in range(4)]
    put_staged(place, first, second, [bias], *parts)


def chip_sum(place, keep, got, chip, low):
    chip[...] = keep[...] + got[...].astype(F32)
    low[...] = chip[...].astype(BF)


def combine_one(place, keep_a, got_a, keep_b, got_b, mine_a, for_a, mine_b, for_b):
    mine_a[...] = keep_a[0].astype(F32) + got_a[0].astype(F32)
    for_a[...] = (keep_a[1].astype(F32) + got_a[1].astype(F32)).astype(BF)
    mine_b[...] = keep_b[0].astype(F32) + got_b[0].astype(F32)
    for_b[...] = (keep_b[1].astype(F32) + got_b[1].astype(F32)).astype(BF)


def put_sum(place, a, b, at, mine, mixed, crossed):
    low_a, low_b = a.astype(BF), b.astype(BF)
    mine[at] = low_a
    mixed[at] = jnp.where(place[3] == 1, low_b, low_a)
    crossed[at] = low_b


def combine_staged(place, mine_a, got_a, mine_b, got_b, mine, mixed, crossed):
    a = mine_a[...] + got_a[...].astype(F32)
    b = mine_b[...] + got_b[...].astype(F32)
    put_sum(place, a, b, slice(0, a.shape[0]), mine, mixed, crossed)


def add_chips(refs):
    terms = [ref[...].astype(F32) for ref in refs]
    return (terms[0] + terms[1]) + (terms[2] + terms[3])


def combine_direct(place, own, got1, got2, got3, mine, mixed, crossed):
    total = add_chips((own, got1, got2, got3))
    half = total.shape[0] // 2
    put_sum(place, total[:half], total[half:], slice(0, half), mine, mixed, crossed)


def combine_both(place, mine_a, got_a, mine_b, got_b, own, got1, got2, got3, mine, mixed, crossed):
    a = mine_a[...] + got_a[...].astype(F32)
    b = mine_b[...] + got_b[...].astype(F32)
    rows = a.shape[0]
    put_sum(place, a, b, slice(0, rows), mine, mixed, crossed)
    total = add_chips((own, got1, got2, got3))
    half = total.shape[0] // 2
    put_sum(place, total[:half], total[half:], slice(rows, rows + half), mine, mixed, crossed)


def combine_planes(place, *refs):
    *groups, out = refs
    start = 0
    for i in range(0, len(groups), 3):
        mine, mixed, crossed = groups[i : i + 3]
        rows = mine.shape[0]
        first = jnp.where(place[3] == 1, mine[...], crossed[...])
        out[start : start + rows] = (first.astype(F32) + mixed[...].astype(F32)).astype(BF)
        start += rows


def tail_one(place, keep, got, back, mine, other):
    s = place[2] % 2
    rows = mine.shape[0]
    at, away = multiple(s, rows), multiple(1 - s, rows)
    mine[...] = keep[at] + got[at].astype(F32) + back[at]
    other[...] = (keep[away] + got[away].astype(F32)).astype(BF)


def tail_two(place, mine, got, final, rows, both):
    rows[...] = mine[...] + got[...].astype(F32)
    both[0] = final[...].astype(BF)
    both[1] = rows[...].astype(BF)


def normalize(values):
    center = values - jnp.mean(values, axis=1, keepdims=True)
    spread = jnp.mean(center * center, axis=1, keepdims=True)
    inv = lax.rsqrt(spread + EPS)
    return center * inv, inv


def norm_forward(place, base, chip, got, bias, gain, shift, total, out, low):
    values = base[...].astype(F32) + (chip[...].astype(BF).astype(F32) + got[...].astype(F32) + bias[...])
    total[...] = values
    unit, _ = normalize(values)
    result = unit * gain[...] + shift[...]
    out[...] = result
    low[...] = result.astype(BF)


def back_through(values, gain, grad):
    unit, inv = normalize(values)
    scaled = grad * gain
    first = jnp.mean(scaled, axis=1, keepdims=True)
    second = jnp.mean(scaled * unit, axis=1, keepdims=True)
    back = inv * (scaled - first - unit * second)
    low = back.astype(BF)
    sums = [
        jnp.sum(low.astype(F32), axis=0, keepdims=True),
        jnp.sum(grad * unit, axis=0, keepdims=True),
        jnp.sum(grad, axis=0, keepdims=True),
    ]
    return back, jnp.concatenate([low, extra_rows(sums, low.shape[1]).astype(BF)], axis=0)


def norm_turn(place, base, chip, got, bias, gain, shift, pack, final, back, low):
    half = base.shape[0]
    quarter = half // 2
    values = base[...] + (chip[...].astype(BF).astype(F32) + got[...].astype(F32) + bias[...])
    unit, _ = normalize(values)
    back[...] = unit * gain[...] + shift[...]
    final[...] = back[multiple(place[2] % 2, quarter)]
    grad = pack[2 * half : 3 * half].astype(F32)
    back[...], low[...] = back_through(values, gain[...], grad)


def norm_backward(place, values, base, chip, got, gain, back, low):
    grad = base[...] + (chip[...].astype(BF).astype(F32) + got[...].astype(F32))
    back[...], low[...] = back_through(values[...], gain[...], grad)


def join_pieces(place, p0, p1, p2, p3, mine, sem):
    copy_all([(ref, mine.at[k]) for k, ref in enumerate((p0, p1, p2, p3))], sem)


def unpack_layer(place, mine, got, *refs, earlier, unit_half):
    up, down, qkv, out, small_u, small_h, parts, sem = refs[earlier:]
    chip, native = place[0], place[3]
    p = pl.program_id(0)

    def copy(ref, i, k):
        return pltpu.make_async_copy(ref.at[k], parts.at[i, chip ^ k], sem.at[i, k])

    for flip, refs in enumerate(((got, mine), (mine, got))):

        @pl.when(native == flip)
        def _(refs=refs):
            @pl.when(p == 0)
            def _():
                for i in range(2):
                    for k in range(4):
                        copy(refs[i], i, k).start()

            for k in range(4):

                @pl.when(chip ^ k == p)
                def _(k=k):
                    for i in range(2):
                        copy(refs[i], i, k).wait()

    rows = up.shape[1]
    cut = out.shape[1] // 2
    up[0] = parts[0, p, 0:rows].astype(F32)
    down[0] = parts[1, p, 0:rows].astype(F32)
    heads = [parts[i, p, unit_half : unit_half + cut].astype(F32) for i in range(2)]

    @pl.when(p < 3)
    def _():
        for i in range(2):
            qkv[0, i * cut : (i + 1) * cut] = heads[i]

    @pl.when(p == 3)
    def _():
        for i in range(2):
            out[0, i * cut : (i + 1) * cut] = heads[i]

    @pl.when(p == 0)
    def _():
        small_u[...] = parts[0, 0, rows:unit_half].astype(F32)
        small_h[...] = parts[0, 0, unit_half + cut :].astype(F32)


def write_small(place, u1, h1, u2, h2, bup, bqv, bias, gain, shift):
    width = bqv.shape[2]
    for n, (u, h) in enumerate(((u1, h1), (u2, h2))):
        bup[n : n + 1] = u[0:1]
        bqv[n, 0:1] = h[0:1, 0:width]
        bqv[n, 1:2] = h[0:1, 2 * width : 3 * width]
        for i in range(2):
            for ref, at in ((bias, 0), (gain, 1), (shift, 2)):
                row = 1 + (2 * n + i) * 3 + at
                ref[n, i : i + 1] = h1[row : row + 1]


def on_device(
    hidden_in,
    out_grad,
    segment_ids,
    loss_mask,
    w_qkv,
    b_query_value,
    w_out,
    branch_bias,
    norm_gain,
    norm_shift,
    w_up,
    b_up,
    w_down,
):
    place = Place()
    at = place.vector
    layers, features = w_qkv.shape[:2]
    width = w_qkv.shape[-1]
    inner = 3 * width
    tokens = hidden_in.shape[0]
    half, quarter = tokens // 2, tokens // 4
    units = w_up.shape[-1]
    unit_rows, head_rows = features // 4, (inner + width) // 4
    w_qkv_t = jnp.transpose(w_qkv, (0, 2, 3, 1)).reshape(layers, inner, features)

    def gain_of(n, i):
        return branch_bias[n, i][None], norm_gain[n, i][None], norm_shift[n, i][None]

    half_f = ((half, features), F32)
    half_b = ((half, features), BF)
    half_e = ((half + EXTRA, features), BF)
    unit_piece = ((2 * unit_rows + EXTRA, features), BF)
    head_piece = ((head_rows + EXTRA, features), BF)
    row_quarter_f = ((quarter, features), F32)
    sem = pltpu.SemaphoreType.DMA((9,))
    tail = pltpu.VMEM((EXTRA, features), BF)

    def spread_chips(values):
        return [values] + [place.chip(values, k, native=False) for k in (1, 2, 3)]

    def unit_weights(n, pieces, after=()):
        return run(
            "choose_units",
            functools.partial(choose_units, n=n),
            [((2, units, features), BF), ((1, units), F32)],
            at, Argument(w_up), Argument(w_down), b_up, *pieces,
            scratch=[tail, sem],
            hbm=(1, 2, *range(4, 4 + len(pieces))),
            hbm_out=(0,),
            after=after,
        )

    def unit_pack(n, whole, after=()):
        rows = 2 * (units if whole else unit_rows) + EXTRA
        return run(
            "pack_units",
            functools.partial(pack_units, n=n, whole=whole),
            [((rows, features), BF)],
            at, Argument(w_up), Argument(w_down), b_up,
            scratch=[tail, sem],
            hbm=(1, 2),
            hbm_out=(0,),
            after=after,
        )[0]

    def head_weights(n, pieces, after=()):
        return run(
            "choose_heads",
            functools.partial(choose_heads, n=n),
            [((inner + width, features), BF), ((1, inner), F32)],
            at, Argument(w_qkv_t), Argument(w_out), Layer(b_query_value, n), *pieces,
            scratch=[tail, sem],
            hbm=(1, 2, *range(4, 4 + len(pieces))),
            hbm_out=(0,),
            after=after,
        )

    def quad_sum(keep, send, after=()):
        chip, low = run(
            "chip_sum", chip_sum, [half_f, half_b], at, keep, place.core(send), after=after
        )
        return chip, place.side(low)

    (tail1,) = run("bias_rows", bias_rows, [((EXTRA, features), BF)], at, b_up)
    start = at[0] * unit_rows
    units1 = jnp.concatenate(
        [lax.dynamic_slice(w, (0, start, 0), (1, unit_rows, features))[0] for w in (w_up, w_down)]
        + [tail1]
    )
    early = units1
    out_got = place.cross(w_out[0])
    units1 = place.cross(units1)
    row_pack = ((tokens + half + EXTRA, features), BF)
    pack_own, pack_other = run(
        "pack_rows",
        pack_rows,
        [row_pack, row_pack],
        at, hidden_in, out_grad, segment_ids, loss_mask,
        after=[early],
    )
    (mixed_home,) = run(
        "attention_home",
        attention_home,
        [((tokens, width), BF)],
        at, hidden_in, Layer(w_qkv_t, 0), Layer(b_query_value, 0), segment_ids,
        scratch=[
            pltpu.VMEM((tokens, features), BF),
            pltpu.VMEM((tokens, inner), BF),
            pltpu.VMEM((tokens, 128), F32),
        ],
        after=[pack_own],
        cost=10,
    )
    mixed_got = place.cross(mixed_home)
    pack = jnp.where(place.native, pack_own, place.to_foreign(pack_other))

    mixed1, keep, send = run(
        "project_first",
        project_first,
        [((tokens, width), BF), half_f, half_b],
        at, mixed_home, mixed_got, Layer(w_out, 0), out_got,
    )
    chip, others = quad_sum(keep, send, [units1])
    head_pack_rows = width + inner // 4 + 2 * EXTRA
    (heads,) = run(
        "pack_heads",
        pack_heads,
        [((head_pack_rows, features), BF)],
        at, Argument(w_qkv_t), Argument(w_out), b_query_value,
        scratch=[pltpu.VMEM((2, EXTRA, features), BF), sem],
        hbm=(1, 2),
        hbm_out=(0,),
        after=[chip],
    )
    heads = place.cross(heads)
    sum11, norm11, low11 = run(
        "norm_forward",
        norm_forward,
        [half_f, half_f, half_b],
        at, pack[:half], chip, others, *gain_of(0, 0),
    )
    got11 = place.core(low11)
    weights1, b_up1 = unit_weights(0, spread_chips(units1), after=[low11])
    ffn_outs = [((tokens, units), BF), ((tokens, units), F32), half_f, half_b]
    activ1, slope1, keep, send = run(
        "feed_forward",
        feed_forward,
        ffn_outs,
        at, low11, got11, weights1, b_up1,
        after=[heads],
    )
    matrix_of = ((inner + width, features), BF)
    chip, others = quad_sum(keep, send)
    units2 = place.cross(unit_pack(1, False, [chip]))
    sum12, norm12, low12 = run(
        "norm_forward",
        norm_forward,
        [half_f, half_f, half_b],
        at, norm11, chip, others, *gain_of(0, 1),
    )
    got12 = place.core(low12)
    heads = spread_chips(heads)
    matrix2, bias2 = head_weights(1, heads, [low12])
    lse_of = ((tokens, 128), F32)
    qkv2, mixed2, lse2, keep, send = run(
        "attention_column",
        attention_column,
        [((tokens, inner), BF), ((tokens, width), BF), lse_of, half_f, half_b],
        at, low12, got12, matrix2, bias2, pack,
        after=[units2],
    )
    chip, others = quad_sum(keep, send)
    sum21, norm21, low21 = run(
        "norm_forward",
        norm_forward,
        [half_f, half_f, half_b],
        at, low12, chip, others, *gain_of(1, 0),
    )
    got21 = place.core(low21)
    weights2, b_up2 = unit_weights(1, spread_chips(units2), after=[low21])
    activ2, slope2, keep, send = run(
        "feed_forward", feed_forward, ffn_outs, at, low21, got21, weights2, b_up2
    )
    chip, others = quad_sum(keep, send)
    final, back, low = run(
        "norm_turn",
        norm_turn,
        [row_quarter_f, half_f, half_e],
        at, norm21, chip, others, *gain_of(1, 1), pack,
    )

    shapes = [
        (layers, features, units),
        (layers, units, features),
        (layers, inner, features),
        (layers, width, features),
    ]

    def unpack(n, given, earlier, after=()):
        extra = (EXTRA, features)
        *grads, small_u, small_h = pl.pallas_call(
            functools.partial(
                unpack_layer, earlier=len(earlier) + len(after), unit_half=unit_half
            ),
            name="unpack_layer",
            grid=(4,),
            out_shape=[jax.ShapeDtypeStruct(s, F32) for s in shapes + [extra, extra]],
            in_specs=[pl.BlockSpec(memory_space=pltpu.SMEM)]
            + [pl.BlockSpec(memory_space=pl.ANY)] * (2 + len(earlier) + len(after)),
            out_specs=[
                pl.BlockSpec((1, unit_rows, units), lambda p: (n, p, 0)),
                pl.BlockSpec((1, units // 4, features), lambda p: (n, p, 0)),
                pl.BlockSpec((1, head_rows, features), lambda p: (n, jnp.minimum(p, 2), 0)),
                pl.BlockSpec((1, head_rows, features), lambda p: (n, 0, 0)),
                pl.BlockSpec(extra, lambda p: (0, 0)),
                pl.BlockSpec(extra, lambda p: (0, 0)),
            ],
            input_output_aliases={3 + i: i for i in range(len(earlier))},
            scratch_shapes=[
                pltpu.VMEM((2, 4, unit_half + head_half, features), BF),
                pltpu.SemaphoreType.DMA((2, 4)),
            ],
            cost_estimate=pl.CostEstimate(flops=0, bytes_accessed=0, transcendentals=0),
            compiler_params=pltpu.CompilerParams(
                vmem_limit_bytes=VMEM_BYTES, dimension_semantics=("arbitrary",)
            ),
        )(at, *given, *earlier, *after)
        return grads, (small_u, small_h)

    unit_half, head_half = unit_rows + EXTRA, head_rows // 2 + EXTRA
    unit_parts = [((2, unit_half, features), BF)] * 4
    head_parts = [((2 * head_half, features), BF)] * 4

    def send_direct(parts):
        return [parts[0]] + [place.chip(parts[k], k) for k in (1, 2, 3)]

    def send_staged(keep_a, send_a, keep_b, send_b):
        return keep_a, place.chip(send_a, 1), keep_b, place.chip(send_b, 2)

    def next_stage(parts, after=()):
        of = (unit_half, features)
        mine_a, for_a, mine_b, for_b = run(
            "combine_one",
            combine_one,
            [(of, F32), (of, BF), (of, F32), (of, BF)],
            at, *parts,
            after=after,
        )
        return mine_a, place.chip(for_a, 2), mine_b, place.chip(for_b, 1)

    def sum_chips(kernel, parts, rows, after=()):
        half_rows = ((rows, features), BF)
        mine, mixed, crossed = run(
            kernel.__name__, kernel, [half_rows] * 3, at, *parts, after=after
        )
        return mine, place.mix(mixed), place.cross(crossed)

    def sum_planes(groups, after=()):
        rows = sum(group[0].shape[0] for group in groups)
        (piece,) = run(
            "combine_planes",
            combine_planes,
            [((rows, features), BF)],
            at, *[part for group in groups for part in group],
            after=after,
        )
        piece = place.add_far(piece)
        return [piece] + [place.chip(piece, k) for k in (1, 2, 3)]

    def with_partner(pieces, after=()):
        (mine,) = run(
            "join_pieces",
            join_pieces,
            [((4,) + pieces[0].shape, BF)],
            at, *pieces,
            scratch=[sem],
            hbm=(1, 2, 3, 4),
            hbm_out=(0,),
            after=after,
        )
        return mine, place.core(mine)

    grad_of = [((tokens, units), BF), half_f, half_b]
    back_of = [half_f, half_e]
    inner_of = [((tokens, inner), BF), half_f, half_b]

    got = place.core(low)
    grad_upper2, keep, send = run(
        "feed_back", feed_back, grad_of, at, low, got, weights2, slope2
    )
    chip, others = quad_sum(keep, send)
    units2 = run(
        "unit_grads",
        unit_grads,
        unit_parts,
        at, low21, got21, low, got, activ2, grad_upper2,
        after=[chip],
    )
    early = units2[0]
    units2 = send_staged(*units2)
    matrix1, bias1 = head_weights(0, [*heads, out_got], [early])
    qkv1, lse1, _ = run(
        "attention_again",
        attention_again,
        [((tokens, inner), BF), lse_of, ((tokens, width), BF)],
        at, pack, matrix1, bias1,
        after=[matrix1],
    )
    sums = [low, got]
    back, low = run(
        "norm_backward",
        norm_backward,
        back_of,
        at, sum21, back, chip, others, norm_gain[1, 0][None],
        after=[early, lse1],
    )
    got = place.core(low)
    grad_qkv2, keep, send = run(
        "attention_back",
        attention_back,
        inner_of,
        at, low, got, matrix2, qkv2, lse2, pack,
    )
    chip, others = quad_sum(keep, send, [units2[1], units2[3]])
    heads2 = run(
        "head_grads",
        head_grads_later,
        head_parts,
        at, low12, got12, grad_qkv2, mixed2, low, got,
        after=[send],
    )
    early = heads2[0]
    heads2 = send_direct(heads2)
    sums = [low, got] + sums
    back, low = run(
        "norm_backward",
        norm_backward,
        back_of,
        at, sum12, back, chip, others, norm_gain[0, 1][None],
        after=[early, *heads2[1:3]],
    )
    got = place.core(low)
    grad_upper1, keep, send = run(
        "feed_back", feed_back, grad_of, at, low, got, weights1, slope1
    )
    chip, others = quad_sum(keep, send)
    units1 = run(
        "unit_grads",
        unit_grads,
        unit_parts,
        at, low11, got11, low, got, activ1, grad_upper1,
        after=[send],
    )
    early = units1[0]
    units1 = send_staged(*units1)
    units2 = next_stage(units2, after=[send])
    sums = [low, got] + sums
    back, low = run(
        "norm_backward",
        norm_backward,
        back_of,
        at, sum11, back, chip, others, norm_gain[0, 0][None],
        after=[early, units2[1], units2[3], heads2[3]],
    )
    got = place.core(low)
    sums = [low, got] + sums
    later = sum_chips(combine_both, (*units2, *heads2), unit_half + head_half, after=[low])
    grad_qkv1, keep, send = run(
        "attention_back",
        attention_back,
        inner_of,
        at, low, got, matrix1, qkv1, lse1, pack,
        after=[later[0]],
    )
    units1 = next_stage(units1, after=[send])
    heads1 = run(
        "head_grads",
        head_grads_first,
        head_parts,
        at, pack, grad_qkv1, mixed1, low, got, *sums,
        scratch=[pltpu.VMEM((8, EXTRA, features), BF), pltpu.SemaphoreType.DMA((8,))],
        hbm=range(6, 14),
        after=[units1[0]],
    )
    early = heads1[0]
    heads1 = send_direct(heads1)
    row_quarter = (quarter, features)
    mine, other = run(
        "tail_one",
        tail_one,
        [(row_quarter, F32), (row_quarter, BF)],
        at, keep, place.core(send), back,
        after=[early],
    )
    units1 = sum_chips(combine_staged, units1, unit_half, after=[mine])
    rows, both = run(
        "tail_two",
        tail_two,
        [row_quarter_f, ((2, quarter, features), BF)],
        at, mine, place.side(other), final,
        after=[units1[0]],
    )
    both = place.cross(both)
    final_out, input_grad = (
        jnp.where(place.native, own, got.astype(F32)) for own, got in zip((final, rows), both)
    )
    later = sum_planes([later], after=[rows, *units1[1:], *heads1[1:]])
    early = later[0]
    heads1 = sum_chips(combine_direct, heads1, head_half, after=[early])
    first = sum_planes([units1, heads1])
    later = with_partner(later, [first[0]])
    grads, small2 = unpack(1, later, [], [both])
    first = with_partner(first, grads[:1])

    (up, down, qkv, out), small1 = unpack(0, first, grads)
    pairs = (layers, 2, features)
    bup, bqv, bias, gain, shift = run(
        "write_small",
        write_small,
        [((layers, units), F32), ((layers, 2, width), F32)] + [(pairs, F32)] * 3,
        at, *small1, *small2,
    )
    return (
        final_out,
        input_grad,
        jnp.transpose(qkv.reshape(layers, 3, width, features), (0, 3, 1, 2)),
        bqv,
        out,
        bias,
        gain,
        shift,
        up,
        bup,
        down,
    )


def solution(mesh):
    columns = Mesh(mesh.devices.reshape(-1, 2, 2, 2, mesh.shape["tp"]), AXES)
    rows = P(AXES[:4], None)
    return jax.shard_map(
        on_device,
        mesh=columns,
        in_specs=(
            rows,
            rows,
            rows,
            rows,
            P(None, None, None, "tp"),
            P(None, None, "tp"),
            P(None, "tp", None),
            P(),
            P(),
            P(),
            P(None, None, "tp"),
            P(None, "tp"),
            P(None, "tp", None),
        ),
        out_specs=(
            P(AXES, None),
            P(AXES, None),
            P(None, None, None, "tp"),
            P(None, None, "tp"),
            P(None, "tp", None),
            P(),
            P(),
            P(),
            P(None, None, "tp"),
            P(None, "tp"),
            P(None, "tp", None),
        ),
        check_vma=False,
    )
```

```python
import functools

import jax
import jax.numpy as jnp
from jax import lax
from jax.experimental import pallas as pl
from jax.experimental.pallas import tpu as pltpu
from jax.sharding import Mesh
from jax.sharding import PartitionSpec as P

HEAD_DIM = 64
EPS = 1e-06
NEG = -1e30
EXTRA = 16
AXES = ("far", "u", "v", "c", "tp")
BF = jnp.bfloat16
F32 = jnp.float32
VMEM_BYTES = 24 << 20


class Place:
    def __init__(self):
        self.fars = lax.axis_size("far")
        self.core_no = lax.axis_index("c")
        self.z = lax.axis_index("tp")
        self.native = self.core_no == self.z // 2
        chip = lax.axis_index("u") * 2 + lax.axis_index("v")
        self.vector = jnp.stack(
            [chip, self.core_no, self.z, self.native.astype(jnp.int32)]
        ).astype(jnp.int32)

    def move(self, values, where):
        pairs = []
        for far in range(self.fars):
            for chip in range(4):
                for c in range(2):
                    for z in range(4):
                        to = where(chip, c, z)
                        if to is not None:
                            base = far * 4
                            source = ((base + chip) * 2 + c) * 4 + z
                            target = ((base + to[0]) * 2 + to[1]) * 4 + to[2]
                            pairs.append((source, target))
        return lax.ppermute(values, AXES, pairs)

    def core(self, values):
        return self.move(values, lambda i, c, z: (i, c ^ 1, z))

    def to_foreign(self, values):
        return self.move(values, lambda i, c, z: (i, c ^ 1, z) if c == z // 2 else None)

    def side(self, values):
        return self.move(values, lambda i, c, z: (i, c, z ^ 1))

    def cross(self, values):
        return self.move(values, lambda i, c, z: (i, c ^ 1, z ^ 2) if c != z // 2 else None)

    def over(self, values):
        return self.move(values, lambda i, c, z: (i, c, z ^ 2) if c != z // 2 else None)

    def chip(self, values, k, native=None):
        def where(i, c, z):
            if native is None or native == (c == z // 2):
                return (i ^ k, c, z)
            return None

        return self.move(values, where)

    def add_far(self, values):
        step = 1
        while step < self.fars:
            pairs = []
            for far in range(self.fars):
                pairs += [(far * 32 + i, (far ^ step) * 32 + i) for i in range(32)]
            got = lax.ppermute(values, AXES, pairs)
            values = (values.astype(F32) + got.astype(F32)).astype(values.dtype)
            step *= 2
        return values


class Layer:
    def __init__(self, whole, n):
        self.whole, self.n = whole, n


class Argument:
    def __init__(self, whole):
        self.whole = whole


def run(name, kernel, outs, *args, scratch=(), after=(), hbm=(), hbm_out=(), cost=0):
    n = len(args)

    def body(*refs):
        kernel(*refs[:n], *refs[n + len(after) :])

    anywhere = pl.BlockSpec(memory_space=pl.ANY)
    vmem = pl.BlockSpec(memory_space=pltpu.VMEM)
    in_specs, given = [pl.BlockSpec(memory_space=pltpu.SMEM)], [args[0]]
    for i in range(1, n):
        arg = args[i]
        if isinstance(arg, Layer):
            block = (None,) + arg.whole.shape[1:]
            zeros = (0,) * (arg.whole.ndim - 1)
            in_specs.append(pl.BlockSpec(block, lambda i, at=(arg.n,) + zeros: at))
            given.append(arg.whole)
        else:
            pinned = isinstance(arg, Argument)
            space = pltpu.HBM if pinned else pl.ANY if i in hbm else pltpu.VMEM
            in_specs.append(pl.BlockSpec(memory_space=space))
            given.append(arg.whole if pinned else arg)
    in_specs += [anywhere] * len(after)
    return pl.pallas_call(
        body,
        name=name,
        grid=(1,) if any(isinstance(arg, Layer) for arg in args) else (),
        out_shape=[jax.ShapeDtypeStruct(s, d) for s, d in outs],
        in_specs=in_specs,
        out_specs=[anywhere if i in hbm_out else vmem for i in range(len(outs))],
        scratch_shapes=list(scratch),
        cost_estimate=pl.CostEstimate(
            flops=cost * 10**9, bytes_accessed=0, transcendentals=0
        ),
        compiler_params=pltpu.CompilerParams(vmem_limit_bytes=VMEM_BYTES),
    )(*given, *after)


def dot_nn(a, b):
    return lax.dot_general(a, b, (((1,), (0,)), ((), ())), preferred_element_type=F32)


def dot_nt(a, b):
    return lax.dot_general(a, b, (((1,), (1,)), ((), ())), preferred_element_type=F32)


def dot_tn(a, b):
    return lax.dot_general(a, b, (((0,), (0,)), ((), ())), preferred_element_type=F32)


def thirds(value):
    hi = value.astype(BF).astype(F32)
    mid = (value - hi).astype(BF).astype(F32)
    return hi, mid, value - hi - mid


def extra_rows(rows, columns):
    padded = [
        jnp.concatenate([r, jnp.zeros((1, columns - r.shape[1]), F32)], axis=1)
        if r.shape[1] < columns
        else r
        for r in rows
    ]
    return jnp.concatenate(padded + [jnp.zeros((EXTRA - len(rows), columns), F32)], axis=0)


def multiple(index, size):
    return pl.ds(pl.multiple_of(index * size, size), size)


def bias_rows(place, bias, rows):
    rows[...] = extra_rows(thirds(bias[0:1]), rows.shape[1]).astype(BF)


def copy_all(pairs, sem):
    copies = [pltpu.make_async_copy(a, b, sem.at[i]) for i, (a, b) in enumerate(pairs)]
    for copy in copies:
        copy.start()
    for copy in copies:
        copy.wait()


def pack_units(place, up, down, bias, piece, tail, sem, n, whole):
    rows = up.shape[1] if whole else up.shape[1] // 4
    at = slice(0, rows) if whole else multiple(place[0], rows)
    tail[...] = extra_rows(thirds(bias[n : n + 1]), up.shape[2]).astype(BF)
    copy_all(
        [
            (up.at[n, at], piece.at[0:rows]),
            (down.at[n, at], piece.at[rows : 2 * rows]),
            (tail, piece.at[2 * rows :]),
        ],
        sem,
    )


def head_biases(bias):
    both = jnp.concatenate([bias[0:1], bias[1:2]], axis=1)
    return extra_rows(thirds(both), 4 * bias.shape[1]).astype(BF)


def pack_heads(place, qkv_w, out_w, bias, pack, tail, sem):
    chip = place[0]
    rows, fewer = out_w.shape[1], qkv_w.shape[1] // 4
    inner = qkv_w.shape[1] // rows
    for n in range(2):
        tail[n] = head_biases(bias[n])
    second = rows + EXTRA

    @pl.when(chip < inner)
    def _():
        copy_all([(qkv_w.at[1, multiple(chip, rows)], pack.at[0:rows])], sem)

    @pl.when(chip >= inner)
    def _():
        copy_all([(out_w.at[1], pack.at[0:rows])], sem)

    copy_all(
        [
            (qkv_w.at[0, multiple(chip, fewer)], pack.at[second : second + fewer]),
            (tail.at[1], pack.at[rows:second]),
            (tail.at[0], pack.at[second + fewer :]),
        ],
        sem,
    )


def pack_rows(place, hidden, grad, seg, mask, own, other):
    c = place[1]
    tokens, features = hidden.shape
    half = tokens // 2
    for ref, first in ((own, c), (other, 1 - c)):
        ids = []
        for i, h in enumerate((first, 1 - first)):
            at = multiple(h, half)
            ref[i * half : (i + 1) * half] = hidden[at]
            ids.append(seg[0:1, at])
        at = multiple(first, half)
        scale = seg_column(mask[0:1, at].astype(F32))
        ref[tokens : tokens + half] = (grad[at].astype(F32) * scale).astype(BF)
        ids = jnp.concatenate(ids, axis=1).astype(F32)
        ref[tokens + half :] = extra_rows([ids], features).astype(BF)


def choose_units(place, up, down, bias, *refs, n):
    *pieces, both, bias_out, tail, sem = refs
    chip, native = place[0], place[3]
    rows = up.shape[1] // len(pieces)

    @pl.when(native == 1)
    def _():
        copy_all([(up.at[n], both.at[0]), (down.at[n], both.at[1])], sem)
        bias_out[...] = bias[n : n + 1]

    @pl.when(native == 0)
    def _():
        pairs = [(pieces[0].at[2 * rows :], tail)]
        for k, ref in enumerate(pieces):
            to = slice(0, rows) if len(pieces) == 1 else multiple(chip ^ k, rows)
            for m in range(2):
                pairs.append((ref.at[m * rows : (m + 1) * rows], both.at[m, to]))
        copy_all(pairs, sem)
        parts = tail[...].astype(F32)
        bias_out[...] = parts[0:1] + parts[1:2] + parts[2:3]


def choose_heads(place, qkv_w, out_w, bias, *refs, n):
    *pieces, matrix, bias_out, tail, sem = refs
    chip, native = place[0], place[3]
    width, inner = out_w.shape[1], qkv_w.shape[1]

    @pl.when(native == 1)
    def _():
        copy_all([(qkv_w.at[n], matrix.at[0:inner]), (out_w.at[n], matrix.at[inner:])], sem)
        bias_out[...] = qkv_bias(bias[0:1], bias[1:2])

    @pl.when(native == 0)
    def _():
        start, rows = (0, width) if n else (width + EXTRA, inner // 4)
        pairs = [(pieces[0].at[start + rows : start + rows + EXTRA], tail)]
        for k in range(4):
            pairs.append(
                (pieces[k].at[start : start + rows], matrix.at[multiple(chip ^ k, rows)])
            )
        if n == 0:
            pairs.append((pieces[4], matrix.at[inner:]))
        copy_all(pairs, sem)
        parts = tail[...].astype(F32)
        row = parts[0:1] + parts[1:2] + parts[2:3]
        bias_out[...] = qkv_bias(row[:, :width], row[:, width : 2 * width])


def seg_column(seg_row):
    n = seg_row.shape[1]
    parts = [
        jnp.broadcast_to(seg_row[:, i : i + 128], (128, 128)).T[:, 0:1] for i in range(0, n, 128)
    ]
    return jnp.concatenate(parts, axis=0)


def attend(qkv, seg_row, mixed, lse, tile):
    tokens = qkv.shape[0]
    width = qkv.shape[1] // 3
    heads = width // HEAD_DIM
    column = seg_column(seg_row)
    for start in range(0, tokens, tile):
        same = column[start : start + tile] == seg_row
        outs, logs = [], []
        for head in range(heads):
            at = head * HEAD_DIM
            query = qkv[start : start + tile, at : at + HEAD_DIM] * HEAD_DIM ** (-0.5)
            keys = qkv[:, width + at : width + at + HEAD_DIM]
            values = qkv[:, 2 * width + at : 2 * width + at + HEAD_DIM]
            scores = jnp.where(same, dot_nt(query, keys), NEG)
            top = jnp.max(scores, axis=1, keepdims=True)
            expon = jnp.exp(scores - top)
            total = jnp.sum(expon, axis=1, keepdims=True)
            outs.append(dot_nn(expon.astype(BF), values) / total)
            logs.append(top + jnp.log(total))
        mixed[start : start + tile] = jnp.concatenate(outs, axis=1).astype(BF)
        logs.append(jnp.zeros((tile, lse.shape[1] - heads), F32))
        lse[start : start + tile] = jnp.concatenate(logs, axis=1)


def qkv_bias(bias_q, bias_v):
    return jnp.concatenate([bias_q, jnp.zeros_like(bias_q), bias_v], axis=1)


def attention_home(place, hidden, weight, bias, seg, mixed, ordered, qkv, lse):
    first = place[2] // 2
    tokens = hidden.shape[0]
    half = tokens // 2
    ids = []
    for i, h in enumerate((first, 1 - first)):
        at = multiple(h, half)
        ordered[i * half : (i + 1) * half] = hidden[at]
        ids.append(seg[0:1, at])
    seg_row = jnp.concatenate(ids, axis=1).astype(F32)
    qkv[...] = (dot_nt(ordered[...], weight[...]) + qkv_bias(bias[0:1], bias[1:2])).astype(BF)
    attend(qkv, seg_row, mixed, lse, half)


def put_half(part, keep, send):
    half = part.shape[0] // 2
    keep[...] = part[:half]
    send[...] = part[half:].astype(BF)


def project_first(place, mixed, mixed_got, out_w, out_got, kept, keep, send):
    native = place[3] == 1
    rows = jnp.where(native, out_w[...], out_got[...])
    values = jnp.where(native, mixed[...], mixed_got[...])
    kept[...] = values
    put_half(dot_nn(values, rows), keep, send)


def seg_of(pack, tokens):
    return pack[-EXTRA:].astype(F32)[0:1, :tokens]


def attention_again(place, pack, matrix, bias, qkv, lse, mixed):
    tokens, inner = qkv.shape
    qkv[...] = (dot_nt(pack[:tokens], matrix[:inner]) + bias[...]).astype(BF)
    attend(qkv, seg_of(pack, tokens), mixed, lse, tokens // 2)


def attention_column(place, own, got, matrix, bias, pack, qkv, mixed, lse, keep, send):
    tokens, inner = qkv.shape
    hidden = jnp.concatenate([own[...], got[...]], axis=0)
    qkv[...] = (dot_nt(hidden, matrix[:inner]) + bias[...]).astype(BF)
    attend(qkv, seg_of(pack, tokens), mixed, lse, tokens // 2)
    put_half(dot_nn(mixed[...], matrix[inner:]), keep, send)


def attend_back(qkv, lse, grad_mixed, seg_row, grad_qkv, tile):
    tokens = qkv.shape[0]
    width = qkv.shape[1] // 3
    heads = width // HEAD_DIM
    column = seg_column(seg_row)
    scale = HEAD_DIM ** (-0.5)
    grads = [[], [], []]
    for head in range(heads):
        at = head * HEAD_DIM
        keys = qkv[:, width + at : width + at + HEAD_DIM]
        values = qkv[:, 2 * width + at : 2 * width + at + HEAD_DIM]
        grad_keys = jnp.zeros((tokens, HEAD_DIM), F32)
        grad_values = jnp.zeros((tokens, HEAD_DIM), F32)
        grad_query = []
        for start in range(0, tokens, tile):
            rows = slice(start, start + tile)
            query = qkv[rows, at : at + HEAD_DIM] * scale
            grad_out = grad_mixed[rows, at : at + HEAD_DIM]
            scores = jnp.where(column[rows] == seg_row, dot_nt(query, keys), NEG)
            probs = jnp.exp(scores - lse[rows, head : head + 1])
            grad_probs = dot_nt(grad_out, values)
            inner = jnp.sum(probs * grad_probs, axis=1, keepdims=True)
            grad_scores = (probs * (grad_probs - inner)).astype(BF)
            grad_query.append(dot_nn(grad_scores, keys) * scale)
            grad_keys += dot_tn(grad_scores, query)
            grad_values += dot_tn(probs.astype(BF), grad_out)
        grads[0].append(jnp.concatenate(grad_query, axis=0))
        grads[1].append(grad_keys)
        grads[2].append(grad_values)
    grad_qkv[...] = jnp.concatenate(grads[0] + grads[1] + grads[2], axis=1).astype(BF)


def join_grads(own, got):
    return jnp.concatenate([own[:-EXTRA], got[:-EXTRA]], axis=0)


def attention_back(place, own, got, matrix, qkv, lse, pack, grad_qkv, keep, send):
    tokens, inner = qkv.shape
    grad_att = join_grads(own, got)
    grad_mixed = dot_nt(grad_att, matrix[inner:]).astype(BF)
    attend_back(qkv, lse, grad_mixed, seg_of(pack, tokens), grad_qkv, tokens // 2)
    put_half(dot_nn(grad_qkv[...], matrix[:inner]), keep, send)


def part_rows(whole_a, whole_b, sums, sums_in_b):
    features = whole_a[0].shape[1]
    for p in range(4):
        parts = [whole_a[p], whole_b[p]]
        rows = extra_rows(sums if p == 0 else [], features)
        parts[sums_in_b] = jnp.concatenate([parts[sums_in_b], rows], axis=0)
        yield p, parts[0].astype(BF), parts[1].astype(BF)


def put_direct(place, whole_a, whole_b, sums, *refs):
    for p, a, b in part_rows(whole_a, whole_b, sums, 1):
        part = jnp.concatenate([a, b], axis=0)
        for k, ref in enumerate(refs):

            @pl.when(place[0] ^ p == k)
            def _(ref=ref):
                ref[...] = part


def put_staged(place, whole_a, whole_b, sums, sums_in_b, keep_a, send_a, keep_b, send_b):
    for p, a, b in part_rows(whole_a, whole_b, sums, sums_in_b):
        offset = place[0] ^ p
        over_u, over_v = offset // 2, offset % 2

        @pl.when(over_v == 0)
        def _():
            keep_a[over_u] = a

        @pl.when(over_v == 1)
        def _():
            send_a[multiple(over_u, a.shape[0])] = a

        @pl.when(over_u == 0)
        def _():
            keep_b[over_v] = b

        @pl.when(over_u == 1)
        def _():
            send_b[multiple(over_v, b.shape[0])] = b


def head_grads(hidden, grad_qkv, mixed, a_own, a_got, sums):
    grad_att = join_grads(a_own, a_got)
    whole = jnp.concatenate([dot_tn(grad_qkv[...], hidden), dot_tn(mixed[...], grad_att)], axis=0)
    bias = jnp.sum(grad_qkv[...].astype(F32), axis=0, keepdims=True)
    rows = whole.shape[0] // 4
    cut = rows // 2
    first = [whole[p * rows : p * rows + cut] for p in range(4)]
    second = [whole[p * rows + cut : (p + 1) * rows] for p in range(4)]
    return first, second, [bias] + sums


def head_grads_first(place, pack, grad_qkv, mixed, a_own, a_got, *refs):
    norms, (u_keep_a, u_got_a, u_keep_b, u_got_b) = refs[:8], refs[8:12]
    keep_a, keep_b, mine_a, mine_b, over_v, over_u, rows, sem = refs[12:]
    copy_all([(ref.at[ref.shape[0] - EXTRA :], rows.at[i]) for i, ref in enumerate(norms)], sem)
    total = []
    for i in range(4):
        both = rows[2 * i].astype(F32) + rows[2 * i + 1].astype(F32)
        total += [both[j : j + 1] for j in range(3)]
    hidden = pack[: grad_qkv.shape[0]]
    parts = head_grads(hidden, grad_qkv, mixed, a_own, a_got, total)
    put_staged(place, *parts, 1, keep_a, over_v, keep_b, over_u)
    mine_a[...], over_u[2 * keep_b.shape[1] :] = next_parts(u_keep_a, u_got_a)
    mine_b[...], over_v[2 * keep_a.shape[1] :] = next_parts(u_keep_b, u_got_b)


def head_grads_later(place, own, got, grad_qkv, mixed, a_own, a_got, *parts):
    hidden = jnp.concatenate([own[...], got[...]], axis=0)
    put_direct(place, *head_grads(hidden, grad_qkv, mixed, a_own, a_got, []), *parts)


def feed_forward(place, own, got, weights, bias, activ, slope, keep, send):
    hidden = jnp.concatenate([own[...], got[...]], axis=0)
    upper = dot_nn(hidden, weights[0]) + bias[...]
    cdf = 0.5 * (1.0 + lax.erf(upper * (0.5**0.5)))
    activ[...] = (upper * cdf).astype(BF)
    slope[...] = cdf + upper * jnp.exp(-0.5 * upper * upper) * 0.3989422804014327
    put_half(dot_nn(activ[...], weights[1]), keep, send)


def feed_back(place, own, got, weights, slope, grad_upper, keep, send):
    grad = join_grads(own, got)
    grad_upper[...] = (dot_nt(grad, weights[1]) * slope[...]).astype(BF)
    put_half(dot_nt(grad_upper[...], weights[0]), keep, send)


def unit_grads(place, x_own, x_got, g_own, g_got, activ, grad_upper, *parts):
    hidden = jnp.concatenate([x_own[...], x_got[...]], axis=0)
    grad = join_grads(g_own, g_got)
    up = dot_tn(hidden, grad_upper[...])
    down = dot_tn(activ[...], grad)
    bias = jnp.sum(grad_upper[...].astype(F32), axis=0, keepdims=True)
    rows = up.shape[0] // 4
    first = [up[p * rows : (p + 1) * rows] for p in range(4)]
    second = [down[p * rows : (p + 1) * rows] for p in range(4)]
    put_staged(place, first, second, [bias], 0, *parts)


def chip_sum(place, keep, got, chip, low):
    chip[...] = keep[...] + got[...].astype(F32)
    low[...] = chip[...].astype(BF)


def next_parts(keep, got):
    rows = keep.shape[1]
    mine = keep[0].astype(F32) + got[0:rows].astype(F32)
    return mine, (keep[1].astype(F32) + got[rows : 2 * rows].astype(F32)).astype(BF)


def combine_one(place, keep_a, got_a, keep_b, got_b, mine_a, for_a, mine_b, for_b):
    mine_a[...], for_a[...] = next_parts(keep_a, got_a)
    mine_b[...], for_b[...] = next_parts(keep_b, got_b)


def combine_joint(
    place, keep_a, keep_b, u_a, u_b, got_v, got_u, mine_a, for_a, mine_b, for_b, units
):
    mine_a[...], for_a[...] = next_parts(keep_a, got_v)
    mine_b[...], for_b[...] = next_parts(keep_b, got_u)
    rows = u_a.shape[0]
    units[:rows] = (u_a[...] + got_u[2 * keep_b.shape[1] :].astype(F32)).astype(BF)
    units[rows:] = (u_b[...] + got_v[2 * keep_a.shape[1] :].astype(F32)).astype(BF)


def combine_staged(place, mine_a, got_a, mine_b, got_b, total):
    rows = mine_a.shape[0]
    total[:rows] = (mine_a[...] + got_a[...].astype(F32)).astype(BF)
    total[rows:] = (mine_b[...] + got_b[...].astype(F32)).astype(BF)


def combine_both(place, mine_a, got_a, mine_b, got_b, own, got1, got2, got3, total):
    start = mine_a.shape[0] + mine_b.shape[0]
    combine_staged(place, mine_a, got_a, mine_b, got_b, total.at[0:start])
    terms = [ref[...].astype(F32) for ref in (own, got1, got2, got3)]
    total[start:] = ((terms[0] + terms[1]) + (terms[2] + terms[3])).astype(BF)


def combine_planes(place, *refs, spans):
    *parts, first, second = refs
    at = [0, 0]
    for i, parts_of in enumerate(spans):
        mine, got = parts[2 * i : 2 * i + 2]
        start = 0
        for halves in parts_of:
            for j, (out, rows) in enumerate(zip((first, second), halves)):
                value = mine[start : start + rows].astype(F32) + got[start : start + rows].astype(F32)
                out[at[j] : at[j] + rows] = value.astype(BF)
                start += rows
                at[j] += rows


def tail_one(place, keep, got, back, mine, other):
    s = place[2] % 2
    rows = mine.shape[0]
    at, away = multiple(s, rows), multiple(1 - s, rows)
    mine[...] = keep[at] + got[at].astype(F32) + back[at]
    other[...] = (keep[away] + got[away].astype(F32)).astype(BF)


def tail_two(place, mine, got, final, rows, both):
    rows[...] = mine[...] + got[...].astype(F32)
    both[0] = final[...].astype(BF)
    both[1] = rows[...].astype(BF)


def normalize(values):
    center = values - jnp.mean(values, axis=1, keepdims=True)
    spread = jnp.mean(center * center, axis=1, keepdims=True)
    inv = lax.rsqrt(spread + EPS)
    return center * inv, inv


def norm_forward(place, base, chip, got, bias, gain, shift, total, out, low):
    values = base[...].astype(F32) + (chip[...].astype(BF).astype(F32) + got[...].astype(F32) + bias[...])
    total[...] = values
    unit, _ = normalize(values)
    result = unit * gain[...] + shift[...]
    out[...] = result
    low[...] = result.astype(BF)


def back_through(values, gain, grad):
    unit, inv = normalize(values)
    scaled = grad * gain
    first = jnp.mean(scaled, axis=1, keepdims=True)
    second = jnp.mean(scaled * unit, axis=1, keepdims=True)
    back = inv * (scaled - first - unit * second)
    low = back.astype(BF)
    sums = [
        jnp.sum(low.astype(F32), axis=0, keepdims=True),
        jnp.sum(grad * unit, axis=0, keepdims=True),
        jnp.sum(grad, axis=0, keepdims=True),
    ]
    return back, jnp.concatenate([low, extra_rows(sums, low.shape[1]).astype(BF)], axis=0)


def norm_turn(place, base, chip, got, bias, gain, shift, pack, final, back, low):
    half = base.shape[0]
    quarter = half // 2
    values = base[...] + (chip[...].astype(BF).astype(F32) + got[...].astype(F32) + bias[...])
    unit, _ = normalize(values)
    back[...] = unit * gain[...] + shift[...]
    final[...] = back[multiple(place[2] % 2, quarter)]
    grad = pack[2 * half : 3 * half].astype(F32)
    back[...], low[...] = back_through(values, gain[...], grad)


def norm_backward(place, values, base, chip, got, gain, back, low):
    grad = base[...] + (chip[...].astype(BF).astype(F32) + got[...].astype(F32))
    back[...], low[...] = back_through(values[...], gain[...], grad)


def join_pieces(place, *refs):
    *pieces, mine, sem = refs
    copy_all([(ref, mine.at[k]) for k, ref in enumerate(pieces)], sem)


def unpack_parts(place, *refs, n, ks, smalls, last, unit_half):
    count = len(ks)
    (mine, got), refs = ([ref.at[i] for i in range(count)] for ref in refs[:2]), refs[2:]
    given, refs = refs[:smalls], refs[smalls:]
    up, down, qkv, out, *small, stage, sem = refs[-(7 + 4 * last) :]
    chip, native = place[0], place[3] == 1
    rows = stage.shape[2]
    cut = rows // 2
    copies, sums = [], jnp.zeros((2, EXTRA, stage.shape[3]), F32)
    for i, k in enumerate(ks):
        p = chip ^ k
        a = jnp.where(native, mine[i][...], got[i][...]).astype(F32)
        b = jnp.where(native, got[i][...], mine[i][...]).astype(F32)
        at = multiple(p, rows)
        stage[i, 0] = a[:rows]
        copies.append(pltpu.make_async_copy(stage.at[i, 0], up.at[n, at], sem.at[i, 0]))
        copies[-1].start()
        stage[i, 1] = b[:rows]
        copies.append(pltpu.make_async_copy(stage.at[i, 1], down.at[n, at], sem.at[i, 1]))
        copies[-1].start()
        stage[i, 2, :cut] = a[unit_half[0] :]
        stage[i, 2, cut:] = b[unit_half[1] : unit_half[1] + cut]

        @pl.when(p < 3)
        def _(i=i, at=at):
            pltpu.make_async_copy(stage.at[i, 2], qkv.at[n, at], sem.at[i, 2]).start()

        @pl.when(p == 3)
        def _(i=i):
            pltpu.make_async_copy(stage.at[i, 2], out.at[n], sem.at[i, 2]).start()

        found = jnp.stack([a[rows : unit_half[0]], b[unit_half[1] + cut :]])
        sums = sums + jnp.where(p == 0, found, 0.0)
    if last:
        other, first = given
        sums = sums + first[...]
        bup, bqv, *norms = small
        width = bqv.shape[2]
        for i, (u, h) in enumerate(((sums[0], sums[1]), (other[0], other[1]))):
            bup[i : i + 1] = u[0:1]
            bqv[i, 0:1] = h[0:1, 0:width]
            bqv[i, 1:2] = h[0:1, 2 * width : 3 * width]
            for j in range(2):
                for m, ref in enumerate(norms):
                    row = 1 + (2 * i + j) * 3 + m
                    ref[i, j : j + 1] = sums[1, row : row + 1]
    else:
        small[0][...] = sums
    for copy in copies:
        copy.wait()
    for i, k in enumerate(ks):
        pltpu.make_async_copy(stage.at[i, 2], out.at[n], sem.at[i, 2]).wait()


def on_device(
    hidden_in,
    out_grad,
    segment_ids,
    loss_mask,
    w_qkv,
    b_query_value,
    w_out,
    branch_bias,
    norm_gain,
    norm_shift,
    w_up,
    b_up,
    w_down,
):
    place = Place()
    at = place.vector
    layers, features = w_qkv.shape[:2]
    width = w_qkv.shape[-1]
    inner = 3 * width
    tokens = hidden_in.shape[0]
    half, quarter = tokens // 2, tokens // 4
    units = w_up.shape[-1]
    unit_rows, head_rows = features // 4, (inner + width) // 4
    w_qkv_t = jnp.transpose(w_qkv, (0, 2, 3, 1)).reshape(layers, inner, features)

    def gain_of(n, i):
        return branch_bias[n, i][None], norm_gain[n, i][None], norm_shift[n, i][None]

    half_f = ((half, features), F32)
    half_b = ((half, features), BF)
    half_e = ((half + EXTRA, features), BF)
    unit_piece = ((2 * unit_rows + EXTRA, features), BF)
    head_piece = ((head_rows + EXTRA, features), BF)
    row_quarter_f = ((quarter, features), F32)
    sem = pltpu.SemaphoreType.DMA((9,))
    tail = pltpu.VMEM((EXTRA, features), BF)

    def spread_chips(values):
        return [values] + [place.chip(values, k, native=False) for k in (1, 2, 3)]

    def unit_weights(n, pieces, after=()):
        return run(
            "choose_units",
            functools.partial(choose_units, n=n),
            [((2, units, features), BF), ((1, units), F32)],
            at, Argument(w_up), Argument(w_down), b_up, *pieces,
            scratch=[tail, sem],
            hbm=(1, 2, *range(4, 4 + len(pieces))),
            hbm_out=(0,),
            after=after,
        )

    def unit_pack(n, whole, after=()):
        rows = 2 * (units if whole else unit_rows) + EXTRA
        return run(
            "pack_units",
            functools.partial(pack_units, n=n, whole=whole),
            [((rows, features), BF)],
            at, Argument(w_up), Argument(w_down), b_up,
            scratch=[tail, sem],
            hbm=(1, 2),
            hbm_out=(0,),
            after=after,
        )[0]

    def head_weights(n, pieces, after=()):
        return run(
            "choose_heads",
            functools.partial(choose_heads, n=n),
            [((inner + width, features), BF), ((1, inner), F32)],
            at, Argument(w_qkv_t), Argument(w_out), Layer(b_query_value, n), *pieces,
            scratch=[tail, sem],
            hbm=(1, 2, *range(4, 4 + len(pieces))),
            hbm_out=(0,),
            after=after,
        )

    def quad_sum(keep, send, after=()):
        chip, low = run(
            "chip_sum", chip_sum, [half_f, half_b], at, keep, place.core(send), after=after
        )
        return chip, place.side(low)

    (tail1,) = run("bias_rows", bias_rows, [((EXTRA, features), BF)], at, b_up)
    start = at[0] * unit_rows
    units1 = jnp.concatenate(
        [lax.dynamic_slice(w, (0, start, 0), (1, unit_rows, features))[0] for w in (w_up, w_down)]
        + [tail1]
    )
    early = units1
    out_got = place.cross(w_out[0])
    units1 = place.cross(units1)
    row_pack = ((tokens + half + EXTRA, features), BF)
    pack_own, pack_other = run(
        "pack_rows",
        pack_rows,
        [row_pack, row_pack],
        at, hidden_in, out_grad, segment_ids, loss_mask,
        after=[early],
    )
    (mixed_home,) = run(
        "attention_home",
        attention_home,
        [((tokens, width), BF)],
        at, hidden_in, Layer(w_qkv_t, 0), Layer(b_query_value, 0), segment_ids,
        scratch=[
            pltpu.VMEM((tokens, features), BF),
            pltpu.VMEM((tokens, inner), BF),
            pltpu.VMEM((tokens, 128), F32),
        ],
        after=[pack_own],
        cost=10,
    )
    mixed_got = place.cross(mixed_home)
    pack = jnp.where(place.native, pack_own, place.to_foreign(pack_other))

    head_pack_rows = width + inner // 4 + 2 * EXTRA
    (heads,) = run(
        "pack_heads",
        pack_heads,
        [((head_pack_rows, features), BF)],
        at, Argument(w_qkv_t), Argument(w_out), b_query_value,
        scratch=[pltpu.VMEM((2, EXTRA, features), BF), sem],
        hbm=(1, 2),
        hbm_out=(0,),
        after=[mixed_home, pack],
    )
    heads = place.cross(heads)

    mixed1, keep, send = run(
        "project_first",
        project_first,
        [((tokens, width), BF), half_f, half_b],
        at, mixed_home, mixed_got, Layer(w_out, 0), out_got,
    )
    chip, others = quad_sum(keep, send, [units1])
    sum11, norm11, low11 = run(
        "norm_forward",
        norm_forward,
        [half_f, half_f, half_b],
        at, pack[:half], chip, others, *gain_of(0, 0),
        after=[heads],
    )
    got11 = place.core(low11)
    weights1, b_up1 = unit_weights(0, spread_chips(units1), after=[low11])
    ffn_outs = [((tokens, units), BF), ((tokens, units), F32), half_f, half_b]
    activ1, slope1, keep, send = run(
        "feed_forward",
        feed_forward,
        ffn_outs,
        at, low11, got11, weights1, b_up1,
    )
    matrix_of = ((inner + width, features), BF)
    chip, others = quad_sum(keep, send)
    units2 = place.cross(unit_pack(1, False, [chip]))
    sum12, norm12, low12 = run(
        "norm_forward",
        norm_forward,
        [half_f, half_f, half_b],
        at, norm11, chip, others, *gain_of(0, 1),
    )
    got12 = place.core(low12)
    heads = spread_chips(heads)
    matrix2, bias2 = head_weights(1, heads, [low12])
    lse_of = ((tokens, 128), F32)
    qkv2, mixed2, lse2, keep, send = run(
        "attention_column",
        attention_column,
        [((tokens, inner), BF), ((tokens, width), BF), lse_of, half_f, half_b],
        at, low12, got12, matrix2, bias2, pack,
        after=[units2],
    )
    chip, others = quad_sum(keep, send)
    sum21, norm21, low21 = run(
        "norm_forward",
        norm_forward,
        [half_f, half_f, half_b],
        at, low12, chip, others, *gain_of(1, 0),
    )
    got21 = place.core(low21)
    weights2, b_up2 = unit_weights(1, spread_chips(units2), after=[low21])
    activ2, slope2, keep, send = run(
        "feed_forward", feed_forward, ffn_outs, at, low21, got21, weights2, b_up2
    )
    chip, others = quad_sum(keep, send)
    final, back, low = run(
        "norm_turn",
        norm_turn,
        [row_quarter_f, half_f, half_e],
        at, norm21, chip, others, *gain_of(1, 1), pack,
    )

    shapes = [
        (layers, features, units),
        (layers, units, features),
        (layers, inner, features),
        (layers, width, features),
    ]

    def unpack(n, ks, joined, smalls, small=(), earlier=(), after=()):
        sums = [(2, EXTRA, features)]
        given = [joined, place.core(joined), *small]
        vmem = pl.BlockSpec(memory_space=pltpu.VMEM)
        anywhere = pl.BlockSpec(memory_space=pl.ANY)
        return pl.pallas_call(
            functools.partial(
                unpack_parts,
                n=n,
                ks=ks,
                smalls=len(small),
                last=len(smalls) > 0,
                unit_half=unit_half,
            ),
            name="unpack_parts",
            out_shape=[jax.ShapeDtypeStruct(s, F32) for s in shapes + (smalls or sums)],
            in_specs=[pl.BlockSpec(memory_space=pltpu.SMEM)]
            + [vmem] * len(given)
            + [anywhere] * (len(after) + len(earlier)),
            out_specs=[anywhere] * 4 + [vmem] * len(smalls or sums),
            input_output_aliases={
                1 + len(given) + len(after) + i: i for i in range(len(earlier))
            },
            scratch_shapes=[
                pltpu.VMEM((len(ks), 3, unit_rows, features), F32),
                pltpu.SemaphoreType.DMA((len(ks), 3)),
            ],
            cost_estimate=pl.CostEstimate(
                flops=0 if smalls else 4 * 10**10, bytes_accessed=0, transcendentals=0
            ),
            compiler_params=pltpu.CompilerParams(vmem_limit_bytes=VMEM_BYTES),
        )(at, *given, *after, *earlier)

    unit_half = (unit_rows + EXTRA, unit_rows)
    head_half = (head_rows // 2, head_rows // 2 + EXTRA)
    def staged(halves):
        return [
            (shape, BF)
            for rows in halves
            for shape in ((2, rows, features), (2 * rows, features))
        ]

    head_parts = [((sum(head_half), features), BF)] * 4

    def send_direct(parts):
        return [parts[0]] + [place.chip(parts[k], k) for k in (1, 2, 3)]

    def send_staged(keep_a, send_a, keep_b, send_b):
        return keep_a, place.chip(send_a, 1), keep_b, place.chip(send_b, 2)

    def one_of(halves):
        return [((rows, features), kind) for rows in halves for kind in (F32, BF)]

    def next_stage(parts, after=()):
        mine_a, for_a, mine_b, for_b = run(
            "combine_one", combine_one, one_of(unit_half), at, *parts, after=after
        )
        return mine_a, place.chip(for_a, 2), mine_b, place.chip(for_b, 1)

    def sum_chips(kernel, parts, rows, after=()):
        return run(
            kernel.__name__, kernel, [((rows, features), BF)], at, *parts, after=after
        )[0]

    def sum_planes(groups, after=()):
        spans = [group[2] for group in groups]
        rows = sum(halves[0] for parts in spans for halves in parts)
        first, second = run(
            "combine_planes",
            functools.partial(combine_planes, spans=spans),
            [((rows, features), BF)] * 2,
            at, *[part for group in groups for part in group[:2]],
            after=after,
        )
        first, second = place.add_far(first), place.add_far(second)
        piece = jnp.where(place.native, first, place.core(second))
        return [piece] + [place.chip(piece, k) for k in (1, 2, 3)]

    grad_of = [((tokens, units), BF), half_f, half_b]
    back_of = [half_f, half_e]
    inner_of = [((tokens, inner), BF), half_f, half_b]

    got = place.core(low)
    grad_upper2, keep, send = run(
        "feed_back", feed_back, grad_of, at, low, got, weights2, slope2
    )
    chip, others = quad_sum(keep, send)
    units2 = run(
        "unit_grads",
        unit_grads,
        staged(unit_half),
        at, low21, got21, low, got, activ2, grad_upper2,
        after=[chip],
    )
    early = units2[0]
    units2 = send_staged(*units2)
    matrix1, bias1 = head_weights(0, [*heads, out_got], [early])
    qkv1, lse1, _ = run(
        "attention_again",
        attention_again,
        [((tokens, inner), BF), lse_of, ((tokens, width), BF)],
        at, pack, matrix1, bias1,
        after=[matrix1],
    )
    sums = [low, got]
    back, low = run(
        "norm_backward",
        norm_backward,
        back_of,
        at, sum21, back, chip, others, norm_gain[1, 0][None],
        after=[early, lse1],
    )
    got = place.core(low)
    grad_qkv2, keep, send = run(
        "attention_back",
        attention_back,
        inner_of,
        at, low, got, matrix2, qkv2, lse2, pack,
        after=[units2[1], units2[3]],
    )
    units2 = next_stage(units2, after=[send])
    chip, others = quad_sum(keep, send)
    heads2 = run(
        "head_grads",
        head_grads_later,
        head_parts,
        at, low12, got12, grad_qkv2, mixed2, low, got,
        after=[send],
    )
    early = heads2[0]
    heads2 = send_direct(heads2)
    sums = [low, got] + sums
    back, low = run(
        "norm_backward",
        norm_backward,
        back_of,
        at, sum12, back, chip, others, norm_gain[0, 1][None],
        after=[early, *heads2[1:3], units2[1], units2[3]],
    )
    got = place.core(low)
    grad_upper1, keep, send = run(
        "feed_back", feed_back, grad_of, at, low, got, weights1, slope1
    )
    chip, others = quad_sum(keep, send)
    units1 = run(
        "unit_grads",
        unit_grads,
        staged(unit_half),
        at, low11, got11, low, got, activ1, grad_upper1,
        after=[send],
    )
    early = units1[0]
    units1 = send_staged(*units1)
    sums = [low, got] + sums
    back, low = run(
        "norm_backward",
        norm_backward,
        back_of,
        at, sum11, back, chip, others, norm_gain[0, 0][None],
        after=[early, heads2[3]],
    )
    got = place.core(low)
    sums = [low, got] + sums
    later = sum_chips(
        combine_both, (*units2, *heads2), sum(unit_half + head_half), after=[low]
    )
    grad_qkv1, keep, send = run(
        "attention_back",
        attention_back,
        inner_of,
        at, low, got, matrix1, qkv1, lse1, pack,
        after=[later],
    )
    spans = (unit_half, head_half)
    later_got = place.over(later)
    keep_a, over_v, keep_b, over_u = staged(head_half)
    u_a, u_b = (((rows, features), F32) for rows in unit_half)
    over_v, over_u = (
        ((send[0][0] + rows, features), BF) for send, rows in ((over_v, unit_half[1]), (over_u, unit_half[0]))
    )
    keep_a, keep_b, u_a, u_b, over_v, over_u = run(
        "head_grads",
        head_grads_first,
        [keep_a, keep_b, u_a, u_b, over_v, over_u],
        at, pack, grad_qkv1, mixed1, low, got, *sums, *units1,
        scratch=[pltpu.VMEM((8, EXTRA, features), BF), pltpu.SemaphoreType.DMA((8,))],
        hbm=range(6, 14),
        after=[send],
    )
    row_quarter = (quarter, features)
    mine, other = run(
        "tail_one",
        tail_one,
        [(row_quarter, F32), (row_quarter, BF)],
        at, keep, place.core(send), back,
        after=[over_v],
    )
    h_a, for_a, h_b, for_b, units1 = run(
        "combine_joint",
        combine_joint,
        [*one_of(head_half), ((sum(unit_half), features), BF)],
        at, keep_a, keep_b, u_a, u_b, place.chip(over_v, 1), place.chip(over_u, 2),
        after=[mine],
    )
    units_got = place.over(units1)
    rows, both = run(
        "tail_two",
        tail_two,
        [row_quarter_f, ((2, quarter, features), BF)],
        at, mine, place.side(other), final,
        after=[units1],
    )
    both = place.cross(both)
    final_out, input_grad = (
        jnp.where(place.native, own, got.astype(F32)) for own, got in zip((final, rows), both)
    )
    heads1 = sum_chips(
        combine_staged,
        (h_a, place.chip(for_a, 2), h_b, place.chip(for_b, 1)),
        sum(head_half),
        after=[rows],
    )
    later = sum_planes([(later, later_got, spans)], after=[heads1])
    first = sum_planes(
        [(units1, units_got, spans[:1]), (heads1, place.over(heads1), spans[1:])],
        after=later,
    )

    def join(pieces, after):
        return run(
            "join_pieces",
            join_pieces,
            [((len(pieces),) + pieces[0].shape, BF)],
            at, *pieces,
            scratch=[sem],
            hbm=range(1, 5),
            hbm_out=(0,),
            after=after,
        )[0]

    pairs = (layers, 2, features)
    small = [(layers, units), (layers, 2, width), pairs, pairs, pairs]
    *grads, other = unpack(1, (0, 1, 2, 3), join(later, first[:1]), [], after=[both])
    up, down, qkv, out, bup, bqv, bias, gain, shift = unpack(
        0, (0, 1, 2, 3), join(first, [other]), small, [other, jnp.zeros_like(other)], grads
    )
    return (
        final_out,
        input_grad,
        jnp.transpose(qkv.reshape(layers, 3, width, features), (0, 3, 1, 2)),
        bqv,
        out,
        bias,
        gain,
        shift,
        up,
        bup,
        down,
    )


def solution(mesh):
    columns = Mesh(mesh.devices.reshape(-1, 2, 2, 2, mesh.shape["tp"]), AXES)
    rows = P(AXES[:4], None)
    return jax.shard_map(
        on_device,
        mesh=columns,
        in_specs=(
            rows,
            rows,
            rows,
            rows,
            P(None, None, None, "tp"),
            P(None, None, "tp"),
            P(None, "tp", None),
            P(),
            P(),
            P(),
            P(None, None, "tp"),
            P(None, "tp"),
            P(None, "tp", None),
        ),
        out_specs=(
            P(AXES, None),
            P(AXES, None),
            P(None, None, None, "tp"),
            P(None, None, "tp"),
            P(None, "tp", None),
            P(),
            P(),
            P(),
            P(None, None, "tp"),
            P(None, "tp"),
            P(None, "tp", None),
        ),
        check_vma=False,
    )
```

```python
import functools

import jax
import jax.numpy as jnp
from jax import lax
from jax.experimental import pallas as pl
from jax.experimental.pallas import tpu as pltpu
from jax.sharding import Mesh
from jax.sharding import PartitionSpec as P

HEAD_DIM = 64
EPS = 1e-06
NEG = -1e30
EXTRA = 16
AXES = ("far", "u", "v", "c", "tp")
BF = jnp.bfloat16
F32 = jnp.float32
VMEM_BYTES = 24 << 20


class Place:
    def __init__(self):
        self.fars = lax.axis_size("far")
        self.core_no = lax.axis_index("c")
        self.z = lax.axis_index("tp")
        self.native = self.core_no == self.z // 2
        chip = lax.axis_index("u") * 2 + lax.axis_index("v")
        self.vector = jnp.stack(
            [chip, self.core_no, self.z, self.native.astype(jnp.int32)]
        ).astype(jnp.int32)

    def move(self, values, where):
        pairs = []
        for far in range(self.fars):
            for chip in range(4):
                for c in range(2):
                    for z in range(4):
                        to = where(chip, c, z)
                        if to is not None:
                            base = far * 4
                            source = ((base + chip) * 2 + c) * 4 + z
                            target = ((base + to[0]) * 2 + to[1]) * 4 + to[2]
                            pairs.append((source, target))
        return lax.ppermute(values, AXES, pairs)

    def core(self, values):
        return self.move(values, lambda i, c, z: (i, c ^ 1, z))

    def to_foreign(self, values):
        return self.move(values, lambda i, c, z: (i, c ^ 1, z) if c == z // 2 else None)

    def side(self, values):
        return self.move(values, lambda i, c, z: (i, c, z ^ 1))

    def cross(self, values):
        return self.move(values, lambda i, c, z: (i, c ^ 1, z ^ 2) if c != z // 2 else None)

    def over(self, values):
        return self.move(values, lambda i, c, z: (i, c, z ^ 2) if c != z // 2 else None)

    def chip(self, values, k, native=None):
        def where(i, c, z):
            if native is None or native == (c == z // 2):
                return (i ^ k, c, z)
            return None

        return self.move(values, where)

    def add_far(self, values):
        step = 1
        while step < self.fars:
            pairs = []
            for far in range(self.fars):
                pairs += [(far * 32 + i, (far ^ step) * 32 + i) for i in range(32)]
            got = lax.ppermute(values, AXES, pairs)
            values = (values.astype(F32) + got.astype(F32)).astype(values.dtype)
            step *= 2
        return values


class Layer:
    def __init__(self, whole, n):
        self.whole, self.n = whole, n


class Argument:
    def __init__(self, whole):
        self.whole = whole


def run(name, kernel, outs, *args, scratch=(), after=(), hbm=(), hbm_out=(), cost=0):
    n = len(args)

    def body(*refs):
        kernel(*refs[:n], *refs[n + len(after) :])

    anywhere = pl.BlockSpec(memory_space=pl.ANY)
    vmem = pl.BlockSpec(memory_space=pltpu.VMEM)
    in_specs, given = [pl.BlockSpec(memory_space=pltpu.SMEM)], [args[0]]
    for i in range(1, n):
        arg = args[i]
        if isinstance(arg, Layer):
            block = (None,) + arg.whole.shape[1:]
            zeros = (0,) * (arg.whole.ndim - 1)
            in_specs.append(pl.BlockSpec(block, lambda i, at=(arg.n,) + zeros: at))
            given.append(arg.whole)
        else:
            pinned = isinstance(arg, Argument)
            space = pltpu.HBM if pinned else pl.ANY if i in hbm else pltpu.VMEM
            in_specs.append(pl.BlockSpec(memory_space=space))
            given.append(arg.whole if pinned else arg)
    in_specs += [anywhere] * len(after)
    return pl.pallas_call(
        body,
        name=name,
        grid=(1,) if any(isinstance(arg, Layer) for arg in args) else (),
        out_shape=[jax.ShapeDtypeStruct(s, d) for s, d in outs],
        in_specs=in_specs,
        out_specs=[anywhere if i in hbm_out else vmem for i in range(len(outs))],
        scratch_shapes=list(scratch),
        cost_estimate=pl.CostEstimate(
            flops=cost * 10**9, bytes_accessed=0, transcendentals=0
        ),
        compiler_params=pltpu.CompilerParams(vmem_limit_bytes=VMEM_BYTES),
    )(*given, *after)


def dot_nn(a, b):
    return lax.dot_general(a, b, (((1,), (0,)), ((), ())), preferred_element_type=F32)


def dot_nt(a, b):
    return lax.dot_general(a, b, (((1,), (1,)), ((), ())), preferred_element_type=F32)


def dot_tn(a, b):
    return lax.dot_general(a, b, (((0,), (0,)), ((), ())), preferred_element_type=F32)


def thirds(value):
    hi = value.astype(BF).astype(F32)
    mid = (value - hi).astype(BF).astype(F32)
    return hi, mid, value - hi - mid


def extra_rows(rows, columns):
    padded = [
        jnp.concatenate([r, jnp.zeros((1, columns - r.shape[1]), F32)], axis=1)
        if r.shape[1] < columns
        else r
        for r in rows
    ]
    return jnp.concatenate(padded + [jnp.zeros((EXTRA - len(rows), columns), F32)], axis=0)


def multiple(index, size):
    return pl.ds(pl.multiple_of(index * size, size), size)


def bias_rows(place, bias, rows):
    rows[...] = extra_rows(thirds(bias[0:1]), rows.shape[1]).astype(BF)


def copy_all(pairs, sem):
    copies = [pltpu.make_async_copy(a, b, sem.at[i]) for i, (a, b) in enumerate(pairs)]
    for copy in copies:
        copy.start()
    for copy in copies:
        copy.wait()


def pack_units(place, up, down, bias, piece, tail, sem, n, whole):
    rows = up.shape[1] if whole else up.shape[1] // 4
    at = slice(0, rows) if whole else multiple(place[0], rows)
    tail[...] = extra_rows(thirds(bias[n : n + 1]), up.shape[2]).astype(BF)
    copy_all(
        [
            (up.at[n, at], piece.at[0:rows]),
            (down.at[n, at], piece.at[rows : 2 * rows]),
            (tail, piece.at[2 * rows :]),
        ],
        sem,
    )


def head_biases(bias):
    both = jnp.concatenate([bias[0:1], bias[1:2]], axis=1)
    return extra_rows(thirds(both), 4 * bias.shape[1]).astype(BF)


def pack_heads(place, qkv_w, out_w, bias, pack, tail, sem):
    chip = place[0]
    rows, fewer = out_w.shape[1], qkv_w.shape[1] // 4
    inner = qkv_w.shape[1] // rows
    for n in range(2):
        tail[n] = head_biases(bias[n])
    second = rows + EXTRA

    @pl.when(chip < inner)
    def _():
        copy_all([(qkv_w.at[1, multiple(chip, rows)], pack.at[0:rows])], sem)

    @pl.when(chip >= inner)
    def _():
        copy_all([(out_w.at[1], pack.at[0:rows])], sem)

    copy_all(
        [
            (qkv_w.at[0, multiple(chip, fewer)], pack.at[second : second + fewer]),
            (tail.at[1], pack.at[rows:second]),
            (tail.at[0], pack.at[second + fewer :]),
        ],
        sem,
    )


def pack_rows(place, hidden, grad, seg, mask, own, other):
    c = place[1]
    tokens, features = hidden.shape
    half = tokens // 2
    for ref, first in ((own, c), (other, 1 - c)):
        ids = []
        for i, h in enumerate((first, 1 - first)):
            at = multiple(h, half)
            ref[i * half : (i + 1) * half] = hidden[at]
            ids.append(seg[0:1, at])
        at = multiple(first, half)
        scale = seg_column(mask[0:1, at].astype(F32))
        ref[tokens : tokens + half] = (grad[at].astype(F32) * scale).astype(BF)
        ids = jnp.concatenate(ids, axis=1).astype(F32)
        ref[tokens + half :] = extra_rows([ids], features).astype(BF)


def choose_units(place, up, down, bias, *refs, n):
    *pieces, both, bias_out, tail, sem = refs
    chip, native = place[0], place[3]
    rows = up.shape[1] // len(pieces)

    @pl.when(native == 1)
    def _():
        copy_all([(up.at[n], both.at[0]), (down.at[n], both.at[1])], sem)
        bias_out[...] = bias[n : n + 1]

    @pl.when(native == 0)
    def _():
        pairs = [(pieces[0].at[2 * rows :], tail)]
        for k, ref in enumerate(pieces):
            to = slice(0, rows) if len(pieces) == 1 else multiple(chip ^ k, rows)
            for m in range(2):
                pairs.append((ref.at[m * rows : (m + 1) * rows], both.at[m, to]))
        copy_all(pairs, sem)
        parts = tail[...].astype(F32)
        bias_out[...] = parts[0:1] + parts[1:2] + parts[2:3]


def choose_heads(place, qkv_w, out_w, bias, *refs, n):
    *pieces, matrix, bias_out, tail, sem = refs
    chip, native = place[0], place[3]
    width, inner = out_w.shape[1], qkv_w.shape[1]

    @pl.when(native == 1)
    def _():
        copy_all([(qkv_w.at[n], matrix.at[0:inner]), (out_w.at[n], matrix.at[inner:])], sem)
        bias_out[...] = qkv_bias(bias[0:1], bias[1:2])

    @pl.when(native == 0)
    def _():
        start, rows = (0, width) if n else (width + EXTRA, inner // 4)
        pairs = [(pieces[0].at[start + rows : start + rows + EXTRA], tail)]
        for k in range(4):
            pairs.append(
                (pieces[k].at[start : start + rows], matrix.at[multiple(chip ^ k, rows)])
            )
        if n == 0:
            pairs.append((pieces[4], matrix.at[inner:]))
        copy_all(pairs, sem)
        parts = tail[...].astype(F32)
        row = parts[0:1] + parts[1:2] + parts[2:3]
        bias_out[...] = qkv_bias(row[:, :width], row[:, width : 2 * width])


def seg_column(seg_row):
    n = seg_row.shape[1]
    parts = [
        jnp.broadcast_to(seg_row[:, i : i + 128], (128, 128)).T[:, 0:1] for i in range(0, n, 128)
    ]
    return jnp.concatenate(parts, axis=0)


def attend(qkv, seg_row, mixed, lse, tile):
    tokens = qkv.shape[0]
    width = qkv.shape[1] // 3
    heads = width // HEAD_DIM
    column = seg_column(seg_row)
    for start in range(0, tokens, tile):
        same = column[start : start + tile] == seg_row
        outs, logs = [], []
        for head in range(heads):
            at = head * HEAD_DIM
            query = qkv[start : start + tile, at : at + HEAD_DIM] * HEAD_DIM ** (-0.5)
            keys = qkv[:, width + at : width + at + HEAD_DIM]
            values = qkv[:, 2 * width + at : 2 * width + at + HEAD_DIM]
            scores = jnp.where(same, dot_nt(query, keys), NEG)
            top = jnp.max(scores, axis=1, keepdims=True)
            expon = jnp.exp(scores - top)
            total = jnp.sum(expon, axis=1, keepdims=True)
            outs.append(dot_nn(expon.astype(BF), values) / total)
            logs.append(top + jnp.log(total))
        mixed[start : start + tile] = jnp.concatenate(outs, axis=1).astype(BF)
        logs.append(jnp.zeros((tile, lse.shape[1] - heads), F32))
        lse[start : start + tile] = jnp.concatenate(logs, axis=1)


def qkv_bias(bias_q, bias_v):
    return jnp.concatenate([bias_q, jnp.zeros_like(bias_q), bias_v], axis=1)


def attention_home(place, hidden, weight, bias, seg, mixed, ordered, qkv, lse):
    first = place[2] // 2
    tokens = hidden.shape[0]
    half = tokens // 2
    ids = []
    for i, h in enumerate((first, 1 - first)):
        at = multiple(h, half)
        ordered[i * half : (i + 1) * half] = hidden[at]
        ids.append(seg[0:1, at])
    seg_row = jnp.concatenate(ids, axis=1).astype(F32)
    qkv[...] = (dot_nt(ordered[...], weight[...]) + qkv_bias(bias[0:1], bias[1:2])).astype(BF)
    attend(qkv, seg_row, mixed, lse, half)


def put_half(part, keep, send):
    half = part.shape[0] // 2
    keep[...] = part[:half]
    send[...] = part[half:].astype(BF)


def project_first(place, mixed, mixed_got, out_w, out_got, kept, keep, send):
    native = place[3] == 1
    rows = jnp.where(native, out_w[...], out_got[...])
    values = jnp.where(native, mixed[...], mixed_got[...])
    kept[...] = values
    put_half(dot_nn(values, rows), keep, send)


def seg_of(pack, tokens):
    return pack[-EXTRA:].astype(F32)[0:1, :tokens]


def attention_again(place, pack, matrix, bias, qkv, lse, mixed):
    tokens, inner = qkv.shape
    qkv[...] = (dot_nt(pack[:tokens], matrix[:inner]) + bias[...]).astype(BF)
    attend(qkv, seg_of(pack, tokens), mixed, lse, tokens // 2)


def attention_column(place, own, got, matrix, bias, pack, qkv, mixed, lse, keep, send):
    tokens, inner = qkv.shape
    hidden = jnp.concatenate([own[...], got[...]], axis=0)
    qkv[...] = (dot_nt(hidden, matrix[:inner]) + bias[...]).astype(BF)
    attend(qkv, seg_of(pack, tokens), mixed, lse, tokens // 2)
    put_half(dot_nn(mixed[...], matrix[inner:]), keep, send)


def attend_back(qkv, lse, grad_mixed, seg_row, grad_qkv, tile):
    tokens = qkv.shape[0]
    width = qkv.shape[1] // 3
    heads = width // HEAD_DIM
    column = seg_column(seg_row)
    scale = HEAD_DIM ** (-0.5)
    grads = [[], [], []]
    for head in range(heads):
        at = head * HEAD_DIM
        keys = qkv[:, width + at : width + at + HEAD_DIM]
        values = qkv[:, 2 * width + at : 2 * width + at + HEAD_DIM]
        grad_keys = jnp.zeros((tokens, HEAD_DIM), F32)
        grad_values = jnp.zeros((tokens, HEAD_DIM), F32)
        grad_query = []
        for start in range(0, tokens, tile):
            rows = slice(start, start + tile)
            query = qkv[rows, at : at + HEAD_DIM] * scale
            grad_out = grad_mixed[rows, at : at + HEAD_DIM]
            scores = jnp.where(column[rows] == seg_row, dot_nt(query, keys), NEG)
            probs = jnp.exp(scores - lse[rows, head : head + 1])
            grad_probs = dot_nt(grad_out, values)
            inner = jnp.sum(probs * grad_probs, axis=1, keepdims=True)
            grad_scores = (probs * (grad_probs - inner)).astype(BF)
            grad_query.append(dot_nn(grad_scores, keys) * scale)
            grad_keys += dot_tn(grad_scores, query)
            grad_values += dot_tn(probs.astype(BF), grad_out)
        grads[0].append(jnp.concatenate(grad_query, axis=0))
        grads[1].append(grad_keys)
        grads[2].append(grad_values)
    grad_qkv[...] = jnp.concatenate(grads[0] + grads[1] + grads[2], axis=1).astype(BF)


def join_grads(own, got):
    return jnp.concatenate([own[:-EXTRA], got[:-EXTRA]], axis=0)


def attention_back(place, own, got, matrix, qkv, lse, pack, grad_qkv, keep, send):
    tokens, inner = qkv.shape
    grad_att = join_grads(own, got)
    grad_mixed = dot_nt(grad_att, matrix[inner:]).astype(BF)
    attend_back(qkv, lse, grad_mixed, seg_of(pack, tokens), grad_qkv, tokens // 2)
    put_half(dot_nn(grad_qkv[...], matrix[:inner]), keep, send)


def part_rows(whole_a, whole_b, sums, sums_in_b):
    features = whole_a[0].shape[1]
    for p in range(4):
        parts = [whole_a[p], whole_b[p]]
        rows = extra_rows(sums if p == 0 else [], features)
        parts[sums_in_b] = jnp.concatenate([parts[sums_in_b], rows], axis=0)
        yield p, parts[0].astype(BF), parts[1].astype(BF)


def put_direct(place, whole_a, whole_b, sums, *refs):
    for p, a, b in part_rows(whole_a, whole_b, sums, 1):
        part = jnp.concatenate([a, b], axis=0)
        for k, ref in enumerate(refs):

            @pl.when(place[0] ^ p == k)
            def _(ref=ref):
                ref[...] = part


def put_staged(place, whole_a, whole_b, sums, sums_in_b, keep_a, send_a, keep_b, send_b):
    for p, a, b in part_rows(whole_a, whole_b, sums, sums_in_b):
        offset = place[0] ^ p
        over_u, over_v = offset // 2, offset % 2

        @pl.when(over_v == 0)
        def _():
            keep_a[over_u] = a

        @pl.when(over_v == 1)
        def _():
            send_a[multiple(over_u, a.shape[0])] = a

        @pl.when(over_u == 0)
        def _():
            keep_b[over_v] = b

        @pl.when(over_u == 1)
        def _():
            send_b[multiple(over_v, b.shape[0])] = b


def head_grads(hidden, grad_qkv, mixed, a_own, a_got, sums):
    grad_att = join_grads(a_own, a_got)
    whole = jnp.concatenate([dot_tn(grad_qkv[...], hidden), dot_tn(mixed[...], grad_att)], axis=0)
    bias = jnp.sum(grad_qkv[...].astype(F32), axis=0, keepdims=True)
    rows = whole.shape[0] // 4
    cut = rows // 2
    first = [whole[p * rows : p * rows + cut] for p in range(4)]
    second = [whole[p * rows + cut : (p + 1) * rows] for p in range(4)]
    return first, second, [bias] + sums


def head_grads_first(place, pack, grad_qkv, mixed, a_own, a_got, *refs):
    norms, (u_keep_a, u_got_a, u_keep_b, u_got_b) = refs[:8], refs[8:12]
    keep_a, keep_b, mine_a, mine_b, over_v, over_u, rows, sem = refs[12:]
    copy_all([(ref.at[ref.shape[0] - EXTRA :], rows.at[i]) for i, ref in enumerate(norms)], sem)
    total = []
    for i in range(4):
        both = rows[2 * i].astype(F32) + rows[2 * i + 1].astype(F32)
        total += [both[j : j + 1] for j in range(3)]
    hidden = pack[: grad_qkv.shape[0]]
    parts = head_grads(hidden, grad_qkv, mixed, a_own, a_got, total)
    put_staged(place, *parts, 1, keep_a, over_v, keep_b, over_u)
    mine_a[...], over_u[2 * keep_b.shape[1] :] = next_parts(u_keep_a, u_got_a)
    mine_b[...], over_v[2 * keep_a.shape[1] :] = next_parts(u_keep_b, u_got_b)


def head_grads_later(place, own, got, grad_qkv, mixed, a_own, a_got, *parts):
    hidden = jnp.concatenate([own[...], got[...]], axis=0)
    put_direct(place, *head_grads(hidden, grad_qkv, mixed, a_own, a_got, []), *parts)


def feed_forward(place, own, got, weights, bias, activ, slope, keep, send):
    hidden = jnp.concatenate([own[...], got[...]], axis=0)
    upper = dot_nn(hidden, weights[0]) + bias[...]
    cdf = 0.5 * (1.0 + lax.erf(upper * (0.5**0.5)))
    activ[...] = (upper * cdf).astype(BF)
    slope[...] = cdf + upper * jnp.exp(-0.5 * upper * upper) * 0.3989422804014327
    put_half(dot_nn(activ[...], weights[1]), keep, send)


def feed_back(place, own, got, weights, slope, grad_upper, keep, send):
    grad = join_grads(own, got)
    grad_upper[...] = (dot_nt(grad, weights[1]) * slope[...]).astype(BF)
    put_half(dot_nt(grad_upper[...], weights[0]), keep, send)


def unit_grads(place, x_own, x_got, g_own, g_got, activ, grad_upper, *parts):
    hidden = jnp.concatenate([x_own[...], x_got[...]], axis=0)
    grad = join_grads(g_own, g_got)
    up = dot_tn(hidden, grad_upper[...])
    down = dot_tn(activ[...], grad)
    bias = jnp.sum(grad_upper[...].astype(F32), axis=0, keepdims=True)
    rows = up.shape[0] // 4
    first = [up[p * rows : (p + 1) * rows] for p in range(4)]
    second = [down[p * rows : (p + 1) * rows] for p in range(4)]
    put_staged(place, first, second, [bias], 0, *parts)


def chip_sum(place, keep, got, chip, low):
    chip[...] = keep[...] + got[...].astype(F32)
    low[...] = chip[...].astype(BF)


def next_parts(keep, got):
    rows = keep.shape[1]
    mine = keep[0].astype(F32) + got[0:rows].astype(F32)
    return mine, (keep[1].astype(F32) + got[rows : 2 * rows].astype(F32)).astype(BF)


def combine_one(place, keep_a, got_a, keep_b, got_b, mine_a, for_a, mine_b, for_b):
    mine_a[...], for_a[...] = next_parts(keep_a, got_a)
    mine_b[...], for_b[...] = next_parts(keep_b, got_b)


def combine_joint(
    place, keep_a, keep_b, u_a, u_b, got_v, got_u, mine_a, for_a, mine_b, for_b, units
):
    mine_a[...], for_a[...] = next_parts(keep_a, got_v)
    mine_b[...], for_b[...] = next_parts(keep_b, got_u)
    rows = u_a.shape[0]
    units[:rows] = (u_a[...] + got_u[2 * keep_b.shape[1] :].astype(F32)).astype(BF)
    units[rows:] = (u_b[...] + got_v[2 * keep_a.shape[1] :].astype(F32)).astype(BF)


def combine_staged(place, mine_a, got_a, mine_b, got_b, total):
    rows = mine_a.shape[0]
    total[:rows] = (mine_a[...] + got_a[...].astype(F32)).astype(BF)
    total[rows:] = (mine_b[...] + got_b[...].astype(F32)).astype(BF)


def combine_both(place, mine_a, got_a, mine_b, got_b, own, got1, got2, got3, total):
    start = mine_a.shape[0] + mine_b.shape[0]
    combine_staged(place, mine_a, got_a, mine_b, got_b, total.at[0:start])
    terms = [ref[...].astype(F32) for ref in (own, got1, got2, got3)]
    total[start:] = ((terms[0] + terms[1]) + (terms[2] + terms[3])).astype(BF)


def combine_planes(place, *refs, spans):
    *parts, first, second = refs
    at = [0, 0]
    for i, parts_of in enumerate(spans):
        mine, got = parts[2 * i : 2 * i + 2]
        start = 0
        for halves in parts_of:
            for j, (out, rows) in enumerate(zip((first, second), halves)):
                value = mine[start : start + rows].astype(F32) + got[start : start + rows].astype(F32)
                out[at[j] : at[j] + rows] = value.astype(BF)
                start += rows
                at[j] += rows


def tail_one(place, keep, got, back, mine, other):
    s = place[2] % 2
    rows = mine.shape[0]
    at, away = multiple(s, rows), multiple(1 - s, rows)
    mine[...] = keep[at] + got[at].astype(F32) + back[at]
    other[...] = (keep[away] + got[away].astype(F32)).astype(BF)


def tail_two(place, mine, got, final, rows, both):
    rows[...] = mine[...] + got[...].astype(F32)
    both[0] = final[...].astype(BF)
    both[1] = rows[...].astype(BF)


def normalize(values):
    center = values - jnp.mean(values, axis=1, keepdims=True)
    spread = jnp.mean(center * center, axis=1, keepdims=True)
    inv = lax.rsqrt(spread + EPS)
    return center * inv, inv


def norm_forward(place, base, chip, got, bias, gain, shift, total, out, low):
    values = base[...].astype(F32) + (chip[...].astype(BF).astype(F32) + got[...].astype(F32) + bias[...])
    total[...] = values
    unit, _ = normalize(values)
    result = unit * gain[...] + shift[...]
    out[...] = result
    low[...] = result.astype(BF)


def back_through(values, gain, grad):
    unit, inv = normalize(values)
    scaled = grad * gain
    first = jnp.mean(scaled, axis=1, keepdims=True)
    second = jnp.mean(scaled * unit, axis=1, keepdims=True)
    back = inv * (scaled - first - unit * second)
    low = back.astype(BF)
    sums = [
        jnp.sum(low.astype(F32), axis=0, keepdims=True),
        jnp.sum(grad * unit, axis=0, keepdims=True),
        jnp.sum(grad, axis=0, keepdims=True),
    ]
    return back, jnp.concatenate([low, extra_rows(sums, low.shape[1]).astype(BF)], axis=0)


def norm_turn(place, base, chip, got, bias, gain, shift, pack, final, back, low):
    half = base.shape[0]
    quarter = half // 2
    values = base[...] + (chip[...].astype(BF).astype(F32) + got[...].astype(F32) + bias[...])
    unit, _ = normalize(values)
    back[...] = unit * gain[...] + shift[...]
    final[...] = back[multiple(place[2] % 2, quarter)]
    grad = pack[2 * half : 3 * half].astype(F32)
    back[...], low[...] = back_through(values, gain[...], grad)


def norm_backward(place, values, base, chip, got, gain, back, low):
    grad = base[...] + (chip[...].astype(BF).astype(F32) + got[...].astype(F32))
    back[...], low[...] = back_through(values[...], gain[...], grad)


def join_pieces(place, *refs):
    *pieces, mine, sem = refs
    copy_all([(ref, mine.at[k]) for k, ref in enumerate(pieces)], sem)


def unpack_parts(place, *refs, n, ks, smalls, last, unit_half):
    count = len(ks)
    (mine, got), refs = ([ref.at[i] for i in range(count)] for ref in refs[:2]), refs[2:]
    given, refs = refs[:smalls], refs[smalls:]
    up, down, qkv, out, *small, stage, sem = refs[-(7 + 4 * last) :]
    chip, native = place[0], place[3] == 1
    rows = stage.shape[2]
    cut = rows // 2
    copies, sums = [], jnp.zeros((2, EXTRA, stage.shape[3]), F32)
    for i, k in enumerate(ks):
        p = chip ^ k
        a = jnp.where(native, mine[i][...], got[i][...]).astype(F32)
        b = jnp.where(native, got[i][...], mine[i][...]).astype(F32)
        at = multiple(p, rows)
        stage[i, 0] = a[:rows]
        copies.append(pltpu.make_async_copy(stage.at[i, 0], up.at[n, at], sem.at[i, 0]))
        copies[-1].start()
        stage[i, 1] = b[:rows]
        copies.append(pltpu.make_async_copy(stage.at[i, 1], down.at[n, at], sem.at[i, 1]))
        copies[-1].start()
        stage[i, 2, :cut] = a[unit_half[0] :]
        stage[i, 2, cut:] = b[unit_half[1] : unit_half[1] + cut]

        @pl.when(p < 3)
        def _(i=i, at=at):
            pltpu.make_async_copy(stage.at[i, 2], qkv.at[n, at], sem.at[i, 2]).start()

        @pl.when(p == 3)
        def _(i=i):
            pltpu.make_async_copy(stage.at[i, 2], out.at[n], sem.at[i, 2]).start()

        found = jnp.stack([a[rows : unit_half[0]], b[unit_half[1] + cut :]])
        sums = sums + jnp.where(p == 0, found, 0.0)
    if last:
        other, first = given
        sums = sums + first[...]
        bup, bqv, *norms = small
        width = bqv.shape[2]
        for i, (u, h) in enumerate(((sums[0], sums[1]), (other[0], other[1]))):
            bup[i : i + 1] = u[0:1]
            bqv[i, 0:1] = h[0:1, 0:width]
            bqv[i, 1:2] = h[0:1, 2 * width : 3 * width]
            for j in range(2):
                for m, ref in enumerate(norms):
                    row = 1 + (2 * i + j) * 3 + m
                    ref[i, j : j + 1] = sums[1, row : row + 1]
    else:
        small[0][...] = sums
    for copy in copies:
        copy.wait()
    for i, k in enumerate(ks):
        pltpu.make_async_copy(stage.at[i, 2], out.at[n], sem.at[i, 2]).wait()


def on_device(
    hidden_in,
    out_grad,
    segment_ids,
    loss_mask,
    w_qkv,
    b_query_value,
    w_out,
    branch_bias,
    norm_gain,
    norm_shift,
    w_up,
    b_up,
    w_down,
):
    place = Place()
    at = place.vector
    layers, features = w_qkv.shape[:2]
    width = w_qkv.shape[-1]
    inner = 3 * width
    tokens = hidden_in.shape[0]
    half, quarter = tokens // 2, tokens // 4
    units = w_up.shape[-1]
    unit_rows, head_rows = features // 4, (inner + width) // 4
    w_qkv_t = jnp.transpose(w_qkv, (0, 2, 3, 1)).reshape(layers, inner, features)

    def gain_of(n, i):
        return branch_bias[n, i][None], norm_gain[n, i][None], norm_shift[n, i][None]

    half_f = ((half, features), F32)
    half_b = ((half, features), BF)
    half_e = ((half + EXTRA, features), BF)
    unit_piece = ((2 * unit_rows + EXTRA, features), BF)
    head_piece = ((head_rows + EXTRA, features), BF)
    row_quarter_f = ((quarter, features), F32)
    sem = pltpu.SemaphoreType.DMA((9,))
    tail = pltpu.VMEM((EXTRA, features), BF)

    def spread_chips(values):
        return [values] + [place.chip(values, k, native=False) for k in (1, 2, 3)]

    def unit_weights(n, pieces, after=()):
        return run(
            "choose_units",
            functools.partial(choose_units, n=n),
            [((2, units, features), BF), ((1, units), F32)],
            at, Argument(w_up), Argument(w_down), b_up, *pieces,
            scratch=[tail, sem],
            hbm=(1, 2, *range(4, 4 + len(pieces))),
            hbm_out=(0,),
            after=after,
        )

    def unit_pack(n, whole, after=()):
        rows = 2 * (units if whole else unit_rows) + EXTRA
        return run(
            "pack_units",
            functools.partial(pack_units, n=n, whole=whole),
            [((rows, features), BF)],
            at, Argument(w_up), Argument(w_down), b_up,
            scratch=[tail, sem],
            hbm=(1, 2),
            hbm_out=(0,),
            after=after,
        )[0]

    def head_weights(n, pieces, after=()):
        return run(
            "choose_heads",
            functools.partial(choose_heads, n=n),
            [((inner + width, features), BF), ((1, inner), F32)],
            at, Argument(w_qkv_t), Argument(w_out), Layer(b_query_value, n), *pieces,
            scratch=[tail, sem],
            hbm=(1, 2, *range(4, 4 + len(pieces))),
            hbm_out=(0,),
            after=after,
        )

    def quad_sum(keep, send, after=()):
        chip, low = run(
            "chip_sum", chip_sum, [half_f, half_b], at, keep, place.core(send), after=after
        )
        return chip, place.side(low)

    (tail1,) = run("bias_rows", bias_rows, [((EXTRA, features), BF)], at, b_up)
    start = at[0] * unit_rows
    units1 = jnp.concatenate(
        [lax.dynamic_slice(w, (0, start, 0), (1, unit_rows, features))[0] for w in (w_up, w_down)]
        + [tail1]
    )
    early = units1
    out_got = place.cross(w_out[0])
    units1 = place.cross(units1)
    row_pack = ((tokens + half + EXTRA, features), BF)
    pack_own, pack_other = run(
        "pack_rows",
        pack_rows,
        [row_pack, row_pack],
        at, hidden_in, out_grad, segment_ids, loss_mask,
        after=[early],
    )
    (mixed_home,) = run(
        "attention_home",
        attention_home,
        [((tokens, width), BF)],
        at, hidden_in, Layer(w_qkv_t, 0), Layer(b_query_value, 0), segment_ids,
        scratch=[
            pltpu.VMEM((tokens, features), BF),
            pltpu.VMEM((tokens, inner), BF),
            pltpu.VMEM((tokens, 128), F32),
        ],
        after=[pack_own],
        cost=10,
    )
    mixed_got = place.cross(mixed_home)
    pack = jnp.where(place.native, pack_own, place.to_foreign(pack_other))

    head_pack_rows = width + inner // 4 + 2 * EXTRA
    (heads,) = run(
        "pack_heads",
        pack_heads,
        [((head_pack_rows, features), BF)],
        at, Argument(w_qkv_t), Argument(w_out), b_query_value,
        scratch=[pltpu.VMEM((2, EXTRA, features), BF), sem],
        hbm=(1, 2),
        hbm_out=(0,),
        after=[mixed_home, pack],
    )
    heads = place.cross(heads)

    mixed1, keep, send = run(
        "project_first",
        project_first,
        [((tokens, width), BF), half_f, half_b],
        at, mixed_home, mixed_got, Layer(w_out, 0), out_got,
    )
    chip, others = quad_sum(keep, send)
    sum11, norm11, low11 = run(
        "norm_forward",
        norm_forward,
        [half_f, half_f, half_b],
        at, pack[:half], chip, others, *gain_of(0, 0),
        after=[heads],
    )
    got11 = place.core(low11)
    weights1, b_up1 = unit_weights(0, spread_chips(units1), after=[low11])
    ffn_outs = [((tokens, units), BF), ((tokens, units), F32), half_f, half_b]
    activ1, slope1, keep, send = run(
        "feed_forward",
        feed_forward,
        ffn_outs,
        at, low11, got11, weights1, b_up1,
    )
    matrix_of = ((inner + width, features), BF)
    chip, others = quad_sum(keep, send)
    units2 = place.cross(unit_pack(1, False, [chip]))
    sum12, norm12, low12 = run(
        "norm_forward",
        norm_forward,
        [half_f, half_f, half_b],
        at, norm11, chip, others, *gain_of(0, 1),
    )
    got12 = place.core(low12)
    heads = spread_chips(heads)
    matrix2, bias2 = head_weights(1, heads, [low12])
    lse_of = ((tokens, 128), F32)
    qkv2, mixed2, lse2, keep, send = run(
        "attention_column",
        attention_column,
        [((tokens, inner), BF), ((tokens, width), BF), lse_of, half_f, half_b],
        at, low12, got12, matrix2, bias2, pack,
        after=[units2],
    )
    chip, others = quad_sum(keep, send)
    weights2, b_up2 = unit_weights(1, spread_chips(units2))
    sum21, norm21, low21 = run(
        "norm_forward",
        norm_forward,
        [half_f, half_f, half_b],
        at, low12, chip, others, *gain_of(1, 0),
        after=[weights2],
    )
    got21 = place.core(low21)
    activ2, slope2, keep, send = run(
        "feed_forward", feed_forward, ffn_outs, at, low21, got21, weights2, b_up2
    )
    chip, others = quad_sum(keep, send)
    final, back, low = run(
        "norm_turn",
        norm_turn,
        [row_quarter_f, half_f, half_e],
        at, norm21, chip, others, *gain_of(1, 1), pack,
    )

    shapes = [
        (layers, features, units),
        (layers, units, features),
        (layers, inner, features),
        (layers, width, features),
    ]

    def unpack(n, ks, joined, smalls, small=(), earlier=(), after=()):
        sums = [(2, EXTRA, features)]
        given = [joined, place.core(joined), *small]
        vmem = pl.BlockSpec(memory_space=pltpu.VMEM)
        anywhere = pl.BlockSpec(memory_space=pl.ANY)
        return pl.pallas_call(
            functools.partial(
                unpack_parts,
                n=n,
                ks=ks,
                smalls=len(small),
                last=len(smalls) > 0,
                unit_half=unit_half,
            ),
            name="unpack_parts",
            out_shape=[jax.ShapeDtypeStruct(s, F32) for s in shapes + (smalls or sums)],
            in_specs=[pl.BlockSpec(memory_space=pltpu.SMEM)]
            + [vmem] * len(given)
            + [anywhere] * (len(after) + len(earlier)),
            out_specs=[anywhere] * 4 + [vmem] * len(smalls or sums),
            input_output_aliases={
                1 + len(given) + len(after) + i: i for i in range(len(earlier))
            },
            scratch_shapes=[
                pltpu.VMEM((len(ks), 3, unit_rows, features), F32),
                pltpu.SemaphoreType.DMA((len(ks), 3)),
            ],
            cost_estimate=pl.CostEstimate(
                flops=0 if smalls else 4 * 10**10, bytes_accessed=0, transcendentals=0
            ),
            compiler_params=pltpu.CompilerParams(vmem_limit_bytes=VMEM_BYTES),
        )(at, *given, *after, *earlier)

    unit_half = (unit_rows + EXTRA, unit_rows)
    head_half = (head_rows // 2, head_rows // 2 + EXTRA)
    def staged(halves):
        return [
            (shape, BF)
            for rows in halves
            for shape in ((2, rows, features), (2 * rows, features))
        ]

    head_parts = [((sum(head_half), features), BF)] * 4

    def send_direct(parts):
        return [parts[0]] + [place.chip(parts[k], k) for k in (1, 2, 3)]

    def send_staged(keep_a, send_a, keep_b, send_b):
        return keep_a, place.chip(send_a, 1), keep_b, place.chip(send_b, 2)

    def one_of(halves):
        return [((rows, features), kind) for rows in halves for kind in (F32, BF)]

    def next_stage(parts, after=()):
        mine_a, for_a, mine_b, for_b = run(
            "combine_one", combine_one, one_of(unit_half), at, *parts, after=after
        )
        return mine_a, place.chip(for_a, 2), mine_b, place.chip(for_b, 1)

    def sum_chips(kernel, parts, rows, after=()):
        return run(
            kernel.__name__, kernel, [((rows, features), BF)], at, *parts, after=after
        )[0]

    def sum_planes(groups, after=()):
        spans = [group[2] for group in groups]
        rows = sum(halves[0] for parts in spans for halves in parts)
        first, second = run(
            "combine_planes",
            functools.partial(combine_planes, spans=spans),
            [((rows, features), BF)] * 2,
            at, *[part for group in groups for part in group[:2]],
            after=after,
        )
        first, second = place.add_far(first), place.add_far(second)
        piece = jnp.where(place.native, first, place.core(second))
        return [piece] + [place.chip(piece, k) for k in (1, 2, 3)]

    grad_of = [((tokens, units), BF), half_f, half_b]
    back_of = [half_f, half_e]
    inner_of = [((tokens, inner), BF), half_f, half_b]

    got = place.core(low)
    grad_upper2, keep, send = run(
        "feed_back", feed_back, grad_of, at, low, got, weights2, slope2
    )
    chip, others = quad_sum(keep, send)
    units2 = run(
        "unit_grads",
        unit_grads,
        staged(unit_half),
        at, low21, got21, low, got, activ2, grad_upper2,
        after=[chip],
    )
    early = units2[0]
    units2 = send_staged(*units2)
    matrix1, bias1 = head_weights(0, [*heads, out_got], [early])
    qkv1, lse1, _ = run(
        "attention_again",
        attention_again,
        [((tokens, inner), BF), lse_of, ((tokens, width), BF)],
        at, pack, matrix1, bias1,
        after=[matrix1],
    )
    sums = [low, got]
    back, low = run(
        "norm_backward",
        norm_backward,
        back_of,
        at, sum21, back, chip, others, norm_gain[1, 0][None],
        after=[early, lse1],
    )
    got = place.core(low)
    grad_qkv2, keep, send = run(
        "attention_back",
        attention_back,
        inner_of,
        at, low, got, matrix2, qkv2, lse2, pack,
        after=[units2[1], units2[3]],
    )
    units2 = next_stage(units2, after=[send])
    chip, others = quad_sum(keep, send)
    heads2 = run(
        "head_grads",
        head_grads_later,
        head_parts,
        at, low12, got12, grad_qkv2, mixed2, low, got,
        after=[send],
    )
    early = heads2[0]
    heads2 = send_direct(heads2)
    sums = [low, got] + sums
    back, low = run(
        "norm_backward",
        norm_backward,
        back_of,
        at, sum12, back, chip, others, norm_gain[0, 1][None],
        after=[early, units2[1], units2[3]],
    )
    got = place.core(low)
    grad_upper1, keep, send = run(
        "feed_back", feed_back, grad_of, at, low, got, weights1, slope1
    )
    chip, others = quad_sum(keep, send)
    units1 = run(
        "unit_grads",
        unit_grads,
        staged(unit_half),
        at, low11, got11, low, got, activ1, grad_upper1,
        after=[send],
    )
    early = units1[0]
    units1 = send_staged(*units1)
    sums = [low, got] + sums
    back, low = run(
        "norm_backward",
        norm_backward,
        back_of,
        at, sum11, back, chip, others, norm_gain[0, 0][None],
        after=[early, *heads2[1:]],
    )
    got = place.core(low)
    sums = [low, got] + sums
    later = sum_chips(
        combine_both, (*units2, *heads2), sum(unit_half + head_half), after=[low]
    )
    grad_qkv1, keep, send = run(
        "attention_back",
        attention_back,
        inner_of,
        at, low, got, matrix1, qkv1, lse1, pack,
        after=[later],
    )
    spans = (unit_half, head_half)
    later_got = place.over(later)
    keep_a, over_v, keep_b, over_u = staged(head_half)
    u_a, u_b = (((rows, features), F32) for rows in unit_half)
    over_v, over_u = (
        ((send[0][0] + rows, features), BF) for send, rows in ((over_v, unit_half[1]), (over_u, unit_half[0]))
    )
    keep_a, keep_b, u_a, u_b, over_v, over_u = run(
        "head_grads",
        head_grads_first,
        [keep_a, keep_b, u_a, u_b, over_v, over_u],
        at, pack, grad_qkv1, mixed1, low, got, *sums, *units1,
        scratch=[pltpu.VMEM((8, EXTRA, features), BF), pltpu.SemaphoreType.DMA((8,))],
        hbm=range(6, 14),
        after=[send],
    )
    row_quarter = (quarter, features)
    mine, other = run(
        "tail_one",
        tail_one,
        [(row_quarter, F32), (row_quarter, BF)],
        at, keep, place.core(send), back,
        after=[over_v],
    )
    h_a, for_a, h_b, for_b, units1 = run(
        "combine_joint",
        combine_joint,
        [*one_of(head_half), ((sum(unit_half), features), BF)],
        at, keep_a, keep_b, u_a, u_b, place.chip(over_v, 1), place.chip(over_u, 2),
        after=[mine],
    )
    units_got = place.over(units1)
    rows, both = run(
        "tail_two",
        tail_two,
        [row_quarter_f, ((2, quarter, features), BF)],
        at, mine, place.side(other), final,
        after=[units1],
    )
    both = place.cross(both)
    final_out, input_grad = (
        jnp.where(place.native, own, got.astype(F32)) for own, got in zip((final, rows), both)
    )
    heads1 = sum_chips(
        combine_staged,
        (h_a, place.chip(for_a, 2), h_b, place.chip(for_b, 1)),
        sum(head_half),
        after=[rows],
    )
    later = sum_planes([(later, later_got, spans)], after=[units1])
    first = sum_planes(
        [(units1, units_got, spans[:1]), (heads1, place.over(heads1), spans[1:])],
        after=later,
    )

    def join(pieces, after):
        return run(
            "join_pieces",
            join_pieces,
            [((len(pieces),) + pieces[0].shape, BF)],
            at, *pieces,
            scratch=[sem],
            hbm=range(1, 5),
            hbm_out=(0,),
            after=after,
        )[0]

    pairs = (layers, 2, features)
    small = [(layers, units), (layers, 2, width), pairs, pairs, pairs]
    *grads, other = unpack(1, (0, 1, 2, 3), join(later, first[:1]), [])
    up, down, qkv, out, bup, bqv, bias, gain, shift = unpack(
        0, (0, 1, 2, 3), join(first, [other, both]), small, [other, jnp.zeros_like(other)], grads
    )
    return (
        final_out,
        input_grad,
        jnp.transpose(qkv.reshape(layers, 3, width, features), (0, 3, 1, 2)),
        bqv,
        out,
        bias,
        gain,
        shift,
        up,
        bup,
        down,
    )


def solution(mesh):
    columns = Mesh(mesh.devices.reshape(-1, 2, 2, 2, mesh.shape["tp"]), AXES)
    rows = P(AXES[:4], None)
    return jax.shard_map(
        on_device,
        mesh=columns,
        in_specs=(
            rows,
            rows,
            rows,
            rows,
            P(None, None, None, "tp"),
            P(None, None, "tp"),
            P(None, "tp", None),
            P(),
            P(),
            P(),
            P(None, None, "tp"),
            P(None, "tp"),
            P(None, "tp", None),
        ),
        out_specs=(
            P(AXES, None),
            P(AXES, None),
            P(None, None, None, "tp"),
            P(None, None, "tp"),
            P(None, "tp", None),
            P(),
            P(),
            P(),
            P(None, None, "tp"),
            P(None, "tp"),
            P(None, "tp", None),
        ),
        check_vma=False,
    )
```

```python
import functools

import jax
import jax.numpy as jnp
from jax import lax
from jax.experimental import pallas as pl
from jax.experimental.pallas import tpu as pltpu
from jax.sharding import Mesh
from jax.sharding import PartitionSpec as P

HEAD_DIM = 64
EPS = 1e-06
NEG = -1e30
EXTRA = 16
AXES = ("far", "u", "v", "c", "tp")
BF = jnp.bfloat16
F32 = jnp.float32
VMEM_BYTES = 24 << 20


class Place:
    def __init__(self):
        self.fars = lax.axis_size("far")
        self.core_no = lax.axis_index("c")
        self.z = lax.axis_index("tp")
        self.native = self.core_no == self.z // 2
        chip = lax.axis_index("u") * 2 + lax.axis_index("v")
        self.vector = jnp.stack(
            [chip, self.core_no, self.z, self.native.astype(jnp.int32)]
        ).astype(jnp.int32)

    def move(self, values, where):
        pairs = []
        for far in range(self.fars):
            for chip in range(4):
                for c in range(2):
                    for z in range(4):
                        to = where(chip, c, z)
                        if to is not None:
                            base = far * 4
                            source = ((base + chip) * 2 + c) * 4 + z
                            target = ((base + to[0]) * 2 + to[1]) * 4 + to[2]
                            pairs.append((source, target))
        return lax.ppermute(values, AXES, pairs)

    def core(self, values):
        return self.move(values, lambda i, c, z: (i, c ^ 1, z))

    def to_foreign(self, values):
        return self.move(values, lambda i, c, z: (i, c ^ 1, z) if c == z // 2 else None)

    def side(self, values):
        return self.move(values, lambda i, c, z: (i, c, z ^ 1))

    def cross(self, values):
        return self.move(values, lambda i, c, z: (i, c ^ 1, z ^ 2) if c != z // 2 else None)

    def over(self, values):
        return self.move(values, lambda i, c, z: (i, c, z ^ 2) if c != z // 2 else None)

    def chip(self, values, k, native=None):
        def where(i, c, z):
            if native is None or native == (c == z // 2):
                return (i ^ k, c, z)
            return None

        return self.move(values, where)

    def add_far(self, values):
        step = 1
        while step < self.fars:
            pairs = []
            for far in range(self.fars):
                pairs += [(far * 32 + i, (far ^ step) * 32 + i) for i in range(32)]
            got = lax.ppermute(values, AXES, pairs)
            values = (values.astype(F32) + got.astype(F32)).astype(values.dtype)
            step *= 2
        return values


class Layer:
    def __init__(self, whole, n):
        self.whole, self.n = whole, n


class Argument:
    def __init__(self, whole):
        self.whole = whole


def run(name, kernel, outs, *args, scratch=(), after=(), hbm=(), hbm_out=(), cost=0):
    n = len(args)

    def body(*refs):
        kernel(*refs[:n], *refs[n + len(after) :])

    anywhere = pl.BlockSpec(memory_space=pl.ANY)
    vmem = pl.BlockSpec(memory_space=pltpu.VMEM)
    in_specs, given = [pl.BlockSpec(memory_space=pltpu.SMEM)], [args[0]]
    for i in range(1, n):
        arg = args[i]
        if isinstance(arg, Layer):
            block = (None,) + arg.whole.shape[1:]
            zeros = (0,) * (arg.whole.ndim - 1)
            in_specs.append(pl.BlockSpec(block, lambda i, at=(arg.n,) + zeros: at))
            given.append(arg.whole)
        else:
            pinned = isinstance(arg, Argument)
            space = pltpu.HBM if pinned else pl.ANY if i in hbm else pltpu.VMEM
            in_specs.append(pl.BlockSpec(memory_space=space))
            given.append(arg.whole if pinned else arg)
    in_specs += [anywhere] * len(after)
    return pl.pallas_call(
        body,
        name=name,
        grid=(1,) if any(isinstance(arg, Layer) for arg in args) else (),
        out_shape=[jax.ShapeDtypeStruct(s, d) for s, d in outs],
        in_specs=in_specs,
        out_specs=[anywhere if i in hbm_out else vmem for i in range(len(outs))],
        scratch_shapes=list(scratch),
        cost_estimate=pl.CostEstimate(
            flops=cost * 10**9, bytes_accessed=0, transcendentals=0
        ),
        compiler_params=pltpu.CompilerParams(vmem_limit_bytes=VMEM_BYTES),
    )(*given, *after)


def dot_nn(a, b):
    return lax.dot_general(a, b, (((1,), (0,)), ((), ())), preferred_element_type=F32)


def dot_nt(a, b):
    return lax.dot_general(a, b, (((1,), (1,)), ((), ())), preferred_element_type=F32)


def dot_tn(a, b):
    return lax.dot_general(a, b, (((0,), (0,)), ((), ())), preferred_element_type=F32)


def thirds(value):
    hi = value.astype(BF).astype(F32)
    mid = (value - hi).astype(BF).astype(F32)
    return hi, mid, value - hi - mid


def extra_rows(rows, columns):
    padded = [
        jnp.concatenate([r, jnp.zeros((1, columns - r.shape[1]), F32)], axis=1)
        if r.shape[1] < columns
        else r
        for r in rows
    ]
    return jnp.concatenate(padded + [jnp.zeros((EXTRA - len(rows), columns), F32)], axis=0)


def multiple(index, size):
    return pl.ds(pl.multiple_of(index * size, size), size)


def bias_rows(place, bias, rows):
    rows[...] = extra_rows(thirds(bias[0:1]), rows.shape[1]).astype(BF)


def copy_all(pairs, sem):
    copies = [pltpu.make_async_copy(a, b, sem.at[i]) for i, (a, b) in enumerate(pairs)]
    for copy in copies:
        copy.start()
    for copy in copies:
        copy.wait()


def pack_units(place, up, down, bias, piece, tail, sem, n, whole):
    rows = up.shape[1] if whole else up.shape[1] // 4
    at = slice(0, rows) if whole else multiple(place[0], rows)
    tail[...] = extra_rows(thirds(bias[n : n + 1]), up.shape[2]).astype(BF)
    copy_all(
        [
            (up.at[n, at], piece.at[0:rows]),
            (down.at[n, at], piece.at[rows : 2 * rows]),
            (tail, piece.at[2 * rows :]),
        ],
        sem,
    )


def head_biases(bias):
    both = jnp.concatenate([bias[0:1], bias[1:2]], axis=1)
    return extra_rows(thirds(both), 4 * bias.shape[1]).astype(BF)


def pack_heads(place, qkv_w, out_w, bias, pack, tail, sem):
    chip = place[0]
    rows, fewer = out_w.shape[1], qkv_w.shape[1] // 4
    inner = qkv_w.shape[1] // rows
    for n in range(2):
        tail[n] = head_biases(bias[n])
    second = rows + EXTRA

    @pl.when(chip < inner)
    def _():
        copy_all([(qkv_w.at[1, multiple(chip, rows)], pack.at[0:rows])], sem)

    @pl.when(chip >= inner)
    def _():
        copy_all([(out_w.at[1], pack.at[0:rows])], sem)

    copy_all(
        [
            (qkv_w.at[0, multiple(chip, fewer)], pack.at[second : second + fewer]),
            (tail.at[1], pack.at[rows:second]),
            (tail.at[0], pack.at[second + fewer :]),
        ],
        sem,
    )


def pack_rows(place, hidden, grad, seg, mask, own, other):
    c = place[1]
    tokens, features = hidden.shape
    half = tokens // 2
    for ref, first in ((own, c), (other, 1 - c)):
        ids = []
        for i, h in enumerate((first, 1 - first)):
            at = multiple(h, half)
            ref[i * half : (i + 1) * half] = hidden[at]
            ids.append(seg[0:1, at])
        at = multiple(first, half)
        scale = seg_column(mask[0:1, at].astype(F32))
        ref[tokens : tokens + half] = (grad[at].astype(F32) * scale).astype(BF)
        ids = jnp.concatenate(ids, axis=1).astype(F32)
        ref[tokens + half :] = extra_rows([ids], features).astype(BF)


def choose_units(place, up, down, bias, *refs, n):
    *pieces, both, bias_out, tail, sem = refs
    chip, native = place[0], place[3]
    rows = up.shape[1] // len(pieces)

    @pl.when(native == 1)
    def _():
        copy_all([(up.at[n], both.at[0]), (down.at[n], both.at[1])], sem)
        bias_out[...] = bias[n : n + 1]

    @pl.when(native == 0)
    def _():
        pairs = [(pieces[0].at[2 * rows :], tail)]
        for k, ref in enumerate(pieces):
            to = slice(0, rows) if len(pieces) == 1 else multiple(chip ^ k, rows)
            for m in range(2):
                pairs.append((ref.at[m * rows : (m + 1) * rows], both.at[m, to]))
        copy_all(pairs, sem)
        parts = tail[...].astype(F32)
        bias_out[...] = parts[0:1] + parts[1:2] + parts[2:3]


def choose_heads(place, qkv_w, out_w, bias, *refs, n):
    *pieces, matrix, bias_out, tail, sem = refs
    chip, native = place[0], place[3]
    width, inner = out_w.shape[1], qkv_w.shape[1]

    @pl.when(native == 1)
    def _():
        copy_all([(qkv_w.at[n], matrix.at[0:inner]), (out_w.at[n], matrix.at[inner:])], sem)
        bias_out[...] = qkv_bias(bias[0:1], bias[1:2])

    @pl.when(native == 0)
    def _():
        start, rows = (0, width) if n else (width + EXTRA, inner // 4)
        pairs = [(pieces[0].at[start + rows : start + rows + EXTRA], tail)]
        for k in range(4):
            pairs.append(
                (pieces[k].at[start : start + rows], matrix.at[multiple(chip ^ k, rows)])
            )
        if n == 0:
            pairs.append((pieces[4], matrix.at[inner:]))
        copy_all(pairs, sem)
        parts = tail[...].astype(F32)
        row = parts[0:1] + parts[1:2] + parts[2:3]
        bias_out[...] = qkv_bias(row[:, :width], row[:, width : 2 * width])


def seg_column(seg_row):
    n = seg_row.shape[1]
    parts = [
        jnp.broadcast_to(seg_row[:, i : i + 128], (128, 128)).T[:, 0:1] for i in range(0, n, 128)
    ]
    return jnp.concatenate(parts, axis=0)


def attend(qkv, seg_row, mixed, lse, tile):
    tokens = qkv.shape[0]
    width = qkv.shape[1] // 3
    heads = width // HEAD_DIM
    column = seg_column(seg_row)
    for start in range(0, tokens, tile):
        same = column[start : start + tile] == seg_row
        outs, logs = [], []
        for head in range(heads):
            at = head * HEAD_DIM
            query = qkv[start : start + tile, at : at + HEAD_DIM] * HEAD_DIM ** (-0.5)
            keys = qkv[:, width + at : width + at + HEAD_DIM]
            values = qkv[:, 2 * width + at : 2 * width + at + HEAD_DIM]
            scores = jnp.where(same, dot_nt(query, keys), NEG)
            top = jnp.max(scores, axis=1, keepdims=True)
            expon = jnp.exp(scores - top)
            total = jnp.sum(expon, axis=1, keepdims=True)
            outs.append(dot_nn(expon.astype(BF), values) / total)
            logs.append(top + jnp.log(total))
        mixed[start : start + tile] = jnp.concatenate(outs, axis=1).astype(BF)
        logs.append(jnp.zeros((tile, lse.shape[1] - heads), F32))
        lse[start : start + tile] = jnp.concatenate(logs, axis=1)


def qkv_bias(bias_q, bias_v):
    return jnp.concatenate([bias_q, jnp.zeros_like(bias_q), bias_v], axis=1)


def attention_home(place, hidden, weight, bias, seg, mixed, ordered, qkv, lse):
    first = place[2] // 2
    tokens = hidden.shape[0]
    half = tokens // 2
    ids = []
    for i, h in enumerate((first, 1 - first)):
        at = multiple(h, half)
        ordered[i * half : (i + 1) * half] = hidden[at]
        ids.append(seg[0:1, at])
    seg_row = jnp.concatenate(ids, axis=1).astype(F32)
    qkv[...] = (dot_nt(ordered[...], weight[...]) + qkv_bias(bias[0:1], bias[1:2])).astype(BF)
    attend(qkv, seg_row, mixed, lse, half)


def put_half(part, keep, send):
    half = part.shape[0] // 2
    keep[...] = part[:half]
    send[...] = part[half:].astype(BF)


def project_first(place, mixed, mixed_got, out_w, out_got, kept, keep, send):
    native = place[3] == 1
    rows = jnp.where(native, out_w[...], out_got[...])
    values = jnp.where(native, mixed[...], mixed_got[...])
    kept[...] = values
    put_half(dot_nn(values, rows), keep, send)


def seg_of(pack, tokens):
    return pack[-EXTRA:].astype(F32)[0:1, :tokens]


def attention_again(place, pack, matrix, bias, qkv, lse, mixed):
    tokens, inner = qkv.shape
    qkv[...] = (dot_nt(pack[:tokens], matrix[:inner]) + bias[...]).astype(BF)
    attend(qkv, seg_of(pack, tokens), mixed, lse, tokens // 2)


def attention_column(place, own, got, matrix, bias, pack, qkv, mixed, lse, keep, send):
    tokens, inner = qkv.shape
    hidden = jnp.concatenate([own[...], got[...]], axis=0)
    qkv[...] = (dot_nt(hidden, matrix[:inner]) + bias[...]).astype(BF)
    attend(qkv, seg_of(pack, tokens), mixed, lse, tokens // 2)
    put_half(dot_nn(mixed[...], matrix[inner:]), keep, send)


def attend_back(qkv, lse, grad_mixed, seg_row, grad_qkv, tile):
    tokens = qkv.shape[0]
    width = qkv.shape[1] // 3
    heads = width // HEAD_DIM
    column = seg_column(seg_row)
    scale = HEAD_DIM ** (-0.5)
    grads = [[], [], []]
    for head in range(heads):
        at = head * HEAD_DIM
        keys = qkv[:, width + at : width + at + HEAD_DIM]
        values = qkv[:, 2 * width + at : 2 * width + at + HEAD_DIM]
        grad_keys = jnp.zeros((tokens, HEAD_DIM), F32)
        grad_values = jnp.zeros((tokens, HEAD_DIM), F32)
        grad_query = []
        for start in range(0, tokens, tile):
            rows = slice(start, start + tile)
            query = qkv[rows, at : at + HEAD_DIM] * scale
            grad_out = grad_mixed[rows, at : at + HEAD_DIM]
            scores = jnp.where(column[rows] == seg_row, dot_nt(query, keys), NEG)
            probs = jnp.exp(scores - lse[rows, head : head + 1])
            grad_probs = dot_nt(grad_out, values)
            inner = jnp.sum(probs * grad_probs, axis=1, keepdims=True)
            grad_scores = (probs * (grad_probs - inner)).astype(BF)
            grad_query.append(dot_nn(grad_scores, keys) * scale)
            grad_keys += dot_tn(grad_scores, query)
            grad_values += dot_tn(probs.astype(BF), grad_out)
        grads[0].append(jnp.concatenate(grad_query, axis=0))
        grads[1].append(grad_keys)
        grads[2].append(grad_values)
    grad_qkv[...] = jnp.concatenate(grads[0] + grads[1] + grads[2], axis=1).astype(BF)


def join_grads(own, got):
    return jnp.concatenate([own[:-EXTRA], got[:-EXTRA]], axis=0)


def attention_back(place, own, got, matrix, qkv, lse, pack, grad_qkv, keep, send):
    tokens, inner = qkv.shape
    grad_att = join_grads(own, got)
    grad_mixed = dot_nt(grad_att, matrix[inner:]).astype(BF)
    attend_back(qkv, lse, grad_mixed, seg_of(pack, tokens), grad_qkv, tokens)
    put_half(dot_nn(grad_qkv[...], matrix[:inner]), keep, send)


def part_rows(whole_a, whole_b, sums, sums_in_b):
    features = whole_a[0].shape[1]
    for p in range(4):
        parts = [whole_a[p], whole_b[p]]
        rows = extra_rows(sums if p == 0 else [], features)
        parts[sums_in_b] = jnp.concatenate([parts[sums_in_b], rows], axis=0)
        yield p, parts[0].astype(BF), parts[1].astype(BF)


def put_direct(place, whole_a, whole_b, sums, *refs):
    for p, a, b in part_rows(whole_a, whole_b, sums, 1):
        part = jnp.concatenate([a, b], axis=0)
        for k, ref in enumerate(refs):

            @pl.when(place[0] ^ p == k)
            def _(ref=ref):
                ref[...] = part


def put_staged(place, whole_a, whole_b, sums, sums_in_b, keep_a, send_a, keep_b, send_b):
    for p, a, b in part_rows(whole_a, whole_b, sums, sums_in_b):
        offset = place[0] ^ p
        over_u, over_v = offset // 2, offset % 2

        @pl.when(over_v == 0)
        def _():
            keep_a[over_u] = a

        @pl.when(over_v == 1)
        def _():
            send_a[multiple(over_u, a.shape[0])] = a

        @pl.when(over_u == 0)
        def _():
            keep_b[over_v] = b

        @pl.when(over_u == 1)
        def _():
            send_b[multiple(over_v, b.shape[0])] = b


def head_grads(hidden, grad_qkv, mixed, a_own, a_got, sums):
    grad_att = join_grads(a_own, a_got)
    whole = jnp.concatenate([dot_tn(grad_qkv[...], hidden), dot_tn(mixed[...], grad_att)], axis=0)
    bias = jnp.sum(grad_qkv[...].astype(F32), axis=0, keepdims=True)
    rows = whole.shape[0] // 4
    cut = rows // 2
    first = [whole[p * rows : p * rows + cut] for p in range(4)]
    second = [whole[p * rows + cut : (p + 1) * rows] for p in range(4)]
    return first, second, [bias] + sums


def head_grads_first(place, pack, grad_qkv, mixed, a_own, a_got, *refs):
    norms, (u_keep_a, u_got_a, u_keep_b, u_got_b) = refs[:8], refs[8:12]
    keep_a, keep_b, mine_a, mine_b, over_v, over_u, rows, sem = refs[12:]
    copy_all([(ref.at[ref.shape[0] - EXTRA :], rows.at[i]) for i, ref in enumerate(norms)], sem)
    total = []
    for i in range(4):
        both = rows[2 * i].astype(F32) + rows[2 * i + 1].astype(F32)
        total += [both[j : j + 1] for j in range(3)]
    hidden = pack[: grad_qkv.shape[0]]
    parts = head_grads(hidden, grad_qkv, mixed, a_own, a_got, total)
    put_staged(place, *parts, 1, keep_a, over_v, keep_b, over_u)
    mine_a[...], over_u[2 * keep_b.shape[1] :] = next_parts(u_keep_a, u_got_a)
    mine_b[...], over_v[2 * keep_a.shape[1] :] = next_parts(u_keep_b, u_got_b)


def head_grads_later(place, own, got, grad_qkv, mixed, a_own, a_got, *parts):
    hidden = jnp.concatenate([own[...], got[...]], axis=0)
    put_direct(place, *head_grads(hidden, grad_qkv, mixed, a_own, a_got, []), *parts)


def feed_forward(place, own, got, weights, bias, activ, slope, keep, send):
    hidden = jnp.concatenate([own[...], got[...]], axis=0)
    upper = dot_nn(hidden, weights[0]) + bias[...]
    cdf = 0.5 * (1.0 + lax.erf(upper * (0.5**0.5)))
    activ[...] = (upper * cdf).astype(BF)
    slope[...] = cdf + upper * jnp.exp(-0.5 * upper * upper) * 0.3989422804014327
    put_half(dot_nn(activ[...], weights[1]), keep, send)


def feed_back(place, own, got, weights, slope, grad_upper, keep, send):
    grad = join_grads(own, got)
    grad_upper[...] = (dot_nt(grad, weights[1]) * slope[...]).astype(BF)
    put_half(dot_nt(grad_upper[...], weights[0]), keep, send)


def unit_grads(place, x_own, x_got, g_own, g_got, activ, grad_upper, *parts):
    hidden = jnp.concatenate([x_own[...], x_got[...]], axis=0)
    grad = join_grads(g_own, g_got)
    up = dot_tn(hidden, grad_upper[...])
    down = dot_tn(activ[...], grad)
    bias = jnp.sum(grad_upper[...].astype(F32), axis=0, keepdims=True)
    rows = up.shape[0] // 4
    first = [up[p * rows : (p + 1) * rows] for p in range(4)]
    second = [down[p * rows : (p + 1) * rows] for p in range(4)]
    put_staged(place, first, second, [bias], 0, *parts)


def chip_sum(place, keep, got, chip, low):
    chip[...] = keep[...] + got[...].astype(F32)
    low[...] = chip[...].astype(BF)


def next_parts(keep, got):
    rows = keep.shape[1]
    mine = keep[0].astype(F32) + got[0:rows].astype(F32)
    return mine, (keep[1].astype(F32) + got[rows : 2 * rows].astype(F32)).astype(BF)


def combine_one(place, keep_a, got_a, keep_b, got_b, mine_a, for_a, mine_b, for_b):
    mine_a[...], for_a[...] = next_parts(keep_a, got_a)
    mine_b[...], for_b[...] = next_parts(keep_b, got_b)


def combine_joint(
    place, keep_a, keep_b, u_a, u_b, got_v, got_u, mine_a, for_a, mine_b, for_b, units
):
    mine_a[...], for_a[...] = next_parts(keep_a, got_v)
    mine_b[...], for_b[...] = next_parts(keep_b, got_u)
    rows = u_a.shape[0]
    units[:rows] = (u_a[...] + got_u[2 * keep_b.shape[1] :].astype(F32)).astype(BF)
    units[rows:] = (u_b[...] + got_v[2 * keep_a.shape[1] :].astype(F32)).astype(BF)


def combine_staged(place, mine_a, got_a, mine_b, got_b, total):
    rows = mine_a.shape[0]
    total[:rows] = (mine_a[...] + got_a[...].astype(F32)).astype(BF)
    total[rows:] = (mine_b[...] + got_b[...].astype(F32)).astype(BF)


def combine_both(place, mine_a, got_a, mine_b, got_b, own, got1, got2, got3, total):
    start = mine_a.shape[0] + mine_b.shape[0]
    combine_staged(place, mine_a, got_a, mine_b, got_b, total.at[0:start])
    terms = [ref[...].astype(F32) for ref in (own, got1, got2, got3)]
    total[start:] = ((terms[0] + terms[1]) + (terms[2] + terms[3])).astype(BF)


def combine_planes(place, *refs, spans):
    *parts, first, second = refs
    at = [0, 0]
    for i, parts_of in enumerate(spans):
        mine, got = parts[2 * i : 2 * i + 2]
        start = 0
        for halves in parts_of:
            for j, (out, rows) in enumerate(zip((first, second), halves)):
                value = mine[start : start + rows].astype(F32) + got[start : start + rows].astype(F32)
                out[at[j] : at[j] + rows] = value.astype(BF)
                start += rows
                at[j] += rows


def tail_one(place, keep, got, back, mine, other):
    s = place[2] % 2
    rows = mine.shape[0]
    at, away = multiple(s, rows), multiple(1 - s, rows)
    mine[...] = keep[at] + got[at].astype(F32) + back[at]
    other[...] = (keep[away] + got[away].astype(F32)).astype(BF)


def tail_two(place, mine, got, final, rows, both):
    rows[...] = mine[...] + got[...].astype(F32)
    both[0] = final[...].astype(BF)
    both[1] = rows[...].astype(BF)


def normalize(values):
    center = values - jnp.mean(values, axis=1, keepdims=True)
    spread = jnp.mean(center * center, axis=1, keepdims=True)
    inv = lax.rsqrt(spread + EPS)
    return center * inv, inv


def norm_forward(place, base, chip, got, bias, gain, shift, total, out, low):
    values = base[...].astype(F32) + (chip[...].astype(BF).astype(F32) + got[...].astype(F32) + bias[...])
    total[...] = values
    unit, _ = normalize(values)
    result = unit * gain[...] + shift[...]
    out[...] = result
    low[...] = result.astype(BF)


def back_through(values, gain, grad):
    unit, inv = normalize(values)
    scaled = grad * gain
    first = jnp.mean(scaled, axis=1, keepdims=True)
    second = jnp.mean(scaled * unit, axis=1, keepdims=True)
    back = inv * (scaled - first - unit * second)
    low = back.astype(BF)
    sums = [
        jnp.sum(low.astype(F32), axis=0, keepdims=True),
        jnp.sum(grad * unit, axis=0, keepdims=True),
        jnp.sum(grad, axis=0, keepdims=True),
    ]
    return back, jnp.concatenate([low, extra_rows(sums, low.shape[1]).astype(BF)], axis=0)


def norm_turn(place, base, chip, got, bias, gain, shift, pack, final, back, low):
    half = base.shape[0]
    quarter = half // 2
    values = base[...] + (chip[...].astype(BF).astype(F32) + got[...].astype(F32) + bias[...])
    unit, _ = normalize(values)
    back[...] = unit * gain[...] + shift[...]
    final[...] = back[multiple(place[2] % 2, quarter)]
    grad = pack[2 * half : 3 * half].astype(F32)
    back[...], low[...] = back_through(values, gain[...], grad)


def norm_backward(place, values, base, chip, got, gain, back, low):
    grad = base[...] + (chip[...].astype(BF).astype(F32) + got[...].astype(F32))
    back[...], low[...] = back_through(values[...], gain[...], grad)


def join_pieces(place, *refs):
    *pieces, mine, sem = refs
    copy_all([(ref, mine.at[k]) for k, ref in enumerate(pieces)], sem)


def unpack_parts(place, *refs, n, ks, smalls, last, unit_half):
    count = len(ks)
    (mine, got), refs = ([ref.at[i] for i in range(count)] for ref in refs[:2]), refs[2:]
    given, refs = refs[:smalls], refs[smalls:]
    up, down, qkv, out, *small, stage, sem = refs[-(7 + 4 * last) :]
    chip, native = place[0], place[3] == 1
    rows = stage.shape[2]
    cut = rows // 2
    copies, sums = [], jnp.zeros((2, EXTRA, stage.shape[3]), F32)
    for i, k in enumerate(ks):
        p = chip ^ k
        a = jnp.where(native, mine[i][...], got[i][...]).astype(F32)
        b = jnp.where(native, got[i][...], mine[i][...]).astype(F32)
        at = multiple(p, rows)
        stage[i, 0] = a[:rows]
        copies.append(pltpu.make_async_copy(stage.at[i, 0], up.at[n, at], sem.at[i, 0]))
        copies[-1].start()
        stage[i, 1] = b[:rows]
        copies.append(pltpu.make_async_copy(stage.at[i, 1], down.at[n, at], sem.at[i, 1]))
        copies[-1].start()
        stage[i, 2, :cut] = a[unit_half[0] :]
        stage[i, 2, cut:] = b[unit_half[1] : unit_half[1] + cut]

        @pl.when(p < 3)
        def _(i=i, at=at):
            pltpu.make_async_copy(stage.at[i, 2], qkv.at[n, at], sem.at[i, 2]).start()

        @pl.when(p == 3)
        def _(i=i):
            pltpu.make_async_copy(stage.at[i, 2], out.at[n], sem.at[i, 2]).start()

        found = jnp.stack([a[rows : unit_half[0]], b[unit_half[1] + cut :]])
        sums = sums + jnp.where(p == 0, found, 0.0)
    if last:
        other, first = given
        sums = sums + first[...]
        bup, bqv, *norms = small
        width = bqv.shape[2]
        for i, (u, h) in enumerate(((sums[0], sums[1]), (other[0], other[1]))):
            bup[i : i + 1] = u[0:1]
            bqv[i, 0:1] = h[0:1, 0:width]
            bqv[i, 1:2] = h[0:1, 2 * width : 3 * width]
            for j in range(2):
                for m, ref in enumerate(norms):
                    row = 1 + (2 * i + j) * 3 + m
                    ref[i, j : j + 1] = sums[1, row : row + 1]
    else:
        small[0][...] = sums
    for copy in copies:
        copy.wait()
    for i, k in enumerate(ks):
        pltpu.make_async_copy(stage.at[i, 2], out.at[n], sem.at[i, 2]).wait()


def on_device(
    hidden_in,
    out_grad,
    segment_ids,
    loss_mask,
    w_qkv,
    b_query_value,
    w_out,
    branch_bias,
    norm_gain,
    norm_shift,
    w_up,
    b_up,
    w_down,
):
    place = Place()
    at = place.vector
    layers, features = w_qkv.shape[:2]
    width = w_qkv.shape[-1]
    inner = 3 * width
    tokens = hidden_in.shape[0]
    half, quarter = tokens // 2, tokens // 4
    units = w_up.shape[-1]
    unit_rows, head_rows = features // 4, (inner + width) // 4
    w_qkv_t = jnp.transpose(w_qkv, (0, 2, 3, 1)).reshape(layers, inner, features)

    def gain_of(n, i):
        return branch_bias[n, i][None], norm_gain[n, i][None], norm_shift[n, i][None]

    half_f = ((half, features), F32)
    half_b = ((half, features), BF)
    half_e = ((half + EXTRA, features), BF)
    unit_piece = ((2 * unit_rows + EXTRA, features), BF)
    head_piece = ((head_rows + EXTRA, features), BF)
    row_quarter_f = ((quarter, features), F32)
    sem = pltpu.SemaphoreType.DMA((9,))
    tail = pltpu.VMEM((EXTRA, features), BF)

    def spread_chips(values):
        return [values] + [place.chip(values, k, native=False) for k in (1, 2, 3)]

    def unit_weights(n, pieces, after=()):
        return run(
            "choose_units",
            functools.partial(choose_units, n=n),
            [((2, units, features), BF), ((1, units), F32)],
            at, Argument(w_up), Argument(w_down), b_up, *pieces,
            scratch=[tail, sem],
            hbm=(1, 2, *range(4, 4 + len(pieces))),
            hbm_out=(0,),
            after=after,
        )

    def unit_pack(n, whole, after=()):
        rows = 2 * (units if whole else unit_rows) + EXTRA
        return run(
            "pack_units",
            functools.partial(pack_units, n=n, whole=whole),
            [((rows, features), BF)],
            at, Argument(w_up), Argument(w_down), b_up,
            scratch=[tail, sem],
            hbm=(1, 2),
            hbm_out=(0,),
            after=after,
        )[0]

    def head_weights(n, pieces, after=()):
        return run(
            "choose_heads",
            functools.partial(choose_heads, n=n),
            [((inner + width, features), BF), ((1, inner), F32)],
            at, Argument(w_qkv_t), Argument(w_out), Layer(b_query_value, n), *pieces,
            scratch=[tail, sem],
            hbm=(1, 2, *range(4, 4 + len(pieces))),
            hbm_out=(0,),
            after=after,
        )

    def quad_sum(keep, send, after=()):
        chip, low = run(
            "chip_sum", chip_sum, [half_f, half_b], at, keep, place.core(send), after=after
        )
        return chip, place.side(low)

    (tail1,) = run("bias_rows", bias_rows, [((EXTRA, features), BF)], at, b_up)
    start = at[0] * unit_rows
    units1 = jnp.concatenate(
        [lax.dynamic_slice(w, (0, start, 0), (1, unit_rows, features))[0] for w in (w_up, w_down)]
        + [tail1]
    )
    early = units1
    out_got = place.cross(w_out[0])
    units1 = place.cross(units1)
    row_pack = ((tokens + half + EXTRA, features), BF)
    pack_own, pack_other = run(
        "pack_rows",
        pack_rows,
        [row_pack, row_pack],
        at, hidden_in, out_grad, segment_ids, loss_mask,
        after=[early],
    )
    (mixed_home,) = run(
        "attention_home",
        attention_home,
        [((tokens, width), BF)],
        at, hidden_in, Layer(w_qkv_t, 0), Layer(b_query_value, 0), segment_ids,
        scratch=[
            pltpu.VMEM((tokens, features), BF),
            pltpu.VMEM((tokens, inner), BF),
            pltpu.VMEM((tokens, 128), F32),
        ],
        after=[pack_own],
        cost=10,
    )
    mixed_got = place.cross(mixed_home)
    pack = jnp.where(place.native, pack_own, place.to_foreign(pack_other))

    head_pack_rows = width + inner // 4 + 2 * EXTRA
    (heads,) = run(
        "pack_heads",
        pack_heads,
        [((head_pack_rows, features), BF)],
        at, Argument(w_qkv_t), Argument(w_out), b_query_value,
        scratch=[pltpu.VMEM((2, EXTRA, features), BF), sem],
        hbm=(1, 2),
        hbm_out=(0,),
        after=[mixed_home, pack],
    )
    heads = place.cross(heads)

    mixed1, keep, send = run(
        "project_first",
        project_first,
        [((tokens, width), BF), half_f, half_b],
        at, mixed_home, mixed_got, Layer(w_out, 0), out_got,
    )
    chip, others = quad_sum(keep, send)
    sum11, norm11, low11 = run(
        "norm_forward",
        norm_forward,
        [half_f, half_f, half_b],
        at, pack[:half], chip, others, *gain_of(0, 0),
        after=[heads],
    )
    got11 = place.core(low11)
    weights1, b_up1 = unit_weights(0, spread_chips(units1), after=[low11])
    ffn_outs = [((tokens, units), BF), ((tokens, units), F32), half_f, half_b]
    activ1, slope1, keep, send = run(
        "feed_forward",
        feed_forward,
        ffn_outs,
        at, low11, got11, weights1, b_up1,
    )
    matrix_of = ((inner + width, features), BF)
    chip, others = quad_sum(keep, send)
    units2 = place.cross(unit_pack(1, False, [chip]))
    sum12, norm12, low12 = run(
        "norm_forward",
        norm_forward,
        [half_f, half_f, half_b],
        at, norm11, chip, others, *gain_of(0, 1),
    )
    got12 = place.core(low12)
    heads = spread_chips(heads)
    matrix2, bias2 = head_weights(1, heads, [low12])
    lse_of = ((tokens, 128), F32)
    qkv2, mixed2, lse2, keep, send = run(
        "attention_column",
        attention_column,
        [((tokens, inner), BF), ((tokens, width), BF), lse_of, half_f, half_b],
        at, low12, got12, matrix2, bias2, pack,
        after=[units2],
    )
    chip, others = quad_sum(keep, send)
    weights2, b_up2 = unit_weights(1, spread_chips(units2))
    sum21, norm21, low21 = run(
        "norm_forward",
        norm_forward,
        [half_f, half_f, half_b],
        at, low12, chip, others, *gain_of(1, 0),
        after=[weights2],
    )
    got21 = place.core(low21)
    activ2, slope2, keep, send = run(
        "feed_forward", feed_forward, ffn_outs, at, low21, got21, weights2, b_up2
    )
    chip, others = quad_sum(keep, send)
    final, back, low = run(
        "norm_turn",
        norm_turn,
        [row_quarter_f, half_f, half_e],
        at, norm21, chip, others, *gain_of(1, 1), pack,
    )

    shapes = [
        (layers, features, units),
        (layers, units, features),
        (layers, inner, features),
        (layers, width, features),
    ]

    def unpack(n, ks, joined, smalls, small=(), earlier=(), after=()):
        sums = [(2, EXTRA, features)]
        given = [joined, place.core(joined), *small]
        vmem = pl.BlockSpec(memory_space=pltpu.VMEM)
        anywhere = pl.BlockSpec(memory_space=pl.ANY)
        return pl.pallas_call(
            functools.partial(
                unpack_parts,
                n=n,
                ks=ks,
                smalls=len(small),
                last=len(smalls) > 0,
                unit_half=unit_half,
            ),
            name="unpack_parts",
            out_shape=[jax.ShapeDtypeStruct(s, F32) for s in shapes + (smalls or sums)],
            in_specs=[pl.BlockSpec(memory_space=pltpu.SMEM)]
            + [vmem] * len(given)
            + [anywhere] * (len(after) + len(earlier)),
            out_specs=[anywhere] * 4 + [vmem] * len(smalls or sums),
            input_output_aliases={
                1 + len(given) + len(after) + i: i for i in range(len(earlier))
            },
            scratch_shapes=[
                pltpu.VMEM((len(ks), 3, unit_rows, features), F32),
                pltpu.SemaphoreType.DMA((len(ks), 3)),
            ],
            cost_estimate=pl.CostEstimate(
                flops=0 if smalls else 4 * 10**10, bytes_accessed=0, transcendentals=0
            ),
            compiler_params=pltpu.CompilerParams(vmem_limit_bytes=VMEM_BYTES),
        )(at, *given, *after, *earlier)

    unit_half = (unit_rows + EXTRA, unit_rows)
    head_half = (head_rows // 2, head_rows // 2 + EXTRA)
    def staged(halves):
        return [
            (shape, BF)
            for rows in halves
            for shape in ((2, rows, features), (2 * rows, features))
        ]

    head_parts = [((sum(head_half), features), BF)] * 4

    def send_direct(parts):
        return [parts[0]] + [place.chip(parts[k], k) for k in (1, 2, 3)]

    def send_staged(keep_a, send_a, keep_b, send_b):
        return keep_a, place.chip(send_a, 1), keep_b, place.chip(send_b, 2)

    def one_of(halves):
        return [((rows, features), kind) for rows in halves for kind in (F32, BF)]

    def next_stage(parts, after=()):
        mine_a, for_a, mine_b, for_b = run(
            "combine_one", combine_one, one_of(unit_half), at, *parts, after=after
        )
        return mine_a, place.chip(for_a, 2), mine_b, place.chip(for_b, 1)

    def sum_chips(kernel, parts, rows, after=()):
        return run(
            kernel.__name__, kernel, [((rows, features), BF)], at, *parts, after=after
        )[0]

    def sum_planes(groups, after=()):
        spans = [group[2] for group in groups]
        rows = sum(halves[0] for parts in spans for halves in parts)
        first, second = run(
            "combine_planes",
            functools.partial(combine_planes, spans=spans),
            [((rows, features), BF)] * 2,
            at, *[part for group in groups for part in group[:2]],
            after=after,
        )
        first, second = place.add_far(first), place.add_far(second)
        piece = jnp.where(place.native, first, place.core(second))
        return [piece] + [place.chip(piece, k) for k in (1, 2, 3)]

    grad_of = [((tokens, units), BF), half_f, half_b]
    back_of = [half_f, half_e]
    inner_of = [((tokens, inner), BF), half_f, half_b]

    got = place.core(low)
    grad_upper2, keep, send = run(
        "feed_back", feed_back, grad_of, at, low, got, weights2, slope2
    )
    chip, others = quad_sum(keep, send)
    units2 = run(
        "unit_grads",
        unit_grads,
        staged(unit_half),
        at, low21, got21, low, got, activ2, grad_upper2,
        after=[chip],
    )
    early = units2[0]
    units2 = send_staged(*units2)
    matrix1, bias1 = head_weights(0, [*heads, out_got], [early])
    qkv1, lse1, _ = run(
        "attention_again",
        attention_again,
        [((tokens, inner), BF), lse_of, ((tokens, width), BF)],
        at, pack, matrix1, bias1,
        after=[matrix1],
    )
    sums = [low, got]
    back, low = run(
        "norm_backward",
        norm_backward,
        back_of,
        at, sum21, back, chip, others, norm_gain[1, 0][None],
        after=[early, lse1],
    )
    got = place.core(low)
    grad_qkv2, keep, send = run(
        "attention_back",
        attention_back,
        inner_of,
        at, low, got, matrix2, qkv2, lse2, pack,
        after=[units2[1], units2[3]],
    )
    units2 = next_stage(units2, after=[send])
    chip, others = quad_sum(keep, send)
    heads2 = run(
        "head_grads",
        head_grads_later,
        head_parts,
        at, low12, got12, grad_qkv2, mixed2, low, got,
        after=[send],
    )
    early = heads2[0]
    heads2 = send_direct(heads2)
    sums = [low, got] + sums
    back, low = run(
        "norm_backward",
        norm_backward,
        back_of,
        at, sum12, back, chip, others, norm_gain[0, 1][None],
        after=[early, units2[1], units2[3]],
    )
    got = place.core(low)
    grad_upper1, keep, send = run(
        "feed_back", feed_back, grad_of, at, low, got, weights1, slope1
    )
    chip, others = quad_sum(keep, send)
    units1 = run(
        "unit_grads",
        unit_grads,
        staged(unit_half),
        at, low11, got11, low, got, activ1, grad_upper1,
        after=[send],
    )
    early = units1[0]
    units1 = send_staged(*units1)
    sums = [low, got] + sums
    back, low = run(
        "norm_backward",
        norm_backward,
        back_of,
        at, sum11, back, chip, others, norm_gain[0, 0][None],
        after=[early, *heads2[1:]],
    )
    got = place.core(low)
    sums = [low, got] + sums
    later = sum_chips(
        combine_both, (*units2, *heads2), sum(unit_half + head_half), after=[low]
    )
    grad_qkv1, keep, send = run(
        "attention_back",
        attention_back,
        inner_of,
        at, low, got, matrix1, qkv1, lse1, pack,
        after=[later],
    )
    spans = (unit_half, head_half)
    later_got = place.over(later)
    keep_a, over_v, keep_b, over_u = staged(head_half)
    u_a, u_b = (((rows, features), F32) for rows in unit_half)
    over_v, over_u = (
        ((send[0][0] + rows, features), BF) for send, rows in ((over_v, unit_half[1]), (over_u, unit_half[0]))
    )
    keep_a, keep_b, u_a, u_b, over_v, over_u = run(
        "head_grads",
        head_grads_first,
        [keep_a, keep_b, u_a, u_b, over_v, over_u],
        at, pack, grad_qkv1, mixed1, low, got, *sums, *units1,
        scratch=[pltpu.VMEM((8, EXTRA, features), BF), pltpu.SemaphoreType.DMA((8,))],
        hbm=range(6, 14),
        after=[send],
    )
    row_quarter = (quarter, features)
    mine, other = run(
        "tail_one",
        tail_one,
        [(row_quarter, F32), (row_quarter, BF)],
        at, keep, place.core(send), back,
        after=[over_v],
    )
    h_a, for_a, h_b, for_b, units1 = run(
        "combine_joint",
        combine_joint,
        [*one_of(head_half), ((sum(unit_half), features), BF)],
        at, keep_a, keep_b, u_a, u_b, place.chip(over_v, 1), place.chip(over_u, 2),
        after=[mine],
    )
    units_got = place.over(units1)
    rows, both = run(
        "tail_two",
        tail_two,
        [row_quarter_f, ((2, quarter, features), BF)],
        at, mine, place.side(other), final,
        after=[units1],
    )
    both = place.cross(both)
    final_out, input_grad = (
        jnp.where(place.native, own, got.astype(F32)) for own, got in zip((final, rows), both)
    )
    heads1 = sum_chips(
        combine_staged,
        (h_a, place.chip(for_a, 2), h_b, place.chip(for_b, 1)),
        sum(head_half),
        after=[rows],
    )
    later = sum_planes([(later, later_got, spans)], after=[units1])
    first = sum_planes(
        [(units1, units_got, spans[:1]), (heads1, place.over(heads1), spans[1:])],
        after=later,
    )

    def join(pieces, after):
        return run(
            "join_pieces",
            join_pieces,
            [((len(pieces),) + pieces[0].shape, BF)],
            at, *pieces,
            scratch=[sem],
            hbm=range(1, 5),
            hbm_out=(0,),
            after=after,
        )[0]

    pairs = (layers, 2, features)
    small = [(layers, units), (layers, 2, width), pairs, pairs, pairs]
    *grads, other = unpack(1, (0, 1, 2, 3), join(later, first[:1]), [])
    up, down, qkv, out, bup, bqv, bias, gain, shift = unpack(
        0, (0, 1, 2, 3), join(first, [other, both]), small, [other, jnp.zeros_like(other)], grads
    )
    return (
        final_out,
        input_grad,
        jnp.transpose(qkv.reshape(layers, 3, width, features), (0, 3, 1, 2)),
        bqv,
        out,
        bias,
        gain,
        shift,
        up,
        bup,
        down,
    )


def solution(mesh):
    columns = Mesh(mesh.devices.reshape(-1, 2, 2, 2, mesh.shape["tp"]), AXES)
    rows = P(AXES[:4], None)
    return jax.shard_map(
        on_device,
        mesh=columns,
        in_specs=(
            rows,
            rows,
            rows,
            rows,
            P(None, None, None, "tp"),
            P(None, None, "tp"),
            P(None, "tp", None),
            P(),
            P(),
            P(),
            P(None, None, "tp"),
            P(None, "tp"),
            P(None, "tp", None),
        ),
        out_specs=(
            P(AXES, None),
            P(AXES, None),
            P(None, None, None, "tp"),
            P(None, None, "tp"),
            P(None, "tp", None),
            P(),
            P(),
            P(),
            P(None, None, "tp"),
            P(None, "tp"),
            P(None, "tp", None),
        ),
        check_vma=False,
    )
```

```python
import functools

import jax
import jax.numpy as jnp
from jax import lax
from jax.experimental import pallas as pl
from jax.experimental.pallas import tpu as pltpu
from jax.sharding import Mesh
from jax.sharding import PartitionSpec as P

HEAD_DIM = 64
EPS = 1e-06
NEG = -1e30
EXTRA = 16
AXES = ("far", "u", "v", "c", "tp")
BF = jnp.bfloat16
F32 = jnp.float32
VMEM_BYTES = 24 << 20


class Place:
    def __init__(self):
        self.fars = lax.axis_size("far")
        self.core_no = lax.axis_index("c")
        self.z = lax.axis_index("tp")
        self.native = self.core_no == self.z // 2
        chip = lax.axis_index("u") * 2 + lax.axis_index("v")
        self.vector = jnp.stack(
            [chip, self.core_no, self.z, self.native.astype(jnp.int32)]
        ).astype(jnp.int32)

    def move(self, values, where):
        pairs = []
        for far in range(self.fars):
            for chip in range(4):
                for c in range(2):
                    for z in range(4):
                        to = where(chip, c, z)
                        if to is not None:
                            base = far * 4
                            source = ((base + chip) * 2 + c) * 4 + z
                            target = ((base + to[0]) * 2 + to[1]) * 4 + to[2]
                            pairs.append((source, target))
        return lax.ppermute(values, AXES, pairs)

    def core(self, values):
        return self.move(values, lambda i, c, z: (i, c ^ 1, z))

    def to_foreign(self, values):
        return self.move(values, lambda i, c, z: (i, c ^ 1, z) if c == z // 2 else None)

    def side(self, values):
        return self.move(values, lambda i, c, z: (i, c, z ^ 1))

    def cross(self, values):
        return self.move(values, lambda i, c, z: (i, c ^ 1, z ^ 2) if c != z // 2 else None)

    def over(self, values):
        return self.move(values, lambda i, c, z: (i, c, z ^ 2) if c != z // 2 else None)

    def chip(self, values, k, native=None):
        def where(i, c, z):
            if native is None or native == (c == z // 2):
                return (i ^ k, c, z)
            return None

        return self.move(values, where)

    def add_far(self, values):
        step = 1
        while step < self.fars:
            pairs = []
            for far in range(self.fars):
                pairs += [(far * 32 + i, (far ^ step) * 32 + i) for i in range(32)]
            got = lax.ppermute(values, AXES, pairs)
            values = (values.astype(F32) + got.astype(F32)).astype(values.dtype)
            step *= 2
        return values


class Layer:
    def __init__(self, whole, n):
        self.whole, self.n = whole, n


class Argument:
    def __init__(self, whole):
        self.whole = whole


def run(name, kernel, outs, *args, scratch=(), after=(), hbm=(), hbm_out=(), cost=0):
    n = len(args)

    def body(*refs):
        kernel(*refs[:n], *refs[n + len(after) :])

    anywhere = pl.BlockSpec(memory_space=pl.ANY)
    vmem = pl.BlockSpec(memory_space=pltpu.VMEM)
    in_specs, given = [pl.BlockSpec(memory_space=pltpu.SMEM)], [args[0]]
    for i in range(1, n):
        arg = args[i]
        if isinstance(arg, Layer):
            block = (None,) + arg.whole.shape[1:]
            zeros = (0,) * (arg.whole.ndim - 1)
            in_specs.append(pl.BlockSpec(block, lambda i, at=(arg.n,) + zeros: at))
            given.append(arg.whole)
        else:
            pinned = isinstance(arg, Argument)
            space = pltpu.HBM if pinned else pl.ANY if i in hbm else pltpu.VMEM
            in_specs.append(pl.BlockSpec(memory_space=space))
            given.append(arg.whole if pinned else arg)
    in_specs += [anywhere] * len(after)
    return pl.pallas_call(
        body,
        name=name,
        grid=(1,) if any(isinstance(arg, Layer) for arg in args) else (),
        out_shape=[jax.ShapeDtypeStruct(s, d) for s, d in outs],
        in_specs=in_specs,
        out_specs=[anywhere if i in hbm_out else vmem for i in range(len(outs))],
        scratch_shapes=list(scratch),
        cost_estimate=pl.CostEstimate(
            flops=cost * 10**9, bytes_accessed=0, transcendentals=0
        ),
        compiler_params=pltpu.CompilerParams(vmem_limit_bytes=VMEM_BYTES),
    )(*given, *after)


def dot_nn(a, b):
    return lax.dot_general(a, b, (((1,), (0,)), ((), ())), preferred_element_type=F32)


def dot_nt(a, b):
    return lax.dot_general(a, b, (((1,), (1,)), ((), ())), preferred_element_type=F32)


def dot_tn(a, b):
    return lax.dot_general(a, b, (((0,), (0,)), ((), ())), preferred_element_type=F32)


def thirds(value):
    hi = value.astype(BF).astype(F32)
    mid = (value - hi).astype(BF).astype(F32)
    return hi, mid, value - hi - mid


def extra_rows(rows, columns):
    padded = [
        jnp.concatenate([r, jnp.zeros((1, columns - r.shape[1]), F32)], axis=1)
        if r.shape[1] < columns
        else r
        for r in rows
    ]
    return jnp.concatenate(padded + [jnp.zeros((EXTRA - len(rows), columns), F32)], axis=0)


def multiple(index, size):
    return pl.ds(pl.multiple_of(index * size, size), size)


def bias_rows(place, bias, rows):
    rows[...] = extra_rows(thirds(bias[0:1]), rows.shape[1]).astype(BF)


def copy_all(pairs, sem):
    copies = [pltpu.make_async_copy(a, b, sem.at[i]) for i, (a, b) in enumerate(pairs)]
    for copy in copies:
        copy.start()
    for copy in copies:
        copy.wait()


def pack_units(place, up, down, bias, piece, tail, sem, n, whole):
    rows = up.shape[1] if whole else up.shape[1] // 4
    at = slice(0, rows) if whole else multiple(place[0], rows)
    tail[...] = extra_rows(thirds(bias[n : n + 1]), up.shape[2]).astype(BF)
    copy_all(
        [
            (up.at[n, at], piece.at[0:rows]),
            (down.at[n, at], piece.at[rows : 2 * rows]),
            (tail, piece.at[2 * rows :]),
        ],
        sem,
    )


def head_biases(bias):
    both = jnp.concatenate([bias[0:1], bias[1:2]], axis=1)
    return extra_rows(thirds(both), 4 * bias.shape[1]).astype(BF)


def pack_heads(place, qkv_w, out_w, bias, pack, tail, sem):
    chip = place[0]
    rows, fewer = out_w.shape[1], qkv_w.shape[1] // 4
    inner = qkv_w.shape[1] // rows
    for n in range(2):
        tail[n] = head_biases(bias[n])
    second = rows + EXTRA

    @pl.when(chip < inner)
    def _():
        copy_all([(qkv_w.at[1, multiple(chip, rows)], pack.at[0:rows])], sem)

    @pl.when(chip >= inner)
    def _():
        copy_all([(out_w.at[1], pack.at[0:rows])], sem)

    copy_all(
        [
            (qkv_w.at[0, multiple(chip, fewer)], pack.at[second : second + fewer]),
            (tail.at[1], pack.at[rows:second]),
            (tail.at[0], pack.at[second + fewer :]),
        ],
        sem,
    )


def pack_rows(place, hidden, grad, seg, mask, own, other):
    c = place[1]
    tokens, features = hidden.shape
    half = tokens // 2
    for ref, first in ((own, c), (other, 1 - c)):
        ids = []
        for i, h in enumerate((first, 1 - first)):
            at = multiple(h, half)
            ref[i * half : (i + 1) * half] = hidden[at]
            ids.append(seg[0:1, at])
        at = multiple(first, half)
        scale = seg_column(mask[0:1, at].astype(F32))
        ref[tokens : tokens + half] = (grad[at].astype(F32) * scale).astype(BF)
        ids = jnp.concatenate(ids, axis=1).astype(F32)
        ref[tokens + half :] = extra_rows([ids], features).astype(BF)


def choose_units(place, up, down, bias, *refs, n):
    *pieces, both, bias_out, tail, sem = refs
    chip, native = place[0], place[3]
    rows = up.shape[1] // len(pieces)

    @pl.when(native == 1)
    def _():
        copy_all([(up.at[n], both.at[0]), (down.at[n], both.at[1])], sem)
        bias_out[...] = bias[n : n + 1]

    @pl.when(native == 0)
    def _():
        pairs = [(pieces[0].at[2 * rows :], tail)]
        for k, ref in enumerate(pieces):
            to = slice(0, rows) if len(pieces) == 1 else multiple(chip ^ k, rows)
            for m in range(2):
                pairs.append((ref.at[m * rows : (m + 1) * rows], both.at[m, to]))
        copy_all(pairs, sem)
        parts = tail[...].astype(F32)
        bias_out[...] = parts[0:1] + parts[1:2] + parts[2:3]


def choose_heads(place, qkv_w, out_w, bias, *refs, n):
    *pieces, matrix, bias_out, tail, sem = refs
    chip, native = place[0], place[3]
    width, inner = out_w.shape[1], qkv_w.shape[1]

    @pl.when(native == 1)
    def _():
        copy_all([(qkv_w.at[n], matrix.at[0:inner]), (out_w.at[n], matrix.at[inner:])], sem)
        bias_out[...] = qkv_bias(bias[0:1], bias[1:2])

    @pl.when(native == 0)
    def _():
        start, rows = (0, width) if n else (width + EXTRA, inner // 4)
        pairs = [(pieces[0].at[start + rows : start + rows + EXTRA], tail)]
        for k in range(4):
            pairs.append(
                (pieces[k].at[start : start + rows], matrix.at[multiple(chip ^ k, rows)])
            )
        if n == 0:
            pairs.append((pieces[4], matrix.at[inner:]))
        copy_all(pairs, sem)
        parts = tail[...].astype(F32)
        row = parts[0:1] + parts[1:2] + parts[2:3]
        bias_out[...] = qkv_bias(row[:, :width], row[:, width : 2 * width])


def seg_column(seg_row):
    n = seg_row.shape[1]
    parts = [
        jnp.broadcast_to(seg_row[:, i : i + 128], (128, 128)).T[:, 0:1] for i in range(0, n, 128)
    ]
    return jnp.concatenate(parts, axis=0)


def attend(qkv, seg_row, mixed, lse, tile):
    tokens = qkv.shape[0]
    width = qkv.shape[1] // 3
    heads = width // HEAD_DIM
    column = seg_column(seg_row)
    for start in range(0, tokens, tile):
        same = column[start : start + tile] == seg_row
        outs, logs = [], []
        for head in range(heads):
            at = head * HEAD_DIM
            query = qkv[start : start + tile, at : at + HEAD_DIM] * HEAD_DIM ** (-0.5)
            keys = qkv[:, width + at : width + at + HEAD_DIM]
            values = qkv[:, 2 * width + at : 2 * width + at + HEAD_DIM]
            scores = jnp.where(same, dot_nt(query, keys), NEG)
            top = jnp.max(scores, axis=1, keepdims=True)
            expon = jnp.exp(scores - top)
            total = jnp.sum(expon, axis=1, keepdims=True)
            outs.append(dot_nn(expon.astype(BF), values) / total)
            logs.append(top + jnp.log(total))
        mixed[start : start + tile] = jnp.concatenate(outs, axis=1).astype(BF)
        logs.append(jnp.zeros((tile, lse.shape[1] - heads), F32))
        lse[start : start + tile] = jnp.concatenate(logs, axis=1)


def qkv_bias(bias_q, bias_v):
    return jnp.concatenate([bias_q, jnp.zeros_like(bias_q), bias_v], axis=1)


def attention_home(place, hidden, weight, bias, seg, mixed, ordered, qkv, lse):
    first = place[2] // 2
    tokens = hidden.shape[0]
    half = tokens // 2
    ids = []
    for i, h in enumerate((first, 1 - first)):
        at = multiple(h, half)
        ordered[i * half : (i + 1) * half] = hidden[at]
        ids.append(seg[0:1, at])
    seg_row = jnp.concatenate(ids, axis=1).astype(F32)
    qkv[...] = (dot_nt(ordered[...], weight[...]) + qkv_bias(bias[0:1], bias[1:2])).astype(BF)
    attend(qkv, seg_row, mixed, lse, half)


def put_half(part, keep, send):
    half = part.shape[0] // 2
    keep[...] = part[:half]
    send[...] = part[half:].astype(BF)


def project_first(place, mixed, mixed_got, out_w, out_got, kept, keep, send):
    native = place[3] == 1
    rows = jnp.where(native, out_w[...], out_got[...])
    values = jnp.where(native, mixed[...], mixed_got[...])
    kept[...] = values
    put_half(dot_nn(values, rows), keep, send)


def seg_of(pack, tokens):
    return pack[-EXTRA:].astype(F32)[0:1, :tokens]


def attention_again(place, pack, matrix, bias, qkv, lse, mixed):
    tokens, inner = qkv.shape
    qkv[...] = (dot_nt(pack[:tokens], matrix[:inner]) + bias[...]).astype(BF)
    attend(qkv, seg_of(pack, tokens), mixed, lse, tokens // 2)


def attention_column(place, own, got, matrix, bias, pack, qkv, mixed, lse, keep, send):
    tokens, inner = qkv.shape
    hidden = jnp.concatenate([own[...], got[...]], axis=0)
    qkv[...] = (dot_nt(hidden, matrix[:inner]) + bias[...]).astype(BF)
    attend(qkv, seg_of(pack, tokens), mixed, lse, tokens // 2)
    put_half(dot_nn(mixed[...], matrix[inner:]), keep, send)


def attend_back(qkv, lse, grad_mixed, seg_row, grad_qkv, tile):
    tokens = qkv.shape[0]
    width = qkv.shape[1] // 3
    heads = width // HEAD_DIM
    column = seg_column(seg_row)
    scale = HEAD_DIM ** (-0.5)
    grads = [[], [], []]
    for head in range(heads):
        at = head * HEAD_DIM
        keys = qkv[:, width + at : width + at + HEAD_DIM]
        values = qkv[:, 2 * width + at : 2 * width + at + HEAD_DIM]
        grad_keys = jnp.zeros((tokens, HEAD_DIM), F32)
        grad_values = jnp.zeros((tokens, HEAD_DIM), F32)
        grad_query = []
        for start in range(0, tokens, tile):
            rows = slice(start, start + tile)
            query = qkv[rows, at : at + HEAD_DIM] * scale
            grad_out = grad_mixed[rows, at : at + HEAD_DIM]
            scores = jnp.where(column[rows] == seg_row, dot_nt(query, keys), NEG)
            probs = jnp.exp(scores - lse[rows, head : head + 1])
            grad_probs = dot_nt(grad_out, values)
            inner = jnp.sum(probs * grad_probs, axis=1, keepdims=True)
            grad_scores = (probs * (grad_probs - inner)).astype(BF)
            grad_query.append(dot_nn(grad_scores, keys) * scale)
            grad_keys += dot_tn(grad_scores, query)
            grad_values += dot_tn(probs.astype(BF), grad_out)
        grads[0].append(jnp.concatenate(grad_query, axis=0))
        grads[1].append(grad_keys)
        grads[2].append(grad_values)
    grad_qkv[...] = jnp.concatenate(grads[0] + grads[1] + grads[2], axis=1).astype(BF)


def join_grads(own, got):
    return jnp.concatenate([own[:-EXTRA], got[:-EXTRA]], axis=0)


def attention_back(place, own, got, matrix, qkv, lse, pack, grad_qkv, keep, send):
    tokens, inner = qkv.shape
    grad_att = join_grads(own, got)
    grad_mixed = dot_nt(grad_att, matrix[inner:]).astype(BF)
    attend_back(qkv, lse, grad_mixed, seg_of(pack, tokens), grad_qkv, tokens)
    put_half(dot_nn(grad_qkv[...], matrix[:inner]), keep, send)


def part_rows(whole_a, whole_b, sums, sums_in_b):
    features = whole_a[0].shape[1]
    for p in range(4):
        parts = [whole_a[p], whole_b[p]]
        rows = extra_rows(sums if p == 0 else [], features)
        parts[sums_in_b] = jnp.concatenate([parts[sums_in_b], rows], axis=0)
        yield p, parts[0].astype(BF), parts[1].astype(BF)


def put_direct(place, whole_a, whole_b, sums, *refs):
    for p, a, b in part_rows(whole_a, whole_b, sums, 1):
        part = jnp.concatenate([a, b], axis=0)
        for k, ref in enumerate(refs):

            @pl.when(place[0] ^ p == k)
            def _(ref=ref):
                ref[...] = part


def put_staged(place, whole_a, whole_b, sums, sums_in_b, keep_a, send_a, keep_b, send_b):
    for p, a, b in part_rows(whole_a, whole_b, sums, sums_in_b):
        offset = place[0] ^ p
        over_u, over_v = offset // 2, offset % 2

        @pl.when(over_v == 0)
        def _():
            keep_a[over_u] = a

        @pl.when(over_v == 1)
        def _():
            send_a[multiple(over_u, a.shape[0])] = a

        @pl.when(over_u == 0)
        def _():
            keep_b[over_v] = b

        @pl.when(over_u == 1)
        def _():
            send_b[multiple(over_v, b.shape[0])] = b


def head_grads(hidden, grad_qkv, mixed, a_own, a_got, sums):
    grad_att = join_grads(a_own, a_got)
    whole = jnp.concatenate([dot_tn(grad_qkv[...], hidden), dot_tn(mixed[...], grad_att)], axis=0)
    bias = jnp.sum(grad_qkv[...].astype(F32), axis=0, keepdims=True)
    rows = whole.shape[0] // 4
    cut = rows // 2
    first = [whole[p * rows : p * rows + cut] for p in range(4)]
    second = [whole[p * rows + cut : (p + 1) * rows] for p in range(4)]
    return first, second, [bias] + sums


def head_grads_first(place, pack, grad_qkv, mixed, a_own, a_got, *refs):
    norms, (u_keep_a, u_got_a, u_keep_b, u_got_b) = refs[:8], refs[8:12]
    keep_a, keep_b, mine_a, mine_b, over_v, over_u, rows, sem = refs[12:]
    copy_all([(ref.at[ref.shape[0] - EXTRA :], rows.at[i]) for i, ref in enumerate(norms)], sem)
    total = []
    for i in range(4):
        both = rows[2 * i].astype(F32) + rows[2 * i + 1].astype(F32)
        total += [both[j : j + 1] for j in range(3)]
    hidden = pack[: grad_qkv.shape[0]]
    parts = head_grads(hidden, grad_qkv, mixed, a_own, a_got, total)
    put_staged(place, *parts, 1, keep_a, over_v, keep_b, over_u)
    mine_a[...], over_u[2 * keep_b.shape[1] :] = next_parts(u_keep_a, u_got_a)
    mine_b[...], over_v[2 * keep_a.shape[1] :] = next_parts(u_keep_b, u_got_b)


def head_grads_later(place, own, got, grad_qkv, mixed, a_own, a_got, *parts):
    hidden = jnp.concatenate([own[...], got[...]], axis=0)
    put_direct(place, *head_grads(hidden, grad_qkv, mixed, a_own, a_got, []), *parts)


def feed_forward(place, own, got, weights, bias, activ, slope, keep, send):
    hidden = jnp.concatenate([own[...], got[...]], axis=0)
    upper = dot_nn(hidden, weights[0]) + bias[...]
    cdf = 0.5 * (1.0 + lax.erf(upper * (0.5**0.5)))
    activ[...] = (upper * cdf).astype(BF)
    slope[...] = cdf + upper * jnp.exp(-0.5 * upper * upper) * 0.3989422804014327
    put_half(dot_nn(activ[...], weights[1]), keep, send)


def feed_back(place, own, got, weights, slope, grad_upper, keep, send):
    grad = join_grads(own, got)
    grad_upper[...] = (dot_nt(grad, weights[1]) * slope[...]).astype(BF)
    put_half(dot_nt(grad_upper[...], weights[0]), keep, send)


def unit_grads(place, x_own, x_got, g_own, g_got, activ, grad_upper, *parts):
    hidden = jnp.concatenate([x_own[...], x_got[...]], axis=0)
    grad = join_grads(g_own, g_got)
    up = dot_tn(hidden, grad_upper[...])
    down = dot_tn(activ[...], grad)
    bias = jnp.sum(grad_upper[...].astype(F32), axis=0, keepdims=True)
    rows = up.shape[0] // 4
    first = [up[p * rows : (p + 1) * rows] for p in range(4)]
    second = [down[p * rows : (p + 1) * rows] for p in range(4)]
    put_staged(place, first, second, [bias], 0, *parts)


def chip_sum(place, keep, got, chip, low):
    chip[...] = keep[...] + got[...].astype(F32)
    low[...] = chip[...].astype(BF)


def next_parts(keep, got):
    rows = keep.shape[1]
    mine = keep[0].astype(F32) + got[0:rows].astype(F32)
    return mine, (keep[1].astype(F32) + got[rows : 2 * rows].astype(F32)).astype(BF)


def combine_one(place, keep_a, got_a, keep_b, got_b, mine_a, for_a, mine_b, for_b):
    mine_a[...], for_a[...] = next_parts(keep_a, got_a)
    mine_b[...], for_b[...] = next_parts(keep_b, got_b)


def combine_joint(
    place, keep_a, keep_b, u_a, u_b, got_v, got_u, mine_a, for_a, mine_b, for_b, units
):
    mine_a[...], for_a[...] = next_parts(keep_a, got_v)
    mine_b[...], for_b[...] = next_parts(keep_b, got_u)
    rows = u_a.shape[0]
    units[:rows] = (u_a[...] + got_u[2 * keep_b.shape[1] :].astype(F32)).astype(BF)
    units[rows:] = (u_b[...] + got_v[2 * keep_a.shape[1] :].astype(F32)).astype(BF)


def combine_staged(place, mine_a, got_a, mine_b, got_b, total):
    rows = mine_a.shape[0]
    total[:rows] = (mine_a[...] + got_a[...].astype(F32)).astype(BF)
    total[rows:] = (mine_b[...] + got_b[...].astype(F32)).astype(BF)


def combine_both(place, mine_a, got_a, mine_b, got_b, own, got1, got2, got3, total):
    start = mine_a.shape[0] + mine_b.shape[0]
    combine_staged(place, mine_a, got_a, mine_b, got_b, total.at[0:start])
    terms = [ref[...].astype(F32) for ref in (own, got1, got2, got3)]
    total[start:] = ((terms[0] + terms[1]) + (terms[2] + terms[3])).astype(BF)


def combine_planes(place, *refs, spans):
    *parts, first, second = refs
    at = [0, 0]
    for i, parts_of in enumerate(spans):
        mine, got = parts[2 * i : 2 * i + 2]
        start = 0
        for halves in parts_of:
            for j, (out, rows) in enumerate(zip((first, second), halves)):
                value = mine[start : start + rows].astype(F32) + got[start : start + rows].astype(F32)
                out[at[j] : at[j] + rows] = value.astype(BF)
                start += rows
                at[j] += rows


def tail_one(place, keep, got, back, mine, other):
    s = place[2] % 2
    rows = mine.shape[0]
    at, away = multiple(s, rows), multiple(1 - s, rows)
    mine[...] = keep[at] + got[at].astype(F32) + back[at]
    other[...] = (keep[away] + got[away].astype(F32)).astype(BF)


def tail_two(place, mine, got, final, rows, both):
    rows[...] = mine[...] + got[...].astype(F32)
    both[0] = final[...].astype(BF)
    both[1] = rows[...].astype(BF)


def normalize(values):
    center = values - jnp.mean(values, axis=1, keepdims=True)
    spread = jnp.mean(center * center, axis=1, keepdims=True)
    inv = lax.rsqrt(spread + EPS)
    return center * inv, inv


def norm_forward(place, base, chip, got, bias, gain, shift, total, out, low):
    values = base[...].astype(F32) + (chip[...].astype(BF).astype(F32) + got[...].astype(F32) + bias[...])
    total[...] = values
    unit, _ = normalize(values)
    result = unit * gain[...] + shift[...]
    out[...] = result
    low[...] = result.astype(BF)


def back_through(values, gain, grad):
    unit, inv = normalize(values)
    scaled = grad * gain
    first = jnp.mean(scaled, axis=1, keepdims=True)
    second = jnp.mean(scaled * unit, axis=1, keepdims=True)
    back = inv * (scaled - first - unit * second)
    low = back.astype(BF)
    sums = [
        jnp.sum(low.astype(F32), axis=0, keepdims=True),
        jnp.sum(grad * unit, axis=0, keepdims=True),
        jnp.sum(grad, axis=0, keepdims=True),
    ]
    return back, jnp.concatenate([low, extra_rows(sums, low.shape[1]).astype(BF)], axis=0)


def norm_turn(place, base, chip, got, bias, gain, shift, pack, final, back, low):
    half = base.shape[0]
    quarter = half // 2
    values = base[...] + (chip[...].astype(BF).astype(F32) + got[...].astype(F32) + bias[...])
    unit, _ = normalize(values)
    back[...] = unit * gain[...] + shift[...]
    final[...] = back[multiple(place[2] % 2, quarter)]
    grad = pack[2 * half : 3 * half].astype(F32)
    back[...], low[...] = back_through(values, gain[...], grad)


def norm_backward(place, values, base, chip, got, gain, back, low):
    grad = base[...] + (chip[...].astype(BF).astype(F32) + got[...].astype(F32))
    back[...], low[...] = back_through(values[...], gain[...], grad)


def join_pieces(place, *refs):
    *pieces, mine, sem = refs
    copy_all([(ref, mine.at[k]) for k, ref in enumerate(pieces)], sem)


def unpack_parts(place, *refs, n, ks, smalls, last, unit_half):
    count = len(ks)
    (mine, got), refs = ([ref.at[i] for i in range(count)] for ref in refs[:2]), refs[2:]
    given, refs = refs[:smalls], refs[smalls:]
    up, down, qkv, out, *small, stage, sem = refs[-(7 + 4 * last) :]
    chip, native = place[0], place[3] == 1
    rows = stage.shape[2]
    cut = rows // 2
    copies, sums = [], jnp.zeros((2, EXTRA, stage.shape[3]), F32)
    for i, k in enumerate(ks):
        p = chip ^ k
        a = jnp.where(native, mine[i][...], got[i][...]).astype(F32)
        b = jnp.where(native, got[i][...], mine[i][...]).astype(F32)
        at = multiple(p, rows)
        stage[i, 0] = a[:rows]
        copies.append(pltpu.make_async_copy(stage.at[i, 0], up.at[n, at], sem.at[i, 0]))
        copies[-1].start()
        stage[i, 1] = b[:rows]
        copies.append(pltpu.make_async_copy(stage.at[i, 1], down.at[n, at], sem.at[i, 1]))
        copies[-1].start()
        stage[i, 2, :cut] = a[unit_half[0] :]
        stage[i, 2, cut:] = b[unit_half[1] : unit_half[1] + cut]

        @pl.when(p < 3)
        def _(i=i, at=at):
            pltpu.make_async_copy(stage.at[i, 2], qkv.at[n, at], sem.at[i, 2]).start()

        @pl.when(p == 3)
        def _(i=i):
            pltpu.make_async_copy(stage.at[i, 2], out.at[n], sem.at[i, 2]).start()

        found = jnp.stack([a[rows : unit_half[0]], b[unit_half[1] + cut :]])
        sums = sums + jnp.where(p == 0, found, 0.0)
    if last:
        other, first = given
        sums = sums + first[...]
        bup, bqv, *norms = small
        width = bqv.shape[2]
        for i, (u, h) in enumerate(((sums[0], sums[1]), (other[0], other[1]))):
            bup[i : i + 1] = u[0:1]
            bqv[i, 0:1] = h[0:1, 0:width]
            bqv[i, 1:2] = h[0:1, 2 * width : 3 * width]
            for j in range(2):
                for m, ref in enumerate(norms):
                    row = 1 + (2 * i + j) * 3 + m
                    ref[i, j : j + 1] = sums[1, row : row + 1]
    else:
        small[0][...] = sums
    for copy in copies:
        copy.wait()
    for i, k in enumerate(ks):
        pltpu.make_async_copy(stage.at[i, 2], out.at[n], sem.at[i, 2]).wait()


def on_device(
    hidden_in,
    out_grad,
    segment_ids,
    loss_mask,
    w_qkv,
    b_query_value,
    w_out,
    branch_bias,
    norm_gain,
    norm_shift,
    w_up,
    b_up,
    w_down,
):
    place = Place()
    at = place.vector
    layers, features = w_qkv.shape[:2]
    width = w_qkv.shape[-1]
    inner = 3 * width
    tokens = hidden_in.shape[0]
    half, quarter = tokens // 2, tokens // 4
    units = w_up.shape[-1]
    unit_rows, head_rows = features // 4, (inner + width) // 4
    w_qkv_t = jnp.transpose(w_qkv, (0, 2, 3, 1)).reshape(layers, inner, features)

    def gain_of(n, i):
        return branch_bias[n, i][None], norm_gain[n, i][None], norm_shift[n, i][None]

    half_f = ((half, features), F32)
    half_b = ((half, features), BF)
    half_e = ((half + EXTRA, features), BF)
    unit_piece = ((2 * unit_rows + EXTRA, features), BF)
    head_piece = ((head_rows + EXTRA, features), BF)
    row_quarter_f = ((quarter, features), F32)
    sem = pltpu.SemaphoreType.DMA((9,))
    tail = pltpu.VMEM((EXTRA, features), BF)

    def spread_chips(values):
        return [values] + [place.chip(values, k, native=False) for k in (1, 2, 3)]

    def unit_weights(n, pieces, after=()):
        return run(
            "choose_units",
            functools.partial(choose_units, n=n),
            [((2, units, features), BF), ((1, units), F32)],
            at, Argument(w_up), Argument(w_down), b_up, *pieces,
            scratch=[tail, sem],
            hbm=(1, 2, *range(4, 4 + len(pieces))),
            hbm_out=(0,),
            after=after,
        )

    def unit_pack(n, whole, after=()):
        rows = 2 * (units if whole else unit_rows) + EXTRA
        return run(
            "pack_units",
            functools.partial(pack_units, n=n, whole=whole),
            [((rows, features), BF)],
            at, Argument(w_up), Argument(w_down), b_up,
            scratch=[tail, sem],
            hbm=(1, 2),
            hbm_out=(0,),
            after=after,
        )[0]

    def head_weights(n, pieces, after=()):
        return run(
            "choose_heads",
            functools.partial(choose_heads, n=n),
            [((inner + width, features), BF), ((1, inner), F32)],
            at, Argument(w_qkv_t), Argument(w_out), Layer(b_query_value, n), *pieces,
            scratch=[tail, sem],
            hbm=(1, 2, *range(4, 4 + len(pieces))),
            hbm_out=(0,),
            after=after,
        )

    def quad_sum(keep, send, after=()):
        chip, low = run(
            "chip_sum", chip_sum, [half_f, half_b], at, keep, place.core(send), after=after
        )
        return chip, place.side(low)

    (tail1,) = run("bias_rows", bias_rows, [((EXTRA, features), BF)], at, b_up)
    start = at[0] * unit_rows
    units1 = jnp.concatenate(
        [lax.dynamic_slice(w, (0, start, 0), (1, unit_rows, features))[0] for w in (w_up, w_down)]
        + [tail1]
    )
    early = units1
    out_got = place.cross(w_out[0])
    units1 = place.cross(units1)
    row_pack = ((tokens + half + EXTRA, features), BF)
    pack_own, pack_other = run(
        "pack_rows",
        pack_rows,
        [row_pack, row_pack],
        at, hidden_in, out_grad, segment_ids, loss_mask,
        after=[early],
    )
    (mixed_home,) = run(
        "attention_home",
        attention_home,
        [((tokens, width), BF)],
        at, hidden_in, Layer(w_qkv_t, 0), Layer(b_query_value, 0), segment_ids,
        scratch=[
            pltpu.VMEM((tokens, features), BF),
            pltpu.VMEM((tokens, inner), BF),
            pltpu.VMEM((tokens, 128), F32),
        ],
        after=[pack_own],
        cost=10,
    )
    mixed_got = place.cross(mixed_home)
    pack = jnp.where(place.native, pack_own, place.to_foreign(pack_other))

    head_pack_rows = width + inner // 4 + 2 * EXTRA
    (heads,) = run(
        "pack_heads",
        pack_heads,
        [((head_pack_rows, features), BF)],
        at, Argument(w_qkv_t), Argument(w_out), b_query_value,
        scratch=[pltpu.VMEM((2, EXTRA, features), BF), sem],
        hbm=(1, 2),
        hbm_out=(0,),
        after=[mixed_home, pack],
    )
    heads = place.cross(heads)

    mixed1, keep, send = run(
        "project_first",
        project_first,
        [((tokens, width), BF), half_f, half_b],
        at, mixed_home, mixed_got, Layer(w_out, 0), out_got,
    )
    chip, others = quad_sum(keep, send)
    sum11, norm11, low11 = run(
        "norm_forward",
        norm_forward,
        [half_f, half_f, half_b],
        at, pack[:half], chip, others, *gain_of(0, 0),
        after=[heads],
    )
    got11 = place.core(low11)
    weights1, b_up1 = unit_weights(0, spread_chips(units1), after=[low11])
    ffn_outs = [((tokens, units), BF), ((tokens, units), F32), half_f, half_b]
    activ1, slope1, keep, send = run(
        "feed_forward",
        feed_forward,
        ffn_outs,
        at, low11, got11, weights1, b_up1,
    )
    matrix_of = ((inner + width, features), BF)
    chip, others = quad_sum(keep, send)
    units2 = place.cross(unit_pack(1, False, [chip]))
    sum12, norm12, low12 = run(
        "norm_forward",
        norm_forward,
        [half_f, half_f, half_b],
        at, norm11, chip, others, *gain_of(0, 1),
    )
    got12 = place.core(low12)
    heads = spread_chips(heads)
    matrix2, bias2 = head_weights(1, heads, [low12])
    lse_of = ((tokens, 128), F32)
    qkv2, mixed2, lse2, keep, send = run(
        "attention_column",
        attention_column,
        [((tokens, inner), BF), ((tokens, width), BF), lse_of, half_f, half_b],
        at, low12, got12, matrix2, bias2, pack,
        after=[units2],
    )
    chip, others = quad_sum(keep, send)
    weights2, b_up2 = unit_weights(1, spread_chips(units2))
    sum21, norm21, low21 = run(
        "norm_forward",
        norm_forward,
        [half_f, half_f, half_b],
        at, low12, chip, others, *gain_of(1, 0),
        after=[weights2],
    )
    got21 = place.core(low21)
    activ2, slope2, keep, send = run(
        "feed_forward", feed_forward, ffn_outs, at, low21, got21, weights2, b_up2
    )
    matrix1, bias1 = head_weights(0, [*heads, out_got], [low21])
    qkv1, lse1, _ = run(
        "attention_again",
        attention_again,
        [((tokens, inner), BF), lse_of, ((tokens, width), BF)],
        at, pack, matrix1, bias1,
        after=[send],
    )
    chip, others = quad_sum(keep, send)
    final, back, low = run(
        "norm_turn",
        norm_turn,
        [row_quarter_f, half_f, half_e],
        at, norm21, chip, others, *gain_of(1, 1), pack,
        after=[lse1],
    )

    shapes = [
        (layers, features, units),
        (layers, units, features),
        (layers, inner, features),
        (layers, width, features),
    ]

    def unpack(n, ks, joined, smalls, small=(), earlier=(), after=()):
        sums = [(2, EXTRA, features)]
        given = [joined, place.core(joined), *small]
        vmem = pl.BlockSpec(memory_space=pltpu.VMEM)
        anywhere = pl.BlockSpec(memory_space=pl.ANY)
        return pl.pallas_call(
            functools.partial(
                unpack_parts,
                n=n,
                ks=ks,
                smalls=len(small),
                last=len(smalls) > 0,
                unit_half=unit_half,
            ),
            name="unpack_parts",
            out_shape=[jax.ShapeDtypeStruct(s, F32) for s in shapes + (smalls or sums)],
            in_specs=[pl.BlockSpec(memory_space=pltpu.SMEM)]
            + [vmem] * len(given)
            + [anywhere] * (len(after) + len(earlier)),
            out_specs=[anywhere] * 4 + [vmem] * len(smalls or sums),
            input_output_aliases={
                1 + len(given) + len(after) + i: i for i in range(len(earlier))
            },
            scratch_shapes=[
                pltpu.VMEM((len(ks), 3, unit_rows, features), F32),
                pltpu.SemaphoreType.DMA((len(ks), 3)),
            ],
            cost_estimate=pl.CostEstimate(
                flops=0 if smalls else 4 * 10**10, bytes_accessed=0, transcendentals=0
            ),
            compiler_params=pltpu.CompilerParams(vmem_limit_bytes=VMEM_BYTES),
        )(at, *given, *after, *earlier)

    unit_half = (unit_rows + EXTRA, unit_rows)
    head_half = (head_rows // 2, head_rows // 2 + EXTRA)
    def staged(halves):
        return [
            (shape, BF)
            for rows in halves
            for shape in ((2, rows, features), (2 * rows, features))
        ]

    head_parts = [((sum(head_half), features), BF)] * 4

    def send_direct(parts):
        return [parts[0]] + [place.chip(parts[k], k) for k in (1, 2, 3)]

    def send_staged(keep_a, send_a, keep_b, send_b):
        return keep_a, place.chip(send_a, 1), keep_b, place.chip(send_b, 2)

    def one_of(halves):
        return [((rows, features), kind) for rows in halves for kind in (F32, BF)]

    def next_stage(parts, after=()):
        mine_a, for_a, mine_b, for_b = run(
            "combine_one", combine_one, one_of(unit_half), at, *parts, after=after
        )
        return mine_a, place.chip(for_a, 2), mine_b, place.chip(for_b, 1)

    def sum_chips(kernel, parts, rows, after=()):
        return run(
            kernel.__name__, kernel, [((rows, features), BF)], at, *parts, after=after
        )[0]

    def sum_planes(groups, after=()):
        spans = [group[2] for group in groups]
        rows = sum(halves[0] for parts in spans for halves in parts)
        first, second = run(
            "combine_planes",
            functools.partial(combine_planes, spans=spans),
            [((rows, features), BF)] * 2,
            at, *[part for group in groups for part in group[:2]],
            after=after,
        )
        first, second = place.add_far(first), place.add_far(second)
        piece = jnp.where(place.native, first, place.core(second))
        return [piece] + [place.chip(piece, k) for k in (1, 2, 3)]

    grad_of = [((tokens, units), BF), half_f, half_b]
    back_of = [half_f, half_e]
    inner_of = [((tokens, inner), BF), half_f, half_b]

    got = place.core(low)
    grad_upper2, keep, send = run(
        "feed_back", feed_back, grad_of, at, low, got, weights2, slope2
    )
    chip, others = quad_sum(keep, send)
    units2 = run(
        "unit_grads",
        unit_grads,
        staged(unit_half),
        at, low21, got21, low, got, activ2, grad_upper2,
        after=[chip],
    )
    early = units2[0]
    units2 = send_staged(*units2)
    sums = [low, got]
    back, low = run(
        "norm_backward",
        norm_backward,
        back_of,
        at, sum21, back, chip, others, norm_gain[1, 0][None],
        after=[early],
    )
    got = place.core(low)
    grad_qkv2, keep, send = run(
        "attention_back",
        attention_back,
        inner_of,
        at, low, got, matrix2, qkv2, lse2, pack,
        after=[units2[1], units2[3]],
    )
    units2 = next_stage(units2, after=[send])
    chip, others = quad_sum(keep, send)
    heads2 = run(
        "head_grads",
        head_grads_later,
        head_parts,
        at, low12, got12, grad_qkv2, mixed2, low, got,
        after=[send],
    )
    early = heads2[0]
    heads2 = send_direct(heads2)
    sums = [low, got] + sums
    back, low = run(
        "norm_backward",
        norm_backward,
        back_of,
        at, sum12, back, chip, others, norm_gain[0, 1][None],
        after=[early, units2[1], units2[3]],
    )
    got = place.core(low)
    grad_upper1, keep, send = run(
        "feed_back", feed_back, grad_of, at, low, got, weights1, slope1
    )
    chip, others = quad_sum(keep, send)
    units1 = run(
        "unit_grads",
        unit_grads,
        staged(unit_half),
        at, low11, got11, low, got, activ1, grad_upper1,
        after=[send],
    )
    early = units1[0]
    units1 = send_staged(*units1)
    sums = [low, got] + sums
    back, low = run(
        "norm_backward",
        norm_backward,
        back_of,
        at, sum11, back, chip, others, norm_gain[0, 0][None],
        after=[early, *heads2[1:]],
    )
    got = place.core(low)
    sums = [low, got] + sums
    later = sum_chips(
        combine_both, (*units2, *heads2), sum(unit_half + head_half), after=[low]
    )
    grad_qkv1, keep, send = run(
        "attention_back",
        attention_back,
        inner_of,
        at, low, got, matrix1, qkv1, lse1, pack,
        after=[later],
    )
    spans = (unit_half, head_half)
    later_got = place.over(later)
    keep_a, over_v, keep_b, over_u = staged(head_half)
    u_a, u_b = (((rows, features), F32) for rows in unit_half)
    over_v, over_u = (
        ((send[0][0] + rows, features), BF) for send, rows in ((over_v, unit_half[1]), (over_u, unit_half[0]))
    )
    keep_a, keep_b, u_a, u_b, over_v, over_u = run(
        "head_grads",
        head_grads_first,
        [keep_a, keep_b, u_a, u_b, over_v, over_u],
        at, pack, grad_qkv1, mixed1, low, got, *sums, *units1,
        scratch=[pltpu.VMEM((8, EXTRA, features), BF), pltpu.SemaphoreType.DMA((8,))],
        hbm=range(6, 14),
        after=[send],
    )
    row_quarter = (quarter, features)
    mine, other = run(
        "tail_one",
        tail_one,
        [(row_quarter, F32), (row_quarter, BF)],
        at, keep, place.core(send), back,
    )
    h_a, for_a, h_b, for_b, units1 = run(
        "combine_joint",
        combine_joint,
        [*one_of(head_half), ((sum(unit_half), features), BF)],
        at, keep_a, keep_b, u_a, u_b, place.chip(over_v, 1), place.chip(over_u, 2),
        after=[mine],
    )
    units_got = place.over(units1)
    rows, both = run(
        "tail_two",
        tail_two,
        [row_quarter_f, ((2, quarter, features), BF)],
        at, mine, place.side(other), final,
        after=[units1],
    )
    both = place.cross(both)
    final_out, input_grad = (
        jnp.where(place.native, own, got.astype(F32)) for own, got in zip((final, rows), both)
    )
    heads1 = sum_chips(
        combine_staged,
        (h_a, place.chip(for_a, 2), h_b, place.chip(for_b, 1)),
        sum(head_half),
        after=[rows],
    )
    later = sum_planes([(later, later_got, spans)], after=[units1])
    first = sum_planes(
        [(units1, units_got, spans[:1]), (heads1, place.over(heads1), spans[1:])],
        after=later,
    )

    def join(pieces, after):
        return run(
            "join_pieces",
            join_pieces,
            [((len(pieces),) + pieces[0].shape, BF)],
            at, *pieces,
            scratch=[sem],
            hbm=range(1, 5),
            hbm_out=(0,),
            after=after,
        )[0]

    pairs = (layers, 2, features)
    small = [(layers, units), (layers, 2, width), pairs, pairs, pairs]
    *grads, other = unpack(1, (0, 1, 2, 3), join(later, first[:1]), [])
    up, down, qkv, out, bup, bqv, bias, gain, shift = unpack(
        0, (0, 1, 2, 3), join(first, [other, both]), small, [other, jnp.zeros_like(other)], grads
    )
    return (
        final_out,
        input_grad,
        jnp.transpose(qkv.reshape(layers, 3, width, features), (0, 3, 1, 2)),
        bqv,
        out,
        bias,
        gain,
        shift,
        up,
        bup,
        down,
    )


def solution(mesh):
    columns = Mesh(mesh.devices.reshape(-1, 2, 2, 2, mesh.shape["tp"]), AXES)
    rows = P(AXES[:4], None)
    return jax.shard_map(
        on_device,
        mesh=columns,
        in_specs=(
            rows,
            rows,
            rows,
            rows,
            P(None, None, None, "tp"),
            P(None, None, "tp"),
            P(None, "tp", None),
            P(),
            P(),
            P(),
            P(None, None, "tp"),
            P(None, "tp"),
            P(None, "tp", None),
        ),
        out_specs=(
            P(AXES, None),
            P(AXES, None),
            P(None, None, None, "tp"),
            P(None, None, "tp"),
            P(None, "tp", None),
            P(),
            P(),
            P(),
            P(None, None, "tp"),
            P(None, "tp"),
            P(None, "tp", None),
        ),
        check_vma=False,
    )
```
